32 devices in a mesh: dp: 8 (over z, core), ctx: 4 (over y, x).
Axes of the slice: x: 2, y: 2, z: 4, core: 2. Of those that a mesh axis runs over, the one named last changes fastest.
Arguments:
- proj_read: bfloat16 [4096, 2048], P(('dp', 'ctx')), may hold values from -6 to 6
- norm_gain: float32 [512], replicated, may hold values from 0.1 to 1.9
- owner_of: int32 [16], replicated, may hold values from 0 to 7, as said below
- user_of: int32 [4096], P(('dp', 'ctx')), may hold values from -1 to 15, as said below
- grad_output: bfloat16 [4096, 512], P(('dp', 'ctx')), may hold values from -6 to 6
Outputs:
- layer_out: bfloat16 [4096, 512], P(('dp', 'ctx'))
- grad_read: bfloat16 [4096, 2048], P(('dp', 'ctx'))
The draws below stay inside these ranges and needn't reach their ends.
Inputs may be any that keep to these rules, and one draw needn't show every extreme that they name: `owner_of`: every owner index names exactly 2 users. `user_of`: -1 marks an empty row; at most 16 rows of one reader device hold users of one owner.
All inputs are finite; a program needn't handle non-finite values.
Results may differ from the reference program's by a relative error of at most 0.0085.
Values may be sent and summed in bfloat16 or wider, within the bound.
No kernel may reach another device: no remote copies, remote signals or barrier semaphores. Data moves between devices by JAX's collectives and lax.ppermute only.
A program may use at most 64 MiB of HBM per device.

```python
import jax
import jax.numpy as jnp
from jax import lax

HEADS = 4
HD = 128
HW = 512
ROWS_DEV = 128
UO = 2
PAIR = 16
NS = 512
EVENTS = 4096
N_DP = 8
N_CTX = 4


def user_table(key):
    return jax.random.permutation(jax.random.fold_in(key, 11), UO * N_DP)


def draw_owner_of(key, part):
    order = user_table(key)
    return (order // UO).astype(jnp.int32)


def draw_user_of(key, part):
    per_pair = ROWS_DEV // N_DP
    order = user_table(key)
    members = jnp.argsort(order).astype(jnp.int32)
    hot_owner = jax.random.randint(jax.random.fold_in(key, 21), (N_CTX,), 0, N_DP)
    counts_drawn = jax.random.randint(jax.random.fold_in(key, 22), (N_DP, N_CTX, N_DP), per_pair // 2, per_pair + 1)
    dest_range = jnp.arange(N_DP, dtype=jnp.int32).reshape(1, 1, N_DP)
    counts_drawn = jnp.where(dest_range == hot_owner.reshape(1, N_CTX, 1), per_pair, counts_drawn)
    bounds = jnp.cumsum(counts_drawn, axis=2)
    slot_ids = jnp.arange(ROWS_DEV, dtype=jnp.int32).reshape(1, 1, ROWS_DEV, 1)
    owner_pick = jnp.sum((slot_ids >= bounds[:, :, None, :]).astype(jnp.int32), axis=3)
    is_live = owner_pick < N_DP
    member_pick = jax.random.randint(jax.random.fold_in(key, 23), (N_DP, N_CTX, ROWS_DEV), 0, UO)
    chosen = members[jnp.minimum(owner_pick, N_DP - 1) * UO + member_pick]
    chosen = jnp.where(is_live, chosen, -1)
    row_scores = jax.random.randint(jax.random.fold_in(key, 24), (N_DP, N_CTX, ROWS_DEV), 0, 1 << 20) * ROWS_DEV + jnp.arange(ROWS_DEV, dtype=jnp.int32)
    row_order = jnp.argsort(row_scores, axis=2)
    chosen = jnp.take_along_axis(chosen, row_order, axis=2)
    return chosen.reshape(ROWS_DEV * N_DP * N_CTX).astype(jnp.int32)


def levels(own_key, extent, cuts, least, largest):
    gain, own = 1.0, jax.random.fold_in(own_key, 6)
    for dim, blocks in cuts:
        draws = jnp.exp(jax.random.uniform(jax.random.fold_in(own, dim), (blocks,), jnp.float32, least / len(cuts), largest / len(cuts)))
        gain = gain * jnp.repeat(draws, extent[dim] // blocks).reshape([-1 if axis == dim else 1 for axis in range(len(extent))])
    return gain


def gaussian(key, dims, scale, bound, shards=(), held_as=jnp.bfloat16):
    factor_of = levels(key, dims, shards, -0.22, 0.18) if shards else 1.0
    values = jax.random.normal(key, dims, jnp.float32) * scale * factor_of
    return jnp.minimum(jnp.maximum(values, -bound), bound).astype(held_as)


def setup_inputs(seed: int = 0) -> dict:
    splits = jax.random.split(jax.random.key(seed), 6)
    proj_read = gaussian(splits[0], (EVENTS, 4 * HW), 1.0, 6.0, ((0, 32),))
    norm_gain = jnp.clip(1.0 + 0.18 * jax.random.normal(splits[1], (HW,), jnp.float32), 0.1, 1.9)
    owner_of = draw_owner_of(jax.random.fold_in(splits[5], 71), 0)
    user_of = draw_user_of(jax.random.fold_in(splits[5], 71), 0)
    grad_output = gaussian(splits[4], (EVENTS, HW), 1.0, 6.0, ((0, 32),))
    return {"proj_read": proj_read, "norm_gain": norm_gain, "owner_of": owner_of, "user_of": user_of, "grad_output": grad_output}


epsilon = 1e-05

def silu_slope(scores):
    sigmoid_part = jax.nn.sigmoid(scores)
    return sigmoid_part * (1.0 + scores * (1.0 - sigmoid_part))

def owner_group(group_rows, group_users, grad_rows, norm_gain):
    feature_width = HEADS * HD
    score_scale = HD ** (-0.5)
    positions = jnp.arange(NS, dtype=jnp.int32)
    visible = (group_users[:, None] == group_users[None, :]) & (group_users[:, None] >= 0) & (positions[None, :] <= positions[:, None])

    def split_heads(block_rows):
        return block_rows.reshape(NS, HEADS, HD).transpose(1, 0, 2)

    def merge_heads(head_rows):
        return head_rows.transpose(1, 0, 2).reshape(NS, feature_width)
    unit_rows = group_rows[:, :feature_width].astype(jnp.float32)
    queries = split_heads(group_rows[:, feature_width:2 * feature_width])
    key_heads = split_heads(group_rows[:, 2 * feature_width:3 * feature_width])
    value_heads = split_heads(group_rows[:, 3 * feature_width:])

    def head_forward(head_inputs):
        query_head, key_head, value_head = head_inputs
        scores = jnp.dot(query_head, key_head.T, preferred_element_type=jnp.float32) * score_scale
        weights = jnp.where(visible, jax.nn.silu(scores), 0.0).astype(jnp.bfloat16)
        return jnp.dot(weights, value_head, preferred_element_type=jnp.float32)
    attended = merge_heads(lax.map(head_forward, (queries, key_heads, value_heads)))
    mean_out = lax.optimization_barrier(jnp.mean(attended, axis=1, keepdims=True))
    centered = attended - mean_out
    inv_std = lax.rsqrt(lax.optimization_barrier(jnp.mean(centered * centered, axis=1, keepdims=True)) + epsilon)
    normed = centered * inv_std
    layer_out = (normed * norm_gain * unit_rows).astype(jnp.bfloat16)
    grad_float = grad_rows.astype(jnp.float32)
    unit_grads = (grad_float * norm_gain * normed).astype(jnp.bfloat16)
    grad_normed = grad_float * norm_gain * unit_rows
    mean_grad = lax.optimization_barrier(jnp.mean(grad_normed, axis=1, keepdims=True))
    mean_cross = lax.optimization_barrier(jnp.mean(grad_normed * normed, axis=1, keepdims=True))
    out_grads = (inv_std * (grad_normed - mean_grad - normed * mean_cross)).astype(jnp.bfloat16)

    def head_backward(head_inputs):
        query_head, key_head, value_head, grad_head = head_inputs
        scores = jnp.dot(query_head, key_head.T, preferred_element_type=jnp.float32) * score_scale
        weights = jnp.where(visible, jax.nn.silu(scores), 0.0).astype(jnp.bfloat16)
        value_grad = jnp.dot(weights.T, grad_head, preferred_element_type=jnp.float32)
        weight_grads = jnp.dot(grad_head, value_head.T, preferred_element_type=jnp.float32)
        score_grads = jnp.where(visible, weight_grads * silu_slope(scores) * score_scale, 0.0).astype(jnp.bfloat16)
        key_grad = jnp.dot(score_grads.T, query_head, preferred_element_type=jnp.float32)
        window_sums = jnp.einsum('iwj,wjd->iwd', score_grads.astype(jnp.float32).reshape(NS, N_CTX, ROWS_DEV), key_head.astype(jnp.float32).reshape(N_CTX, ROWS_DEV, HD))
        window_parts = lax.optimization_barrier(window_sums.astype(jnp.bfloat16))
        query_grad = lax.optimization_barrier(jnp.sum(window_parts.astype(jnp.float32), axis=1))
        return (query_grad, key_grad, value_grad)
    query_grads, key_grads, value_grads = lax.map(head_backward, (queries, key_heads, value_heads, split_heads(out_grads)))
    grads_owned = jnp.concatenate([unit_grads, merge_heads(query_grads).astype(jnp.bfloat16), merge_heads(key_grads).astype(jnp.bfloat16), merge_heads(value_grads).astype(jnp.bfloat16)], axis=1)
    return (layer_out, grads_owned)

def reference(proj_read, norm_gain, owner_of, user_of, grad_output):
    feature_width = HEADS * HD
    reader_users = user_of.reshape(N_DP, N_CTX, ROWS_DEV)
    is_live = reader_users >= 0
    owners = jnp.where(is_live, owner_of[jnp.maximum(reader_users, 0)], -1).astype(jnp.int32)
    owner_hits = (owners[..., None] == jnp.arange(N_DP, dtype=jnp.int32)).astype(jnp.int32)
    ranks = lax.optimization_barrier(jnp.sum((jnp.cumsum(owner_hits, axis=2) - 1) * owner_hits, axis=3)).astype(jnp.int32)
    reader_index = jnp.arange(N_DP, dtype=jnp.int32).reshape(N_DP, 1, 1)
    window_index = jnp.arange(N_CTX, dtype=jnp.int32).reshape(1, N_CTX, 1)
    target = (owners * N_CTX + window_index) * ROWS_DEV + reader_index * PAIR + ranks
    target = jnp.where(is_live, target, EVENTS).reshape(EVENTS).astype(jnp.int32)
    owned = jnp.zeros((EVENTS, 4 * feature_width), jnp.bfloat16).at[target].set(proj_read, mode='drop')
    owned_users = jnp.full((EVENTS,), -1, jnp.int32).at[target].set(user_of, mode='drop')
    layer_out, grads_owned = lax.map(lambda group_data: owner_group(group_data[0], group_data[1], group_data[2], norm_gain), (owned.reshape(N_DP, NS, 4 * feature_width), owned_users.reshape(N_DP, NS), grad_output.reshape(N_DP, NS, feature_width)))
    layer_out = layer_out.reshape(EVENTS, feature_width)
    grads_owned = grads_owned.reshape(EVENTS, 4 * feature_width)
    picked = grads_owned[jnp.minimum(target, EVENTS - 1)]
    grad_read = jnp.where(is_live.reshape(EVENTS, 1), picked, jnp.zeros((), jnp.bfloat16)).astype(jnp.bfloat16)
    return (layer_out, grad_read)
```

```python
import functools

import jax
import jax.numpy as jnp
from jax import lax
from jax.experimental import pallas as pl
from jax.experimental.pallas import tpu as pltpu
from jax.sharding import PartitionSpec as P

HEADS = 4
HD = 128


epsilon = 1e-05


def block_length(total_rows, shard_rows):
    shard_total = total_rows // shard_rows
    best_factor = 1
    for factor in range(1, shard_total + 1):
        if shard_total % factor == 0 and factor * shard_rows <= 1024:
            best_factor = factor
    return best_factor * shard_rows


def silu_slope(scores):
    sigmoid_part = jax.nn.sigmoid(scores)
    return sigmoid_part * (1.0 + scores * (1.0 - sigmoid_part))


def visible_pairs(query_users, query_places, key_users, key_places):
    same_user = (query_users[:, None] == key_users[None, :]) & (query_users[:, None] >= 0)
    return same_user & (key_places[None, :] <= query_places[:, None])


def run_blocks(carry_now, shard_piece, block_rows, step_fn):
    total_rows = shard_piece[0].shape[0]

    def one_block(block_index, carry_here):
        offset = block_index * block_rows
        block_part = tuple(
            (
                lax.dynamic_slice_in_dim(array_item, offset, block_rows, 0)
                for array_item in shard_piece
            )
        )
        return step_fn(carry_here, block_part, offset)

    return lax.fori_loop(0, total_rows // block_rows, one_block, carry_now)


def windowed(proj_read, norm_gain, owner_of, user_of, grad_output):
    slot_rows = proj_read.shape[0]
    reader_peers = lax.axis_size("dp")
    per_pair = slot_rows // reader_peers
    feature_width = HEADS * HD
    score_scale = HD ** (-0.5)
    group_rows = slot_rows * lax.axis_size("ctx")
    user_range = jnp.arange(owner_of.shape[0], dtype=jnp.int32)
    owners = jnp.sum(
        jnp.where(user_of[:, None] == user_range[None, :], owner_of[None, :], 0), axis=1
    )
    is_live = user_of >= 0
    owner_hits = (owners[:, None] == jnp.arange(reader_peers, dtype=jnp.int32)[None, :]) & is_live[
        :, None
    ]
    running = jnp.cumsum(owner_hits.astype(jnp.int32), axis=0) - 1
    ranks_mine = jnp.sum(jnp.where(owner_hits, running, 0), axis=1)
    send_slot = jnp.where(is_live, owners * per_pair + ranks_mine, -1)
    slot_range = jnp.arange(slot_rows, dtype=jnp.int32)
    slot_match = send_slot[None, :] == slot_range[:, None]
    filled = jnp.any(slot_match, axis=1)
    source_row = jnp.sum(jnp.where(slot_match, slot_range[None, :], 0), axis=1)
    outgoing = jnp.where(
        filled[:, None], jnp.take(proj_read, source_row, axis=0), jnp.zeros((), jnp.bfloat16)
    )
    outgoing_users = jnp.where(filled, jnp.take(user_of, source_row), -1)
    arrived, arrived_users = (
        lax.all_to_all(outgoing, "dp", split_axis=0, concat_axis=0, tiled=True),
        lax.all_to_all(outgoing_users, "dp", split_axis=0, concat_axis=0, tiled=True),
    )
    own_start = lax.axis_index("ctx") * slot_rows
    own_places = own_start + slot_range
    unit_rows = arrived[:, :feature_width]
    queries = arrived[:, feature_width : 2 * feature_width]
    key_values = arrived[:, 2 * feature_width :]
    query_heads = queries.reshape(slot_rows, HEADS, HD)
    key_heads = key_values[:, :feature_width].reshape(slot_rows, HEADS, HD)
    value_heads = key_values[:, feature_width:].reshape(slot_rows, HEADS, HD)

    def forward_step(total_out, block_part, first_row):
        block_kv, block_users = block_part
        block_size = block_kv.shape[0]
        remote_keys = block_kv[:, :feature_width].reshape(block_size, HEADS, HD)
        remote_values = block_kv[:, feature_width:].reshape(block_size, HEADS, HD)
        scores = (
            jnp.einsum("qhd,khd->hqk", query_heads, remote_keys, preferred_element_type=jnp.float32)
            * score_scale
        )
        visible = visible_pairs(
            arrived_users,
            own_places,
            block_users,
            first_row + jnp.arange(block_size, dtype=jnp.int32),
        )
        weights = jnp.where(visible[None], jax.nn.silu(scores), 0.0).astype(jnp.bfloat16)
        summed = jnp.einsum(
            "hqk,khd->qhd", weights, remote_values, preferred_element_type=jnp.float32
        )
        return total_out + summed.reshape(slot_rows, feature_width)

    zero_rows = jnp.zeros((slot_rows, feature_width), jnp.float32)
    shard_piece = (
        lax.all_gather(key_values, "ctx", axis=0, tiled=True),
        lax.all_gather(arrived_users, "ctx", axis=0, tiled=True),
    )
    block_rows = block_length(shard_piece[0].shape[0], slot_rows)
    forward_result = run_blocks(zero_rows, shard_piece, block_rows, forward_step)
    mean_out = jnp.mean(forward_result, axis=1, keepdims=True)
    centered = forward_result - mean_out
    inv_std = lax.rsqrt(jnp.mean(centered * centered, axis=1, keepdims=True) + epsilon)
    normed = centered * inv_std
    unit_float = unit_rows.astype(jnp.float32)
    layer_out = (normed * norm_gain * unit_float).astype(jnp.bfloat16)
    grad_float = grad_output.astype(jnp.float32)
    unit_grads = (grad_float * norm_gain * normed).astype(jnp.bfloat16)
    grad_normed = grad_float * norm_gain * unit_float
    mean_grad = jnp.mean(grad_normed, axis=1, keepdims=True)
    mean_cross = jnp.mean(grad_normed * normed, axis=1, keepdims=True)
    out_grads = (inv_std * (grad_normed - mean_grad - normed * mean_cross)).astype(jnp.bfloat16)

    def backward_step(carry_here, block_part, first_row):
        block_queries, block_grads, block_users = block_part
        block_size = block_queries.shape[0]
        remote_queries = block_queries.reshape(block_size, HEADS, HD)
        remote_grads = block_grads.reshape(block_size, HEADS, HD)
        scores = (
            jnp.einsum(
                "qhd,khd->hqk", remote_queries, key_heads, preferred_element_type=jnp.float32
            )
            * score_scale
        )
        visible = visible_pairs(
            block_users,
            first_row + jnp.arange(block_size, dtype=jnp.int32),
            arrived_users,
            own_places,
        )[None]
        weights = jnp.where(visible, jax.nn.silu(scores), 0.0).astype(jnp.bfloat16)
        weight_grads = jnp.einsum(
            "qhd,khd->hqk", remote_grads, value_heads, preferred_element_type=jnp.float32
        )
        score_grads = jnp.where(
            visible, weight_grads * silu_slope(scores) * score_scale, 0.0
        ).astype(jnp.bfloat16)
        value_sum = jnp.einsum(
            "hqk,qhd->khd", weights, remote_grads, preferred_element_type=jnp.float32
        ).reshape(slot_rows, feature_width)
        key_sum = jnp.einsum(
            "hqk,qhd->khd", score_grads, remote_queries, preferred_element_type=jnp.float32
        ).reshape(slot_rows, feature_width)
        new_keys = carry_here[0] + key_sum
        new_values = carry_here[1] + value_sum
        window_sum = (
            jnp.einsum("hqk,khd->qhd", score_grads, key_heads, preferred_element_type=jnp.float32)
            .reshape(block_size, feature_width)
            .astype(jnp.bfloat16)
        )
        return (
            new_keys,
            new_values,
            lax.dynamic_update_slice_in_dim(carry_here[2], window_sum, first_row, 0),
        )

    start_carry = (zero_rows, zero_rows, jnp.zeros((group_rows, feature_width), jnp.bfloat16))
    shard_piece = (
        lax.all_gather(queries, "ctx", axis=0, tiled=True),
        lax.all_gather(out_grads, "ctx", axis=0, tiled=True),
        lax.all_gather(arrived_users, "ctx", axis=0, tiled=True),
    )
    block_rows = block_length(shard_piece[0].shape[0], slot_rows)
    key_results = run_blocks(start_carry, shard_piece, block_rows, backward_step)
    key_grads = key_results[0]
    value_grads = key_results[1]
    query_grads = lax.psum_scatter(key_results[2], "ctx", scatter_dimension=0, tiled=True).astype(
        jnp.float32
    )
    grads_owned = jnp.concatenate(
        [
            unit_grads,
            query_grads.astype(jnp.bfloat16),
            key_grads.astype(jnp.bfloat16),
            value_grads.astype(jnp.bfloat16),
        ],
        axis=1,
    )
    returned = lax.all_to_all(grads_owned, "dp", split_axis=0, concat_axis=0, tiled=True)
    back_rows = jnp.take(returned, jnp.maximum(send_slot, 0), axis=0)
    grad_read = jnp.where(is_live[:, None], back_rows, jnp.zeros((), jnp.bfloat16))
    return (layer_out, grad_read)


def vmem(count):
    return [pl.BlockSpec(memory_space=pltpu.VMEM)] * count


def smem():
    return pl.BlockSpec(memory_space=pltpu.SMEM)


def dot(left, right, left_dim, right_dim):
    return lax.dot_general(
        left, right, (((left_dim,), (right_dim,)), ((), ())), preferred_element_type=jnp.float32
    )


def slot_kernel(owner_ref, user_ref, proj_ref, send_ref, users_ref, slot_ref, *, per_pair):
    slots = user_ref.shape[1]
    users = user_ref[...]
    owners = jnp.zeros_like(users)
    for user in range(owner_ref.shape[0]):
        owners = jnp.where(users == user, owner_ref[user], owners)
    is_live = users >= 0
    owner_range = lax.broadcasted_iota(jnp.int32, (slots // per_pair, slots), 0)
    hits = (owner_range == owners) & is_live
    earlier = lax.broadcasted_iota(jnp.int32, (slots, slots), 0)
    later = lax.broadcasted_iota(jnp.int32, (slots, slots), 1)
    upto = (earlier <= later).astype(jnp.bfloat16)
    hits_f = hits.astype(jnp.float32)
    running = dot(hits_f.astype(jnp.bfloat16), upto, 1, 0)
    ranks = jnp.sum(hits_f * running, axis=0, keepdims=True).astype(jnp.int32) - 1
    slot = jnp.where(is_live, owners * per_pair + ranks, -1)
    slot_ref[...] = slot
    placed = (earlier == slot).astype(jnp.bfloat16)
    tagged = (users + 1).astype(jnp.float32).astype(jnp.bfloat16)
    tagged = jnp.broadcast_to(tagged, (16, slots))
    users_ref[...] = dot(tagged, placed, 1, 1)[:1]
    for part in range(4):
        width = HEADS * HD
        rows = dot(placed, proj_ref[:, part * width : (part + 1) * width], 1, 0)
        rows = rows.astype(jnp.bfloat16)
        for head in range(HEADS):
            send_ref[head * slots : (head + 1) * slots, part * HD : (part + 1) * HD] = rows[
                :, head * HD : (head + 1) * HD
            ]


def columns_kernel(place_ref, grad_ref, *piece_refs):
    me = place_ref[0]
    for step, piece_ref in enumerate(piece_refs):
        start = pl.multiple_of((me ^ step) * HD, HD)
        piece_ref[...] = grad_ref[:, pl.ds(start, HD)]


def group_kernel(place_ref, users_ref, *refs, per_pair):
    piece_refs, (group_users_ref, grads_ref) = refs[:HEADS], refs[HEADS:]
    me, owner = place_ref[0], place_ref[1]
    readers = users_ref.shape[0] // HEADS
    slots = users_ref.shape[1]
    source = lax.broadcasted_iota(jnp.int32, (slots, slots), 0)
    target = lax.broadcasted_iota(jnp.int32, (slots, slots), 1)
    same_rank = lax.rem(source, per_pair) == lax.rem(target, per_pair)
    spread = (same_rank & (lax.div(source, per_pair) == owner)).astype(jnp.bfloat16)
    mine = dot(users_ref[...].astype(jnp.bfloat16), spread, 1, 0)
    distance = lax.broadcasted_iota(jnp.int32, (readers, slots), 0)
    reader = lax.div(lax.broadcasted_iota(jnp.int32, (readers, slots), 1), per_pair)
    from_reader = reader == (distance ^ owner)
    for step in range(HEADS):
        window = me ^ step
        rows = mine[step * readers : (step + 1) * readers]
        group_users_ref[pl.ds(window, 1), :] = (
            jnp.sum(jnp.where(from_reader, rows, 0.0), axis=0, keepdims=True) - 1.0
        )
        grads_ref[pl.ds(pl.multiple_of(window * slots, slots), slots), :] = piece_refs[step][...]


def visible_block(users_ref, query_window, key_windows):
    size = users_ref.shape[1]
    query_users = jnp.broadcast_to(users_ref[query_window : query_window + 1], (size, size)).T
    blocks = []
    for window in range(key_windows):
        block = (query_users == users_ref[window : window + 1]) & (query_users >= 0.0)
        if window == query_window:
            rows = lax.broadcasted_iota(jnp.int32, (size, size), 0)
            columns = lax.broadcasted_iota(jnp.int32, (size, size), 1)
            block = block & (columns <= rows)
        blocks.append(block)
    return jnp.concatenate(blocks, axis=1)


def forward_kernel(users_ref, rows_ref, grads_ref, gain_ref, attended_ref, stats_ref):
    size = users_ref.shape[1]
    scale = HD ** (-0.5)
    lane = lax.broadcasted_iota(jnp.int32, (size, HD), 1)
    for window in range(users_ref.shape[0]):
        here = slice(window * size, (window + 1) * size)
        upto = slice(0, (window + 1) * size)
        queries = rows_ref[here, HD : 2 * HD]
        scores = dot(queries, rows_ref[upto, 2 * HD : 3 * HD], 1, 1) * scale
        visible = visible_block(users_ref, window, window + 1)
        weights = jnp.where(visible, scores * jax.nn.sigmoid(scores), 0.0).astype(jnp.bfloat16)
        attended = dot(weights, rows_ref[upto, 3 * HD :], 1, 0)
        attended_ref[here] = attended
        grad_normed = (
            grads_ref[here].astype(jnp.float32)
            * gain_ref[...]
            * rows_ref[here, :HD].astype(jnp.float32)
        )
        mean = jnp.mean(attended, axis=1, keepdims=True)
        centered = attended - mean
        spread = jnp.sum(centered * centered, axis=1, keepdims=True)
        grad_sum = jnp.sum(grad_normed, axis=1, keepdims=True)
        cross = jnp.sum(grad_normed * centered, axis=1, keepdims=True)
        packed = jnp.where(
            lane == 0, mean, jnp.where(lane == 1, spread, jnp.where(lane == 2, grad_sum, cross))
        )
        stats_ref[:, here] = packed.T[:8]


def backward_kernel(
    place_ref, users_ref, rows_ref, grads_ref, gain_ref, attended_ref, *refs
):
    stats_refs = refs[:HEADS]
    out_ref = refs[HEADS]
    layer_refs = refs[HEADS + 1 : 2 * HEADS + 1]
    layer_all, out_grads_all, key_sum, value_sum = refs[2 * HEADS + 1 :]
    me = place_ref[0]
    size = users_ref.shape[1]
    windows = users_ref.shape[0]
    scale = HD ** (-0.5)
    width = float(HEADS * HD)
    stats = [stat_ref[...] for stat_ref in stats_refs]
    mean = sum(stat[0:1] for stat in stats) * (1.0 / HEADS)
    spread = sum(stat[1:2] + HD * (stat[0:1] - mean) * (stat[0:1] - mean) for stat in stats)
    inv_std = lax.rsqrt(spread / width + epsilon)
    mean_grad = sum(stat[2:3] for stat in stats) / width
    cross = sum(stat[3:4] + (stat[0:1] - mean) * stat[2:3] for stat in stats)
    mean_cross = cross * inv_std / width
    key_sum[...] = jnp.zeros_like(key_sum)
    value_sum[...] = jnp.zeros_like(value_sum)
    row = lax.broadcasted_iota(jnp.int32, (size, size), 0)
    for window in range(windows):
        here = slice(window * size, (window + 1) * size)
        upto = slice(0, (window + 1) * size)
        packed = jnp.where(
            row == 0,
            mean[:, here],
            jnp.where(
                row == 1,
                inv_std[:, here],
                jnp.where(row == 2, mean_grad[:, here], mean_cross[:, here]),
            ),
        ).T
        unit = rows_ref[here, :HD].astype(jnp.float32)
        grad_gain = grads_ref[here].astype(jnp.float32) * gain_ref[...]
        normed = (attended_ref[here] - packed[:, 0:1]) * packed[:, 1:2]
        layer_all[here] = (normed * gain_ref[...] * unit).astype(jnp.bfloat16)
        out_ref[here, :HD] = (grad_gain * normed).astype(jnp.bfloat16)
        out_grads = (
            packed[:, 1:2] * (grad_gain * unit - packed[:, 2:3] - normed * packed[:, 3:4])
        ).astype(jnp.bfloat16)
        queries = rows_ref[here, HD : 2 * HD]
        keys = rows_ref[upto, 2 * HD : 3 * HD]
        scores = dot(queries, keys, 1, 1) * scale
        visible = visible_block(users_ref, window, window + 1)
        sigmoid = jax.nn.sigmoid(scores)
        weights = jnp.where(visible, scores * sigmoid, 0.0).astype(jnp.bfloat16)
        slope = jnp.where(visible, sigmoid * (1.0 + scores * (1.0 - sigmoid)) * scale, 0.0)
        score_grads = (dot(out_grads, rows_ref[upto, 3 * HD :], 1, 1) * slope).astype(jnp.bfloat16)
        out_ref[here, HD : 2 * HD] = dot(score_grads, keys, 1, 0).astype(jnp.bfloat16)
        key_sum[upto] += dot(score_grads, queries, 0, 0)
        value_sum[upto] += dot(weights, out_grads, 0, 0)
    out_ref[:, 2 * HD : 3 * HD] = key_sum[...].astype(jnp.bfloat16)
    out_ref[:, 3 * HD :] = value_sum[...].astype(jnp.bfloat16)
    for step, layer_ref in enumerate(layer_refs):
        start = pl.multiple_of((me ^ step) * size, size)
        layer_ref[...] = layer_all[pl.ds(start, size), :]


def unslot_kernel(place_ref, slot_ref, returned_ref, *refs):
    piece_refs, (layer_ref, grad_ref) = refs[:HEADS], refs[HEADS:]
    me = place_ref[0]
    slots = slot_ref.shape[1]
    width = HEADS * HD
    placed = (
        lax.broadcasted_iota(jnp.int32, (slots, slots), 0) == slot_ref[...]
    ).astype(jnp.bfloat16)
    for head in range(HEADS):
        rows = dot(placed, returned_ref[head * slots : (head + 1) * slots], 0, 0)
        rows = rows.astype(jnp.bfloat16)
        for part in range(4):
            start = part * width + head * HD
            grad_ref[:, start : start + HD] = rows[:, part * HD : (part + 1) * HD]
    for step, piece_ref in enumerate(piece_refs):
        start = pl.multiple_of((me ^ step) * HD, HD)
        layer_ref[:, pl.ds(start, HD)] = piece_ref[...]


def swap(value, axis, distance):
    pairs = [(index, index ^ distance) for index in range(lax.axis_size(axis))]
    return lax.ppermute(value, axis, pairs)


def by_heads(proj_read, norm_gain, owner_of, user_of, grad_output):
    slots = proj_read.shape[0]
    readers = lax.axis_size("dp")
    per_pair = slots // readers
    group_rows = slots * HEADS
    width = 4 * HD
    me = lax.axis_index("ctx")
    place = jnp.stack([me, lax.axis_index("dp")]).astype(jnp.int32)
    gain = lax.dynamic_slice_in_dim(norm_gain, me * HD, HD, 0).reshape(1, HD)
    rows_shape = jax.ShapeDtypeStruct((group_rows, width), jnp.bfloat16)
    piece_shape = jax.ShapeDtypeStruct((slots, HD), jnp.bfloat16)
    outgoing, slot_users, slot = pl.pallas_call(
        functools.partial(slot_kernel, per_pair=per_pair),
        out_shape=(
            rows_shape,
            jax.ShapeDtypeStruct((1, slots), jnp.float32),
            jax.ShapeDtypeStruct((1, slots), jnp.int32),
        ),
        in_specs=[smem()] + vmem(2),
        out_specs=tuple(vmem(3)),
        name="slot_rows",
    )(owner_of, user_of.reshape(1, slots), proj_read)
    rows = lax.all_to_all(outgoing, ("ctx", "dp"), split_axis=0, concat_axis=0, tiled=True)
    pieces = pl.pallas_call(
        columns_kernel,
        out_shape=(piece_shape,) * HEADS,
        in_specs=[smem()] + vmem(1),
        out_specs=tuple(vmem(HEADS)),
        name="cut_columns",
    )(place, grad_output)
    users = slot_users
    for axis in ("dp", "ctx"):
        distance = 1
        while distance < lax.axis_size(axis):
            users = jnp.concatenate([users, swap(users, axis, distance)], axis=0)
            distance *= 2
    pieces = (pieces[0],) + tuple(swap(pieces[step], "ctx", step) for step in range(1, HEADS))
    group_users, grads = pl.pallas_call(
        functools.partial(group_kernel, per_pair=per_pair),
        out_shape=(
            jax.ShapeDtypeStruct((HEADS, slots), jnp.float32),
            jax.ShapeDtypeStruct((group_rows, HD), jnp.bfloat16),
        ),
        in_specs=[smem()] + vmem(1 + HEADS),
        out_specs=tuple(vmem(2)),
        name="lay_group",
    )(place, users, *pieces)
    attended, stats = pl.pallas_call(
        forward_kernel,
        out_shape=(
            jax.ShapeDtypeStruct((group_rows, HD), jnp.float32),
            jax.ShapeDtypeStruct((8, group_rows), jnp.float32),
        ),
        in_specs=vmem(4),
        out_specs=tuple(vmem(2)),
        name="forward",
    )(group_users, rows, grads, gain)
    all_stats = (stats,) + tuple(swap(stats, "ctx", step) for step in range(1, HEADS))
    results = pl.pallas_call(
        backward_kernel,
        out_shape=(rows_shape,) + (piece_shape,) * HEADS,
        in_specs=[smem()] + vmem(5 + HEADS),
        out_specs=tuple(vmem(1 + HEADS)),
        scratch_shapes=[
            pltpu.VMEM((group_rows, HD), jnp.bfloat16),
            pltpu.VMEM((group_rows, HD), jnp.bfloat16),
            pltpu.VMEM((group_rows, HD), jnp.float32),
            pltpu.VMEM((group_rows, HD), jnp.float32),
        ],
        name="backward",
    )(place, group_users, rows, grads, gain, attended, *all_stats)
    grads_owned, layers = results[0], results[1:]
    returned = lax.all_to_all(grads_owned, ("ctx", "dp"), split_axis=0, concat_axis=0, tiled=True)
    layers = (layers[0],) + tuple(swap(layers[step], "ctx", step) for step in range(1, HEADS))
    return pl.pallas_call(
        unslot_kernel,
        out_shape=(
            jax.ShapeDtypeStruct((slots, HEADS * HD), jnp.bfloat16),
            jax.ShapeDtypeStruct((slots, 4 * HEADS * HD), jnp.bfloat16),
        ),
        in_specs=[smem()] + vmem(2 + HEADS),
        out_specs=tuple(vmem(2)),
        name="unslot_rows",
    )(place, slot, returned, *layers)


def solution(mesh):
    in_specs = (P(("dp", "ctx"), None), P(), P(), P(("dp", "ctx")), P(("dp", "ctx"), None))
    out_specs = (P(("dp", "ctx"), None), P(("dp", "ctx"), None))
    local = by_heads if mesh.shape["ctx"] == HEADS else windowed
    return jax.shard_map(local, mesh=mesh, in_specs=in_specs, out_specs=out_specs, check_vma=False)
```

```python
import functools

import jax
import jax.numpy as jnp
from jax import lax
from jax.experimental import pallas as pl
from jax.experimental.pallas import tpu as pltpu
from jax.sharding import PartitionSpec as P

HEADS = 4
HD = 128


epsilon = 1e-05


def block_length(total_rows, shard_rows):
    shard_total = total_rows // shard_rows
    best_factor = 1
    for factor in range(1, shard_total + 1):
        if shard_total % factor == 0 and factor * shard_rows <= 1024:
            best_factor = factor
    return best_factor * shard_rows


def silu_slope(scores):
    sigmoid_part = jax.nn.sigmoid(scores)
    return sigmoid_part * (1.0 + scores * (1.0 - sigmoid_part))


def visible_pairs(query_users, query_places, key_users, key_places):
    same_user = (query_users[:, None] == key_users[None, :]) & (query_users[:, None] >= 0)
    return same_user & (key_places[None, :] <= query_places[:, None])


def run_blocks(carry_now, shard_piece, block_rows, step_fn):
    total_rows = shard_piece[0].shape[0]

    def one_block(block_index, carry_here):
        offset = block_index * block_rows
        block_part = tuple(
            (
                lax.dynamic_slice_in_dim(array_item, offset, block_rows, 0)
                for array_item in shard_piece
            )
        )
        return step_fn(carry_here, block_part, offset)

    return lax.fori_loop(0, total_rows // block_rows, one_block, carry_now)


def windowed(proj_read, norm_gain, owner_of, user_of, grad_output):
    slot_rows = proj_read.shape[0]
    reader_peers = lax.axis_size("dp")
    per_pair = slot_rows // reader_peers
    feature_width = HEADS * HD
    score_scale = HD ** (-0.5)
    group_rows = slot_rows * lax.axis_size("ctx")
    user_range = jnp.arange(owner_of.shape[0], dtype=jnp.int32)
    owners = jnp.sum(
        jnp.where(user_of[:, None] == user_range[None, :], owner_of[None, :], 0), axis=1
    )
    is_live = user_of >= 0
    owner_hits = (owners[:, None] == jnp.arange(reader_peers, dtype=jnp.int32)[None, :]) & is_live[
        :, None
    ]
    running = jnp.cumsum(owner_hits.astype(jnp.int32), axis=0) - 1
    ranks_mine = jnp.sum(jnp.where(owner_hits, running, 0), axis=1)
    send_slot = jnp.where(is_live, owners * per_pair + ranks_mine, -1)
    slot_range = jnp.arange(slot_rows, dtype=jnp.int32)
    slot_match = send_slot[None, :] == slot_range[:, None]
    filled = jnp.any(slot_match, axis=1)
    source_row = jnp.sum(jnp.where(slot_match, slot_range[None, :], 0), axis=1)
    outgoing = jnp.where(
        filled[:, None], jnp.take(proj_read, source_row, axis=0), jnp.zeros((), jnp.bfloat16)
    )
    outgoing_users = jnp.where(filled, jnp.take(user_of, source_row), -1)
    arrived, arrived_users = (
        lax.all_to_all(outgoing, "dp", split_axis=0, concat_axis=0, tiled=True),
        lax.all_to_all(outgoing_users, "dp", split_axis=0, concat_axis=0, tiled=True),
    )
    own_start = lax.axis_index("ctx") * slot_rows
    own_places = own_start + slot_range
    unit_rows = arrived[:, :feature_width]
    queries = arrived[:, feature_width : 2 * feature_width]
    key_values = arrived[:, 2 * feature_width :]
    query_heads = queries.reshape(slot_rows, HEADS, HD)
    key_heads = key_values[:, :feature_width].reshape(slot_rows, HEADS, HD)
    value_heads = key_values[:, feature_width:].reshape(slot_rows, HEADS, HD)

    def forward_step(total_out, block_part, first_row):
        block_kv, block_users = block_part
        block_size = block_kv.shape[0]
        remote_keys = block_kv[:, :feature_width].reshape(block_size, HEADS, HD)
        remote_values = block_kv[:, feature_width:].reshape(block_size, HEADS, HD)
        scores = (
            jnp.einsum("qhd,khd->hqk", query_heads, remote_keys, preferred_element_type=jnp.float32)
            * score_scale
        )
        visible = visible_pairs(
            arrived_users,
            own_places,
            block_users,
            first_row + jnp.arange(block_size, dtype=jnp.int32),
        )
        weights = jnp.where(visible[None], jax.nn.silu(scores), 0.0).astype(jnp.bfloat16)
        summed = jnp.einsum(
            "hqk,khd->qhd", weights, remote_values, preferred_element_type=jnp.float32
        )
        return total_out + summed.reshape(slot_rows, feature_width)

    zero_rows = jnp.zeros((slot_rows, feature_width), jnp.float32)
    shard_piece = (
        lax.all_gather(key_values, "ctx", axis=0, tiled=True),
        lax.all_gather(arrived_users, "ctx", axis=0, tiled=True),
    )
    block_rows = block_length(shard_piece[0].shape[0], slot_rows)
    forward_result = run_blocks(zero_rows, shard_piece, block_rows, forward_step)
    mean_out = jnp.mean(forward_result, axis=1, keepdims=True)
    centered = forward_result - mean_out
    inv_std = lax.rsqrt(jnp.mean(centered * centered, axis=1, keepdims=True) + epsilon)
    normed = centered * inv_std
    unit_float = unit_rows.astype(jnp.float32)
    layer_out = (normed * norm_gain * unit_float).astype(jnp.bfloat16)
    grad_float = grad_output.astype(jnp.float32)
    unit_grads = (grad_float * norm_gain * normed).astype(jnp.bfloat16)
    grad_normed = grad_float * norm_gain * unit_float
    mean_grad = jnp.mean(grad_normed, axis=1, keepdims=True)
    mean_cross = jnp.mean(grad_normed * normed, axis=1, keepdims=True)
    out_grads = (inv_std * (grad_normed - mean_grad - normed * mean_cross)).astype(jnp.bfloat16)

    def backward_step(carry_here, block_part, first_row):
        block_queries, block_grads, block_users = block_part
        block_size = block_queries.shape[0]
        remote_queries = block_queries.reshape(block_size, HEADS, HD)
        remote_grads = block_grads.reshape(block_size, HEADS, HD)
        scores = (
            jnp.einsum(
                "qhd,khd->hqk", remote_queries, key_heads, preferred_element_type=jnp.float32
            )
            * score_scale
        )
        visible = visible_pairs(
            block_users,
            first_row + jnp.arange(block_size, dtype=jnp.int32),
            arrived_users,
            own_places,
        )[None]
        weights = jnp.where(visible, jax.nn.silu(scores), 0.0).astype(jnp.bfloat16)
        weight_grads = jnp.einsum(
            "qhd,khd->hqk", remote_grads, value_heads, preferred_element_type=jnp.float32
        )
        score_grads = jnp.where(
            visible, weight_grads * silu_slope(scores) * score_scale, 0.0
        ).astype(jnp.bfloat16)
        value_sum = jnp.einsum(
            "hqk,qhd->khd", weights, remote_grads, preferred_element_type=jnp.float32
        ).reshape(slot_rows, feature_width)
        key_sum = jnp.einsum(
            "hqk,qhd->khd", score_grads, remote_queries, preferred_element_type=jnp.float32
        ).reshape(slot_rows, feature_width)
        new_keys = carry_here[0] + key_sum
        new_values = carry_here[1] + value_sum
        window_sum = (
            jnp.einsum("hqk,khd->qhd", score_grads, key_heads, preferred_element_type=jnp.float32)
            .reshape(block_size, feature_width)
            .astype(jnp.bfloat16)
        )
        return (
            new_keys,
            new_values,
            lax.dynamic_update_slice_in_dim(carry_here[2], window_sum, first_row, 0),
        )

    start_carry = (zero_rows, zero_rows, jnp.zeros((group_rows, feature_width), jnp.bfloat16))
    shard_piece = (
        lax.all_gather(queries, "ctx", axis=0, tiled=True),
        lax.all_gather(out_grads, "ctx", axis=0, tiled=True),
        lax.all_gather(arrived_users, "ctx", axis=0, tiled=True),
    )
    block_rows = block_length(shard_piece[0].shape[0], slot_rows)
    key_results = run_blocks(start_carry, shard_piece, block_rows, backward_step)
    key_grads = key_results[0]
    value_grads = key_results[1]
    query_grads = lax.psum_scatter(key_results[2], "ctx", scatter_dimension=0, tiled=True).astype(
        jnp.float32
    )
    grads_owned = jnp.concatenate(
        [
            unit_grads,
            query_grads.astype(jnp.bfloat16),
            key_grads.astype(jnp.bfloat16),
            value_grads.astype(jnp.bfloat16),
        ],
        axis=1,
    )
    returned = lax.all_to_all(grads_owned, "dp", split_axis=0, concat_axis=0, tiled=True)
    back_rows = jnp.take(returned, jnp.maximum(send_slot, 0), axis=0)
    grad_read = jnp.where(is_live[:, None], back_rows, jnp.zeros((), jnp.bfloat16))
    return (layer_out, grad_read)


LIMIT = pltpu.CompilerParams(vmem_limit_bytes=16 * 2**20)


def device_of(owner, head):
    return (owner & ~1) | (head & 1), ((owner & 1) << 1) | (head >> 1)


def turned(index):
    return ((index & 1) << 1) | (index >> 1)


def vmem(count):
    return [pl.BlockSpec(memory_space=pltpu.VMEM)] * count


def smem():
    return pl.BlockSpec(memory_space=pltpu.SMEM)


def dot(left, right, left_dim, right_dim):
    return lax.dot_general(
        left, right, (((left_dim,), (right_dim,)), ((), ())), preferred_element_type=jnp.float32
    )


def owners_of(users, owner_ref):
    owners = jnp.zeros_like(users)
    for user in range(owner_ref.shape[0]):
        owners = jnp.where(users == user, owner_ref[user], owners)
    return owners


def lower_ones(size):
    earlier = lax.broadcasted_iota(jnp.int32, (size, size), 0)
    later = lax.broadcasted_iota(jnp.int32, (size, size), 1)
    return (earlier <= later).astype(jnp.bfloat16)


def slot_kernel(owner_ref, user_ref, proj_ref, send_ref, slot_ref, *, per_pair):
    slots = user_ref.shape[1]
    readers = slots // per_pair
    users = user_ref[...]
    owners = owners_of(users, owner_ref)
    is_live = users >= 0
    owner_range = lax.broadcasted_iota(jnp.int32, (readers, slots), 0)
    hits = ((owner_range == owners) & is_live).astype(jnp.float32)
    running = dot(hits.astype(jnp.bfloat16), lower_ones(slots), 1, 0)
    ranks = jnp.sum(hits * running, axis=0, keepdims=True).astype(jnp.int32) - 1
    slot = jnp.where(is_live, owners * per_pair + ranks, -1)
    slot_ref[...] = slot
    placed = (lax.broadcasted_iota(jnp.int32, (slots, slots), 0) == slot).astype(jnp.bfloat16)
    for part in range(4):
        width = HEADS * HD
        rows = dot(placed, proj_ref[:, part * width : (part + 1) * width], 1, 0)
        rows = rows.astype(jnp.bfloat16)
        for owner in range(readers):
            for head in range(HEADS):
                dp_index, ctx_index = device_of(owner, head)
                start = (ctx_index * readers + dp_index) * per_pair
                send_ref[start : start + per_pair, part * HD : (part + 1) * HD] = rows[
                    owner * per_pair : (owner + 1) * per_pair, head * HD : (head + 1) * HD
                ]


def columns_kernel(place_ref, grad_ref, *piece_refs):
    first = turned(place_ref[3])
    for step, piece_ref in enumerate(piece_refs):
        start = pl.multiple_of((first ^ step) * HD, HD)
        piece_ref[...] = grad_ref[:, pl.ds(start, HD)]


def group_kernel(place_ref, owner_ref, users_ref, *refs, per_pair):
    piece_refs, (group_users_ref, grads_ref) = refs[:HEADS], refs[HEADS:]
    head, owner, my_dp, my_ctx = [place_ref[index] for index in range(4)]
    count, slots = users_ref.shape
    readers = count // HEADS
    users = users_ref[...]
    hits = (owners_of(users, owner_ref) == owner) & (users >= 0)
    running = dot(hits.astype(jnp.float32).astype(jnp.bfloat16), lower_ones(slots), 1, 0)
    ranks = jnp.where(hits, running - 1.0, -1.0)
    tagged = (users + 1).astype(jnp.float32)
    lane = lax.broadcasted_iota(jnp.int32, (count, slots), 1)
    rank_here = lax.rem(lane, per_pair)
    spread = jnp.zeros((count, slots), jnp.float32)
    for rank in range(per_pair):
        user = jnp.sum(jnp.where(ranks == float(rank), tagged, 0.0), axis=1, keepdims=True)
        spread = jnp.where(rank_here == rank, user, spread)
    order = lax.rem(lax.broadcasted_iota(jnp.int32, (count, slots), 0), readers)
    half = readers // 2
    distance = 2 * lax.rem(order, half) + lax.div(order, half)
    spread = jnp.where(lax.div(lane, per_pair) == (distance ^ my_dp), spread, 0.0)
    for step in range(HEADS):
        group_users_ref[pl.ds(my_ctx ^ step, 1), :] = (
            jnp.sum(spread[step * readers : (step + 1) * readers], axis=0, keepdims=True) - 1.0
        )
        window = turned(head ^ step)
        grads_ref[pl.ds(pl.multiple_of(window * slots, slots), slots), :] = piece_refs[step][...]


def visible_block(users_ref, query_window, key_windows):
    size = users_ref.shape[1]
    query_users = jnp.broadcast_to(users_ref[query_window : query_window + 1], (size, size)).T
    blocks = []
    for window in range(key_windows):
        block = (query_users == users_ref[window : window + 1]) & (query_users >= 0.0)
        if window == query_window:
            rows = lax.broadcasted_iota(jnp.int32, (size, size), 0)
            columns = lax.broadcasted_iota(jnp.int32, (size, size), 1)
            block = block & (columns <= rows)
        blocks.append(block)
    return jnp.concatenate(blocks, axis=1)


def forward_kernel(users_ref, rows_ref, grads_ref, gain_ref, attended_ref, stats_ref):
    size = users_ref.shape[1]
    scale = HD ** (-0.5)
    lane = lax.broadcasted_iota(jnp.int32, (size, HD), 1)
    for window in range(users_ref.shape[0]):
        here = slice(window * size, (window + 1) * size)
        upto = slice(0, (window + 1) * size)
        queries = rows_ref[here, HD : 2 * HD]
        scores = dot(queries, rows_ref[upto, 2 * HD : 3 * HD], 1, 1) * scale
        visible = visible_block(users_ref, window, window + 1)
        weights = jnp.where(visible, scores * jax.nn.sigmoid(scores), 0.0).astype(jnp.bfloat16)
        attended = dot(weights, rows_ref[upto, 3 * HD :], 1, 0)
        attended_ref[here] = attended
        grad_normed = (
            grads_ref[here].astype(jnp.float32)
            * gain_ref[...]
            * rows_ref[here, :HD].astype(jnp.float32)
        )
        mean = jnp.mean(attended, axis=1, keepdims=True)
        centered = attended - mean
        spread = jnp.sum(centered * centered, axis=1, keepdims=True)
        grad_sum = jnp.sum(grad_normed, axis=1, keepdims=True)
        cross = jnp.sum(grad_normed * centered, axis=1, keepdims=True)
        packed = jnp.where(
            lane == 0, mean, jnp.where(lane == 1, spread, jnp.where(lane == 2, grad_sum, cross))
        )
        stats_ref[:, here] = packed.T[:8]


def backward_kernel(
    place_ref, users_ref, rows_ref, grads_ref, gain_ref, attended_ref, *refs
):
    stats_refs = refs[:HEADS]
    out_ref = refs[HEADS]
    layer_refs = refs[HEADS + 1 : 2 * HEADS + 1]
    layer_all, key_sum, value_sum = refs[2 * HEADS + 1 :]
    head = place_ref[0]
    size = users_ref.shape[1]
    windows = users_ref.shape[0]
    scale = HD ** (-0.5)
    width = float(HEADS * HD)
    stats = [stat_ref[...] for stat_ref in stats_refs]
    mean = sum(stat[0:1] for stat in stats) * (1.0 / HEADS)
    spread = sum(stat[1:2] + HD * (stat[0:1] - mean) * (stat[0:1] - mean) for stat in stats)
    inv_std = lax.rsqrt(spread / width + epsilon)
    mean_grad = sum(stat[2:3] for stat in stats) / width
    cross = sum(stat[3:4] + (stat[0:1] - mean) * stat[2:3] for stat in stats)
    mean_cross = cross * inv_std / width
    key_sum[...] = jnp.zeros_like(key_sum)
    value_sum[...] = jnp.zeros_like(value_sum)
    row = lax.broadcasted_iota(jnp.int32, (size, size), 0)
    for window in range(windows):
        here = slice(window * size, (window + 1) * size)
        upto = slice(0, (window + 1) * size)
        packed = jnp.where(
            row == 0,
            mean[:, here],
            jnp.where(
                row == 1,
                inv_std[:, here],
                jnp.where(row == 2, mean_grad[:, here], mean_cross[:, here]),
            ),
        ).T
        unit = rows_ref[here, :HD].astype(jnp.float32)
        grad_gain = grads_ref[here].astype(jnp.float32) * gain_ref[...]
        normed = (attended_ref[here] - packed[:, 0:1]) * packed[:, 1:2]
        layer_all[here] = (normed * gain_ref[...] * unit).astype(jnp.bfloat16)
        out_ref[here, :HD] = (grad_gain * normed).astype(jnp.bfloat16)
        out_grads = (
            packed[:, 1:2] * (grad_gain * unit - packed[:, 2:3] - normed * packed[:, 3:4])
        ).astype(jnp.bfloat16)
        queries = rows_ref[here, HD : 2 * HD]
        keys = rows_ref[upto, 2 * HD : 3 * HD]
        scores = dot(queries, keys, 1, 1) * scale
        visible = visible_block(users_ref, window, window + 1)
        sigmoid = jax.nn.sigmoid(scores)
        weights = jnp.where(visible, scores * sigmoid, 0.0).astype(jnp.bfloat16)
        slope = jnp.where(visible, sigmoid * (1.0 + scores * (1.0 - sigmoid)) * scale, 0.0)
        score_grads = (dot(out_grads, rows_ref[upto, 3 * HD :], 1, 1) * slope).astype(jnp.bfloat16)
        out_ref[here, HD : 2 * HD] = dot(score_grads, keys, 1, 0).astype(jnp.bfloat16)
        key_sum[upto] += dot(score_grads, queries, 0, 0)
        value_sum[upto] += dot(weights, out_grads, 0, 0)
    out_ref[:, 2 * HD : 3 * HD] = key_sum[...].astype(jnp.bfloat16)
    out_ref[:, 3 * HD :] = value_sum[...].astype(jnp.bfloat16)
    for step, layer_ref in enumerate(layer_refs):
        start = pl.multiple_of(turned(head ^ step) * size, size)
        layer_ref[...] = layer_all[pl.ds(start, size), :]


def unslot_kernel(place_ref, slot_ref, returned_ref, *refs, per_pair):
    piece_refs, (layer_ref, grad_ref) = refs[:HEADS], refs[HEADS:]
    slots = slot_ref.shape[1]
    readers = slots // per_pair
    width = HEADS * HD
    placed = (
        lax.broadcasted_iota(jnp.int32, (slots, slots), 0) == slot_ref[...]
    ).astype(jnp.bfloat16)
    for head in range(HEADS):
        chunks = []
        for owner in range(readers):
            dp_index, ctx_index = device_of(owner, head)
            start = (ctx_index * readers + dp_index) * per_pair
            chunks.append(returned_ref[start : start + per_pair])
        rows = dot(placed, jnp.concatenate(chunks, axis=0), 0, 0).astype(jnp.bfloat16)
        for part in range(4):
            start = part * width + head * HD
            grad_ref[:, start : start + HD] = rows[:, part * HD : (part + 1) * HD]
    first = turned(place_ref[3])
    for step, piece_ref in enumerate(piece_refs):
        start = pl.multiple_of((first ^ step) * HD, HD)
        layer_ref[:, pl.ds(start, HD)] = piece_ref[...]


def send(value, target, back=False):
    width = lax.axis_size("ctx")
    pairs = []
    for dp_index in range(lax.axis_size("dp")):
        for ctx_index in range(width):
            to_dp, to_ctx = target(dp_index, ctx_index)
            pair = (dp_index * width + ctx_index, to_dp * width + to_ctx)
            pairs.append(pair[::-1] if back else pair)
    return lax.ppermute(value, ("dp", "ctx"), pairs)


def swap(value, dp_bits, ctx_bits):
    return send(value, lambda dp_index, ctx_index: (dp_index ^ dp_bits, ctx_index ^ ctx_bits))


def regroup(pieces, back=False):
    moved = []
    for step, piece in enumerate(pieces):

        def target(dp_index, ctx_index, step=step):
            return device_of(dp_index, turned(ctx_index) ^ step)

        moved.append(send(piece, target, back))
    return moved


def by_heads(proj_read, norm_gain, owner_of, user_of, grad_output):
    slots = proj_read.shape[0]
    readers = lax.axis_size("dp")
    per_pair = slots // readers
    group_rows = slots * HEADS
    width = 4 * HD
    my_dp, my_ctx = lax.axis_index("dp"), lax.axis_index("ctx")
    head = ((my_ctx & 1) << 1) | (my_dp & 1)
    owner = (my_dp & ~1) | (my_ctx >> 1)
    place = jnp.stack([head, owner, my_dp, my_ctx]).astype(jnp.int32)
    gain = lax.dynamic_slice_in_dim(norm_gain, head * HD, HD, 0).reshape(1, HD)
    rows_shape = jax.ShapeDtypeStruct((group_rows, width), jnp.bfloat16)
    piece_shape = jax.ShapeDtypeStruct((slots, HD), jnp.bfloat16)
    user_row = user_of.reshape(1, slots)
    users = [user_row] + [swap(user_row, bits, 0) for bits in range(2, readers, 2)]
    users = jnp.concatenate(users, axis=0)
    outgoing, slot = pl.pallas_call(
        functools.partial(slot_kernel, per_pair=per_pair),
        out_shape=(
            rows_shape,
            jax.ShapeDtypeStruct((1, slots), jnp.int32),
        ),
        in_specs=[smem()] + vmem(2),
        out_specs=tuple(vmem(2)),
        compiler_params=LIMIT,
        name="slot_rows",
    )(owner_of, user_row, proj_read)
    outgoing, users = lax.optimization_barrier((outgoing, users))
    rows = lax.all_to_all(outgoing, ("ctx", "dp"), split_axis=0, concat_axis=0, tiled=True)
    users = jnp.concatenate([users, swap(users, 1, 0)], axis=0)
    users = jnp.concatenate(
        [users] + [swap(users, 0, bits) for bits in range(1, HEADS)], axis=0
    )
    pieces = pl.pallas_call(
        columns_kernel,
        out_shape=(piece_shape,) * HEADS,
        in_specs=[smem()] + vmem(1),
        out_specs=tuple(vmem(HEADS)),
        compiler_params=LIMIT,
        name="cut_columns",
    )(place, grad_output)
    group_users, grads = pl.pallas_call(
        functools.partial(group_kernel, per_pair=per_pair),
        out_shape=(
            jax.ShapeDtypeStruct((HEADS, slots), jnp.float32),
            jax.ShapeDtypeStruct((group_rows, HD), jnp.bfloat16),
        ),
        in_specs=[smem(), smem()] + vmem(1 + HEADS),
        out_specs=tuple(vmem(2)),
        compiler_params=LIMIT,
        name="lay_group",
    )(place, owner_of, users, *regroup(pieces))
    attended, stats = pl.pallas_call(
        forward_kernel,
        out_shape=(
            jax.ShapeDtypeStruct((group_rows, HD), jnp.float32),
            jax.ShapeDtypeStruct((8, group_rows), jnp.float32),
        ),
        in_specs=vmem(4),
        out_specs=tuple(vmem(2)),
        compiler_params=LIMIT,
        name="forward",
    )(group_users, rows, grads, gain)
    all_stats = [stats, swap(stats, 1, 0), swap(stats, 0, 1), swap(stats, 1, 1)]
    results = pl.pallas_call(
        backward_kernel,
        out_shape=(rows_shape,) + (piece_shape,) * HEADS,
        in_specs=[smem()] + vmem(5 + HEADS),
        out_specs=tuple(vmem(1 + HEADS)),
        scratch_shapes=[
            pltpu.VMEM((group_rows, HD), jnp.bfloat16),
            pltpu.VMEM((group_rows, HD), jnp.float32),
            pltpu.VMEM((group_rows, HD), jnp.float32),
        ],
        compiler_params=LIMIT,
        name="backward",
    )(place, group_users, rows, grads, gain, attended, *all_stats)
    returned = lax.all_to_all(results[0], ("ctx", "dp"), split_axis=0, concat_axis=0, tiled=True)
    return pl.pallas_call(
        functools.partial(unslot_kernel, per_pair=per_pair),
        out_shape=(
            jax.ShapeDtypeStruct((slots, HEADS * HD), jnp.bfloat16),
            jax.ShapeDtypeStruct((slots, 4 * HEADS * HD), jnp.bfloat16),
        ),
        in_specs=[smem()] + vmem(2 + HEADS),
        out_specs=tuple(vmem(2)),
        compiler_params=LIMIT,
        name="unslot_rows",
    )(place, slot, returned, *regroup(results[1:], back=True))


def solution(mesh):
    in_specs = (P(("dp", "ctx"), None), P(), P(), P(("dp", "ctx")), P(("dp", "ctx"), None))
    out_specs = (P(("dp", "ctx"), None), P(("dp", "ctx"), None))
    local = by_heads if mesh.shape["ctx"] == HEADS else windowed
    return jax.shard_map(local, mesh=mesh, in_specs=in_specs, out_specs=out_specs, check_vma=False)
```

```python
import functools

import jax
import jax.numpy as jnp
from jax import lax
from jax.experimental import pallas as pl
from jax.experimental.pallas import tpu as pltpu
from jax.sharding import PartitionSpec as P

HEADS = 4
HD = 128


epsilon = 1e-05


def block_length(total_rows, shard_rows):
    shard_total = total_rows // shard_rows
    best_factor = 1
    for factor in range(1, shard_total + 1):
        if shard_total % factor == 0 and factor * shard_rows <= 1024:
            best_factor = factor
    return best_factor * shard_rows


def silu_slope(scores):
    sigmoid_part = jax.nn.sigmoid(scores)
    return sigmoid_part * (1.0 + scores * (1.0 - sigmoid_part))


def visible_pairs(query_users, query_places, key_users, key_places):
    same_user = (query_users[:, None] == key_users[None, :]) & (query_users[:, None] >= 0)
    return same_user & (key_places[None, :] <= query_places[:, None])


def run_blocks(carry_now, shard_piece, block_rows, step_fn):
    total_rows = shard_piece[0].shape[0]

    def one_block(block_index, carry_here):
        offset = block_index * block_rows
        block_part = tuple(
            (
                lax.dynamic_slice_in_dim(array_item, offset, block_rows, 0)
                for array_item in shard_piece
            )
        )
        return step_fn(carry_here, block_part, offset)

    return lax.fori_loop(0, total_rows // block_rows, one_block, carry_now)


def windowed(proj_read, norm_gain, owner_of, user_of, grad_output):
    slot_rows = proj_read.shape[0]
    reader_peers = lax.axis_size("dp")
    per_pair = slot_rows // reader_peers
    feature_width = HEADS * HD
    score_scale = HD ** (-0.5)
    group_rows = slot_rows * lax.axis_size("ctx")
    user_range = jnp.arange(owner_of.shape[0], dtype=jnp.int32)
    owners = jnp.sum(
        jnp.where(user_of[:, None] == user_range[None, :], owner_of[None, :], 0), axis=1
    )
    is_live = user_of >= 0
    owner_hits = (owners[:, None] == jnp.arange(reader_peers, dtype=jnp.int32)[None, :]) & is_live[
        :, None
    ]
    running = jnp.cumsum(owner_hits.astype(jnp.int32), axis=0) - 1
    ranks_mine = jnp.sum(jnp.where(owner_hits, running, 0), axis=1)
    send_slot = jnp.where(is_live, owners * per_pair + ranks_mine, -1)
    slot_range = jnp.arange(slot_rows, dtype=jnp.int32)
    slot_match = send_slot[None, :] == slot_range[:, None]
    filled = jnp.any(slot_match, axis=1)
    source_row = jnp.sum(jnp.where(slot_match, slot_range[None, :], 0), axis=1)
    outgoing = jnp.where(
        filled[:, None], jnp.take(proj_read, source_row, axis=0), jnp.zeros((), jnp.bfloat16)
    )
    outgoing_users = jnp.where(filled, jnp.take(user_of, source_row), -1)
    arrived, arrived_users = (
        lax.all_to_all(outgoing, "dp", split_axis=0, concat_axis=0, tiled=True),
        lax.all_to_all(outgoing_users, "dp", split_axis=0, concat_axis=0, tiled=True),
    )
    own_start = lax.axis_index("ctx") * slot_rows
    own_places = own_start + slot_range
    unit_rows = arrived[:, :feature_width]
    queries = arrived[:, feature_width : 2 * feature_width]
    key_values = arrived[:, 2 * feature_width :]
    query_heads = queries.reshape(slot_rows, HEADS, HD)
    key_heads = key_values[:, :feature_width].reshape(slot_rows, HEADS, HD)
    value_heads = key_values[:, feature_width:].reshape(slot_rows, HEADS, HD)

    def forward_step(total_out, block_part, first_row):
        block_kv, block_users = block_part
        block_size = block_kv.shape[0]
        remote_keys = block_kv[:, :feature_width].reshape(block_size, HEADS, HD)
        remote_values = block_kv[:, feature_width:].reshape(block_size, HEADS, HD)
        scores = (
            jnp.einsum("qhd,khd->hqk", query_heads, remote_keys, preferred_element_type=jnp.float32)
            * score_scale
        )
        visible = visible_pairs(
            arrived_users,
            own_places,
            block_users,
            first_row + jnp.arange(block_size, dtype=jnp.int32),
        )
        weights = jnp.where(visible[None], jax.nn.silu(scores), 0.0).astype(jnp.bfloat16)
        summed = jnp.einsum(
            "hqk,khd->qhd", weights, remote_values, preferred_element_type=jnp.float32
        )
        return total_out + summed.reshape(slot_rows, feature_width)

    zero_rows = jnp.zeros((slot_rows, feature_width), jnp.float32)
    shard_piece = (
        lax.all_gather(key_values, "ctx", axis=0, tiled=True),
        lax.all_gather(arrived_users, "ctx", axis=0, tiled=True),
    )
    block_rows = block_length(shard_piece[0].shape[0], slot_rows)
    forward_result = run_blocks(zero_rows, shard_piece, block_rows, forward_step)
    mean_out = jnp.mean(forward_result, axis=1, keepdims=True)
    centered = forward_result - mean_out
    inv_std = lax.rsqrt(jnp.mean(centered * centered, axis=1, keepdims=True) + epsilon)
    normed = centered * inv_std
    unit_float = unit_rows.astype(jnp.float32)
    layer_out = (normed * norm_gain * unit_float).astype(jnp.bfloat16)
    grad_float = grad_output.astype(jnp.float32)
    unit_grads = (grad_float * norm_gain * normed).astype(jnp.bfloat16)
    grad_normed = grad_float * norm_gain * unit_float
    mean_grad = jnp.mean(grad_normed, axis=1, keepdims=True)
    mean_cross = jnp.mean(grad_normed * normed, axis=1, keepdims=True)
    out_grads = (inv_std * (grad_normed - mean_grad - normed * mean_cross)).astype(jnp.bfloat16)

    def backward_step(carry_here, block_part, first_row):
        block_queries, block_grads, block_users = block_part
        block_size = block_queries.shape[0]
        remote_queries = block_queries.reshape(block_size, HEADS, HD)
        remote_grads = block_grads.reshape(block_size, HEADS, HD)
        scores = (
            jnp.einsum(
                "qhd,khd->hqk", remote_queries, key_heads, preferred_element_type=jnp.float32
            )
            * score_scale
        )
        visible = visible_pairs(
            block_users,
            first_row + jnp.arange(block_size, dtype=jnp.int32),
            arrived_users,
            own_places,
        )[None]
        weights = jnp.where(visible, jax.nn.silu(scores), 0.0).astype(jnp.bfloat16)
        weight_grads = jnp.einsum(
            "qhd,khd->hqk", remote_grads, value_heads, preferred_element_type=jnp.float32
        )
        score_grads = jnp.where(
            visible, weight_grads * silu_slope(scores) * score_scale, 0.0
        ).astype(jnp.bfloat16)
        value_sum = jnp.einsum(
            "hqk,qhd->khd", weights, remote_grads, preferred_element_type=jnp.float32
        ).reshape(slot_rows, feature_width)
        key_sum = jnp.einsum(
            "hqk,qhd->khd", score_grads, remote_queries, preferred_element_type=jnp.float32
        ).reshape(slot_rows, feature_width)
        new_keys = carry_here[0] + key_sum
        new_values = carry_here[1] + value_sum
        window_sum = (
            jnp.einsum("hqk,khd->qhd", score_grads, key_heads, preferred_element_type=jnp.float32)
            .reshape(block_size, feature_width)
            .astype(jnp.bfloat16)
        )
        return (
            new_keys,
            new_values,
            lax.dynamic_update_slice_in_dim(carry_here[2], window_sum, first_row, 0),
        )

    start_carry = (zero_rows, zero_rows, jnp.zeros((group_rows, feature_width), jnp.bfloat16))
    shard_piece = (
        lax.all_gather(queries, "ctx", axis=0, tiled=True),
        lax.all_gather(out_grads, "ctx", axis=0, tiled=True),
        lax.all_gather(arrived_users, "ctx", axis=0, tiled=True),
    )
    block_rows = block_length(shard_piece[0].shape[0], slot_rows)
    key_results = run_blocks(start_carry, shard_piece, block_rows, backward_step)
    key_grads = key_results[0]
    value_grads = key_results[1]
    query_grads = lax.psum_scatter(key_results[2], "ctx", scatter_dimension=0, tiled=True).astype(
        jnp.float32
    )
    grads_owned = jnp.concatenate(
        [
            unit_grads,
            query_grads.astype(jnp.bfloat16),
            key_grads.astype(jnp.bfloat16),
            value_grads.astype(jnp.bfloat16),
        ],
        axis=1,
    )
    returned = lax.all_to_all(grads_owned, "dp", split_axis=0, concat_axis=0, tiled=True)
    back_rows = jnp.take(returned, jnp.maximum(send_slot, 0), axis=0)
    grad_read = jnp.where(is_live[:, None], back_rows, jnp.zeros((), jnp.bfloat16))
    return (layer_out, grad_read)


LIMIT = pltpu.CompilerParams(vmem_limit_bytes=16 * 2**20)


def device_of(owner, head):
    return (owner & ~1) | (head & 1), ((owner & 1) << 1) | (head >> 1)


def turned(index):
    return ((index & 1) << 1) | (index >> 1)


def vmem(count):
    return [pl.BlockSpec(memory_space=pltpu.VMEM)] * count


def hbm(count):
    return [pl.BlockSpec(memory_space=pltpu.HBM)] * count


def dot(left, right, left_dim, right_dim):
    return lax.dot_general(
        left, right, (((left_dim,), (right_dim,)), ((), ())), preferred_element_type=jnp.float32
    )


def owners_of(users, owner_ref):
    owners = jnp.zeros_like(users)
    for user in range(owner_ref.shape[0]):
        owners = jnp.where(users == user, owner_ref[user], owners)
    return owners


def lower_ones(size):
    earlier = lax.broadcasted_iota(jnp.int32, (size, size), 0)
    later = lax.broadcasted_iota(jnp.int32, (size, size), 1)
    return (earlier <= later).astype(jnp.bfloat16)


def my_place():
    my_dp, my_ctx = lax.axis_index("dp"), lax.axis_index("ctx")
    return ((my_ctx & 1) << 1) | (my_dp & 1), (my_dp & ~1) | (my_ctx >> 1), my_dp, my_ctx


def slot_kernel(
    owner_hbm,
    user_hbm,
    proj_hbm,
    send_hbm,
    slot_hbm,
    owner_ref,
    user_ref,
    slot_ref,
    proj_ref,
    send_ref,
    load_sems,
    store_sems,
    *,
    per_pair,
):
    slots = user_ref.shape[1]
    readers = slots // per_pair
    width = HEADS * HD
    loads = [
        pltpu.make_async_copy(source, target, load_sems.at[index])
        for index, (source, target) in enumerate(
            ((user_hbm, user_ref), (owner_hbm, owner_ref), (proj_hbm, proj_ref))
        )
    ]
    for copy in loads:
        copy.start()
    my_dp = lax.axis_index("dp")
    source = lax.broadcasted_iota(jnp.int32, (slots, slots), 0)
    target = lax.broadcasted_iota(jnp.int32, (slots, slots), 1)
    owner_range = lax.broadcasted_iota(jnp.int32, (readers, slots), 0)
    by_owner = lax.div(lax.broadcasted_iota(jnp.int32, (readers, slots), 1), per_pair)
    to_lane = (lax.div(target, per_pair) == my_dp) & (
        lax.rem(target, per_pair) == lax.rem(source, per_pair)
    )
    loads[0].wait()
    loads[1].wait()
    users = user_ref[...]
    owners = owners_of(users, owner_ref)
    is_live = users >= 0
    hits = ((owner_range == owners) & is_live).astype(jnp.float32)
    running = dot(hits.astype(jnp.bfloat16), lower_ones(slots), 1, 0)
    ranks = jnp.sum(hits * running, axis=0, keepdims=True).astype(jnp.int32) - 1
    slot = jnp.where(is_live, owners * per_pair + ranks, -1)
    slot_ref[...] = slot
    stores = [pltpu.make_async_copy(slot_ref, slot_hbm, store_sems.at[HEADS])]
    stores[0].start()
    placed = (source == slot).astype(jnp.bfloat16)
    tagged = jnp.broadcast_to((users + 1).astype(jnp.float32), (readers, slots))
    tagged = dot(tagged.astype(jnp.bfloat16), placed, 1, 1)
    tagged = jnp.where(by_owner == owner_range, tagged, 0.0).astype(jnp.bfloat16)
    tagged = dot(tagged, to_lane.astype(jnp.bfloat16), 1, 0).astype(jnp.bfloat16)
    extra = send_ref.shape[1] - 4 * per_pair
    for owner in range(readers):
        for head in range(HEADS):
            dp_index, ctx_index = device_of(owner, head)
            send_ref[ctx_index * readers + dp_index, 4 * per_pair :, :] = jnp.broadcast_to(
                tagged[owner : owner + 1], (extra, slots)
            )
    loads[2].wait()
    for half in range(2):
        for part in range(4):
            start = part * width + half * 2 * HD
            rows = dot(placed, proj_ref[:, start : start + 2 * HD], 1, 0).astype(jnp.bfloat16)
            for owner in range(readers):
                for side in range(2):
                    dp_index, ctx_index = device_of(owner, 2 * half + side)
                    chunk = ctx_index * readers + dp_index
                    send_ref[chunk, part * per_pair : (part + 1) * per_pair, :] = rows[
                        owner * per_pair : (owner + 1) * per_pair, side * HD : (side + 1) * HD
                    ]
        for ctx_index in (half, 2 + half):
            span = pl.ds(ctx_index * readers, readers)
            stores.append(
                pltpu.make_async_copy(
                    send_ref.at[span], send_hbm.at[span], store_sems.at[ctx_index]
                )
            )
            stores[-1].start()
    for copy in stores:
        copy.wait()


def columns_kernel(slot_ref, grad_ref, *refs):
    piece_refs, back_ref = refs[:HEADS], refs[HEADS]
    slots = slot_ref.shape[1]
    slot = jnp.broadcast_to(slot_ref[...].astype(jnp.float32), (slots, slots)).T
    lane = lax.broadcasted_iota(jnp.int32, (slots, slots), 1).astype(jnp.float32)
    back_ref[...] = (slot == lane).astype(jnp.bfloat16)
    first = turned(lax.axis_index("ctx"))
    for step, piece_ref in enumerate(piece_refs):
        start = pl.multiple_of((first ^ step) * HD, HD)
        piece_ref[...] = grad_ref[:, pl.ds(start, HD)]


def group_kernel(*refs):
    piece_refs, grads_ref = refs[:HEADS], refs[HEADS]
    head = my_place()[0]
    for step, piece_ref in enumerate(piece_refs):
        slots = piece_ref.shape[0]
        start = pl.multiple_of(turned(head ^ step) * slots, slots)
        grads_ref[pl.ds(start, slots), :] = piece_ref[...]


def part_rows(rows_ref, part, first, last):
    per_pair = HD // (rows_ref.shape[0] // HEADS)
    readers = rows_ref.shape[0] // HEADS
    rows = rows_ref[first * readers : last * readers, part * per_pair : (part + 1) * per_pair, :]
    return rows.reshape((last - first) * readers * per_pair, HD)


def window_users(rows_ref, window):
    readers = rows_ref.shape[0] // HEADS
    per_pair = HD // readers
    tags = rows_ref[window * readers : (window + 1) * readers, 4 * per_pair :, :]
    return jnp.sum(tags.astype(jnp.float32), axis=0)[:1]


def visible_block(users, query_window):
    size = users[0].shape[1]
    query_users = jnp.broadcast_to(users[query_window], (size, size)).T
    blocks = []
    for window in range(query_window + 1):
        block = (query_users == users[window]) & (query_users > 0.0)
        if window == query_window:
            rows = lax.broadcasted_iota(jnp.int32, (size, size), 0)
            columns = lax.broadcasted_iota(jnp.int32, (size, size), 1)
            block = block & (columns <= rows)
        blocks.append(block)
    return jnp.concatenate(blocks, axis=1)


def forward_kernel(rows_ref, grads_ref, gain_ref, attended_ref, stats_ref):
    size = HD
    scale = HD ** (-0.5)
    lane = lax.broadcasted_iota(jnp.int32, (size, HD), 1)
    users = [window_users(rows_ref, window) for window in range(HEADS)]
    for window in range(HEADS):
        here = slice(window * size, (window + 1) * size)
        queries = part_rows(rows_ref, 1, window, window + 1)
        scores = dot(queries, part_rows(rows_ref, 2, 0, window + 1), 1, 1) * scale
        visible = visible_block(users, window)
        weights = jnp.where(visible, scores * jax.nn.sigmoid(scores), 0.0).astype(jnp.bfloat16)
        attended = dot(weights, part_rows(rows_ref, 3, 0, window + 1), 1, 0)
        attended_ref[here] = attended
        grad_normed = (
            grads_ref[here].astype(jnp.float32)
            * gain_ref[...]
            * part_rows(rows_ref, 0, window, window + 1).astype(jnp.float32)
        )
        mean = jnp.mean(attended, axis=1, keepdims=True)
        centered = attended - mean
        spread = jnp.sum(centered * centered, axis=1, keepdims=True)
        grad_sum = jnp.sum(grad_normed, axis=1, keepdims=True)
        cross = jnp.sum(grad_normed * centered, axis=1, keepdims=True)
        packed = jnp.where(
            lane == 0, mean, jnp.where(lane == 1, spread, jnp.where(lane == 2, grad_sum, cross))
        )
        stats_ref[:, here] = packed.T[:8]


def slope_kernel(rows_ref, slopes_ref, turned_slopes_ref, turned_weights_ref):
    size = HD
    scale = HD ** (-0.5)
    users = [window_users(rows_ref, window) for window in range(HEADS)]
    for window in range(HEADS):
        here = slice(window * size, (window + 1) * size)
        upto = slice(0, (window + 1) * size)
        queries = part_rows(rows_ref, 1, window, window + 1)
        scores = dot(queries, part_rows(rows_ref, 2, 0, window + 1), 1, 1) * scale
        sigmoid = jax.nn.sigmoid(scores)
        slopes = sigmoid * (1.0 + scores * (1.0 - sigmoid)) * scale
        visible = visible_block(users, window)
        slopes = jnp.where(visible, slopes, 0.0)
        weights = jnp.where(visible, scores * sigmoid, 0.0)
        slopes_ref[here, upto] = slopes
        for key_window in range(window + 1):
            there = slice(key_window * size, (key_window + 1) * size)
            turned_slopes_ref[there, here] = slopes[:, there].T
            turned_weights_ref[there, here] = weights[:, there].T.astype(jnp.bfloat16)


def backward_kernel(
    rows_ref,
    grads_ref,
    gain_ref,
    attended_ref,
    slopes_ref,
    turned_slopes_ref,
    turned_weights_ref,
    *refs,
):
    stats_refs = refs[:HEADS]
    out_hbm = refs[HEADS]
    layer_refs = refs[HEADS + 1 : 2 * HEADS + 1]
    layer_all, out_ref, out_grads, store_sems = refs[2 * HEADS + 1 :]
    head = my_place()[0]
    size = HD
    width = float(HEADS * HD)
    stats = [stat_ref[...] for stat_ref in stats_refs]
    mean = sum(stat[0:1] for stat in stats) * (1.0 / HEADS)
    spread = sum(stat[1:2] + HD * (stat[0:1] - mean) * (stat[0:1] - mean) for stat in stats)
    inv_std = lax.rsqrt(spread / width + epsilon)
    mean_grad = sum(stat[2:3] for stat in stats) / width
    cross = sum(stat[3:4] + (stat[0:1] - mean) * stat[2:3] for stat in stats)
    mean_cross = cross * inv_std / width
    row = lax.broadcasted_iota(jnp.int32, (size, size), 0)
    for window in range(HEADS):
        here = slice(window * size, (window + 1) * size)
        packed = jnp.where(
            row == 0,
            mean[:, here],
            jnp.where(
                row == 1,
                inv_std[:, here],
                jnp.where(row == 2, mean_grad[:, here], mean_cross[:, here]),
            ),
        ).T
        unit = part_rows(rows_ref, 0, window, window + 1).astype(jnp.float32)
        grad_gain = grads_ref[here].astype(jnp.float32) * gain_ref[...]
        normed = (attended_ref[here] - packed[:, 0:1]) * packed[:, 1:2]
        layer_all[here] = (normed * gain_ref[...] * unit).astype(jnp.bfloat16)
        out_ref[here, :HD] = (grad_gain * normed).astype(jnp.bfloat16)
        out_grads[here] = (
            packed[:, 1:2] * (grad_gain * unit - packed[:, 2:3] - normed * packed[:, 3:4])
        ).astype(jnp.bfloat16)
    stores = []
    for window in range(HEADS):
        here = slice(window * size, (window + 1) * size)
        upto = slice(0, (window + 1) * size)
        after = slice(window * size, HEADS * size)
        score_grads = (
            dot(out_grads[here], part_rows(rows_ref, 3, 0, window + 1), 1, 1)
            * slopes_ref[here, upto]
        ).astype(jnp.bfloat16)
        out_ref[here, HD : 2 * HD] = dot(
            score_grads, part_rows(rows_ref, 2, 0, window + 1), 1, 0
        ).astype(jnp.bfloat16)
        turned_grads = (
            dot(part_rows(rows_ref, 3, window, window + 1), out_grads[after], 1, 1)
            * turned_slopes_ref[here, after]
        ).astype(jnp.bfloat16)
        out_ref[here, 2 * HD : 3 * HD] = dot(
            turned_grads, part_rows(rows_ref, 1, window, HEADS), 1, 0
        ).astype(jnp.bfloat16)
        out_ref[here, 3 * HD :] = dot(
            turned_weights_ref[here, after], out_grads[after], 1, 0
        ).astype(jnp.bfloat16)
        span = pl.ds(window * size, size)
        stores.append(
            pltpu.make_async_copy(out_ref.at[span], out_hbm.at[span], store_sems.at[window])
        )
        stores[-1].start()
    for step, layer_ref in enumerate(layer_refs):
        start = pl.multiple_of(turned(head ^ step) * size, size)
        layer_ref[...] = layer_all[pl.ds(start, size), :]
    for copy in stores:
        copy.wait()


def unslot_kernel(back_ref, returned_ref, *refs, per_pair):
    piece_refs = refs[:HEADS]
    layer_hbm, grad_hbm, layer_ref, grad_ref, store_sems = refs[HEADS:]
    slots = back_ref.shape[0]
    readers = slots // per_pair
    width = HEADS * HD
    first = turned(lax.axis_index("ctx"))
    for step, piece_ref in enumerate(piece_refs):
        start = pl.multiple_of((first ^ step) * HD, HD)
        layer_ref[:, pl.ds(start, HD)] = piece_ref[...]
    stores = [pltpu.make_async_copy(layer_ref, layer_hbm, store_sems.at[2])]
    stores[0].start()
    heads = []
    for head in range(HEADS):
        chunks = []
        for owner in range(readers):
            dp_index, ctx_index = device_of(owner, head)
            start = (ctx_index * readers + dp_index) * per_pair
            chunks.append(returned_ref[start : start + per_pair])
        heads.append(jnp.concatenate(chunks, axis=0))
    half = slots // 2
    for side in range(2):
        span = pl.ds(side * half, half)
        here = slice(side * half, (side + 1) * half)
        for head in range(HEADS):
            rows = dot(back_ref[here], heads[head], 1, 0).astype(jnp.bfloat16)
            for part in range(4):
                start = part * width + head * HD
                grad_ref[here, start : start + HD] = rows[:, part * HD : (part + 1) * HD]
        stores.append(
            pltpu.make_async_copy(grad_ref.at[span], grad_hbm.at[span], store_sems.at[side])
        )
        stores[-1].start()
    for copy in stores:
        copy.wait()


def send(value, target, back=False):
    width = lax.axis_size("ctx")
    pairs = []
    for dp_index in range(lax.axis_size("dp")):
        for ctx_index in range(width):
            to_dp, to_ctx = target(dp_index, ctx_index)
            pair = (dp_index * width + ctx_index, to_dp * width + to_ctx)
            pairs.append(pair[::-1] if back else pair)
    return lax.ppermute(value, ("dp", "ctx"), pairs)


def swap(value, dp_bits, ctx_bits):
    return send(value, lambda dp_index, ctx_index: (dp_index ^ dp_bits, ctx_index ^ ctx_bits))


def regroup(pieces, back=False):
    moved = []
    for step, piece in enumerate(pieces):

        def target(dp_index, ctx_index, step=step):
            return device_of(dp_index, turned(ctx_index) ^ step)

        moved.append(send(piece, target, back))
    return moved


def by_heads(proj_read, norm_gain, owner_of, user_of, grad_output):
    slots = proj_read.shape[0]
    readers = lax.axis_size("dp")
    per_pair = slots // readers
    group_rows = slots * HEADS
    width = 4 * HD
    gain = lax.dynamic_slice_in_dim(norm_gain, my_place()[0] * HD, HD, 0).reshape(1, HD)
    piece_shape = jax.ShapeDtypeStruct((slots, HD), jnp.bfloat16)
    chunk_shape = (HEADS * readers, 4 * per_pair + 8, HD)
    outgoing, slot = pl.pallas_call(
        functools.partial(slot_kernel, per_pair=per_pair),
        out_shape=(
            jax.ShapeDtypeStruct(chunk_shape, jnp.bfloat16),
            jax.ShapeDtypeStruct((1, slots), jnp.int32),
        ),
        in_specs=hbm(3),
        out_specs=tuple(hbm(2)),
        scratch_shapes=[
            pltpu.SMEM(owner_of.shape, jnp.int32),
            pltpu.VMEM((1, slots), jnp.int32),
            pltpu.VMEM((1, slots), jnp.int32),
            pltpu.VMEM(proj_read.shape, jnp.bfloat16),
            pltpu.VMEM(chunk_shape, jnp.bfloat16),
            pltpu.SemaphoreType.DMA((3,)),
            pltpu.SemaphoreType.DMA((HEADS + 1,)),
        ],
        name="slot_rows",
    )(owner_of, user_of.reshape(1, slots), proj_read)
    rows = lax.all_to_all(outgoing, ("ctx", "dp"), split_axis=0, concat_axis=0, tiled=True)
    *pieces, back = pl.pallas_call(
        columns_kernel,
        out_shape=(piece_shape,) * HEADS + (jax.ShapeDtypeStruct((slots, slots), jnp.bfloat16),),
        in_specs=vmem(2),
        out_specs=tuple(vmem(HEADS + 1)),
        compiler_params=LIMIT,
        name="cut_columns",
    )(slot, grad_output)
    grads = pl.pallas_call(
        group_kernel,
        out_shape=jax.ShapeDtypeStruct((group_rows, HD), jnp.bfloat16),
        in_specs=vmem(HEADS),
        out_specs=vmem(1)[0],
        compiler_params=LIMIT,
        name="lay_group",
    )(*regroup(pieces))
    attended, stats = pl.pallas_call(
        forward_kernel,
        out_shape=(
            jax.ShapeDtypeStruct((group_rows, HD), jnp.float32),
            jax.ShapeDtypeStruct((8, group_rows), jnp.float32),
        ),
        in_specs=vmem(3),
        out_specs=tuple(vmem(2)),
        compiler_params=LIMIT,
        name="forward",
    )(rows, grads, gain)
    late_rows, stats = lax.optimization_barrier((rows, stats))
    slopes = pl.pallas_call(
        slope_kernel,
        out_shape=(
            jax.ShapeDtypeStruct((group_rows, group_rows), jnp.float32),
            jax.ShapeDtypeStruct((group_rows, group_rows), jnp.float32),
            jax.ShapeDtypeStruct((group_rows, group_rows), jnp.bfloat16),
        ),
        in_specs=vmem(1),
        out_specs=tuple(vmem(3)),
        compiler_params=LIMIT,
        name="slopes",
    )(late_rows)
    all_stats = [stats, swap(stats, 1, 0), swap(stats, 0, 1), swap(stats, 1, 1)]
    results = pl.pallas_call(
        backward_kernel,
        out_shape=(jax.ShapeDtypeStruct((group_rows, width), jnp.bfloat16),)
        + (piece_shape,) * HEADS,
        in_specs=vmem(7 + HEADS),
        out_specs=tuple(hbm(1) + vmem(HEADS)),
        scratch_shapes=[
            pltpu.VMEM((group_rows, HD), jnp.bfloat16),
            pltpu.VMEM((group_rows, width), jnp.bfloat16),
            pltpu.VMEM((group_rows, HD), jnp.bfloat16),
            pltpu.SemaphoreType.DMA((HEADS,)),
        ],
        compiler_params=LIMIT,
        name="backward",
    )(rows, grads, gain, attended, *slopes, *all_stats)
    returned = lax.all_to_all(results[0], ("ctx", "dp"), split_axis=0, concat_axis=0, tiled=True)
    layer_shape, grad_shape = (slots, HEADS * HD), (slots, 4 * HEADS * HD)
    return pl.pallas_call(
        functools.partial(unslot_kernel, per_pair=per_pair),
        out_shape=(
            jax.ShapeDtypeStruct(layer_shape, jnp.bfloat16),
            jax.ShapeDtypeStruct(grad_shape, jnp.bfloat16),
        ),
        in_specs=vmem(2 + HEADS),
        out_specs=tuple(hbm(2)),
        scratch_shapes=[
            pltpu.VMEM(layer_shape, jnp.bfloat16),
            pltpu.VMEM(grad_shape, jnp.bfloat16),
            pltpu.SemaphoreType.DMA((3,)),
        ],
        compiler_params=LIMIT,
        name="unslot_rows",
    )(back, returned, *regroup(results[1:], back=True))


def solution(mesh):
    in_specs = (P(("dp", "ctx"), None), P(), P(), P(("dp", "ctx")), P(("dp", "ctx"), None))
    out_specs = (P(("dp", "ctx"), None), P(("dp", "ctx"), None))
    local = by_heads if mesh.shape["ctx"] == HEADS else windowed
    return jax.shard_map(local, mesh=mesh, in_specs=in_specs, out_specs=out_specs, check_vma=False)
```

```python
import functools

import jax
import jax.numpy as jnp
from jax import lax
from jax.experimental import pallas as pl
from jax.experimental.pallas import tpu as pltpu
from jax.sharding import PartitionSpec as P

HEADS = 4
HD = 128


epsilon = 1e-05


def block_length(total_rows, shard_rows):
    shard_total = total_rows // shard_rows
    best_factor = 1
    for factor in range(1, shard_total + 1):
        if shard_total % factor == 0 and factor * shard_rows <= 1024:
            best_factor = factor
    return best_factor * shard_rows


def silu_slope(scores):
    sigmoid_part = jax.nn.sigmoid(scores)
    return sigmoid_part * (1.0 + scores * (1.0 - sigmoid_part))


def visible_pairs(query_users, query_places, key_users, key_places):
    same_user = (query_users[:, None] == key_users[None, :]) & (query_users[:, None] >= 0)
    return same_user & (key_places[None, :] <= query_places[:, None])


def run_blocks(carry_now, shard_piece, block_rows, step_fn):
    total_rows = shard_piece[0].shape[0]

    def one_block(block_index, carry_here):
        offset = block_index * block_rows
        block_part = tuple(
            (
                lax.dynamic_slice_in_dim(array_item, offset, block_rows, 0)
                for array_item in shard_piece
            )
        )
        return step_fn(carry_here, block_part, offset)

    return lax.fori_loop(0, total_rows // block_rows, one_block, carry_now)


def windowed(proj_read, norm_gain, owner_of, user_of, grad_output):
    slot_rows = proj_read.shape[0]
    reader_peers = lax.axis_size("dp")
    per_pair = slot_rows // reader_peers
    feature_width = HEADS * HD
    score_scale = HD ** (-0.5)
    group_rows = slot_rows * lax.axis_size("ctx")
    user_range = jnp.arange(owner_of.shape[0], dtype=jnp.int32)
    owners = jnp.sum(
        jnp.where(user_of[:, None] == user_range[None, :], owner_of[None, :], 0), axis=1
    )
    is_live = user_of >= 0
    owner_hits = (owners[:, None] == jnp.arange(reader_peers, dtype=jnp.int32)[None, :]) & is_live[
        :, None
    ]
    running = jnp.cumsum(owner_hits.astype(jnp.int32), axis=0) - 1
    ranks_mine = jnp.sum(jnp.where(owner_hits, running, 0), axis=1)
    send_slot = jnp.where(is_live, owners * per_pair + ranks_mine, -1)
    slot_range = jnp.arange(slot_rows, dtype=jnp.int32)
    slot_match = send_slot[None, :] == slot_range[:, None]
    filled = jnp.any(slot_match, axis=1)
    source_row = jnp.sum(jnp.where(slot_match, slot_range[None, :], 0), axis=1)
    outgoing = jnp.where(
        filled[:, None], jnp.take(proj_read, source_row, axis=0), jnp.zeros((), jnp.bfloat16)
    )
    outgoing_users = jnp.where(filled, jnp.take(user_of, source_row), -1)
    arrived, arrived_users = (
        lax.all_to_all(outgoing, "dp", split_axis=0, concat_axis=0, tiled=True),
        lax.all_to_all(outgoing_users, "dp", split_axis=0, concat_axis=0, tiled=True),
    )
    own_start = lax.axis_index("ctx") * slot_rows
    own_places = own_start + slot_range
    unit_rows = arrived[:, :feature_width]
    queries = arrived[:, feature_width : 2 * feature_width]
    key_values = arrived[:, 2 * feature_width :]
    query_heads = queries.reshape(slot_rows, HEADS, HD)
    key_heads = key_values[:, :feature_width].reshape(slot_rows, HEADS, HD)
    value_heads = key_values[:, feature_width:].reshape(slot_rows, HEADS, HD)

    def forward_step(total_out, block_part, first_row):
        block_kv, block_users = block_part
        block_size = block_kv.shape[0]
        remote_keys = block_kv[:, :feature_width].reshape(block_size, HEADS, HD)
        remote_values = block_kv[:, feature_width:].reshape(block_size, HEADS, HD)
        scores = (
            jnp.einsum("qhd,khd->hqk", query_heads, remote_keys, preferred_element_type=jnp.float32)
            * score_scale
        )
        visible = visible_pairs(
            arrived_users,
            own_places,
            block_users,
            first_row + jnp.arange(block_size, dtype=jnp.int32),
        )
        weights = jnp.where(visible[None], jax.nn.silu(scores), 0.0).astype(jnp.bfloat16)
        summed = jnp.einsum(
            "hqk,khd->qhd", weights, remote_values, preferred_element_type=jnp.float32
        )
        return total_out + summed.reshape(slot_rows, feature_width)

    zero_rows = jnp.zeros((slot_rows, feature_width), jnp.float32)
    shard_piece = (
        lax.all_gather(key_values, "ctx", axis=0, tiled=True),
        lax.all_gather(arrived_users, "ctx", axis=0, tiled=True),
    )
    block_rows = block_length(shard_piece[0].shape[0], slot_rows)
    forward_result = run_blocks(zero_rows, shard_piece, block_rows, forward_step)
    mean_out = jnp.mean(forward_result, axis=1, keepdims=True)
    centered = forward_result - mean_out
    inv_std = lax.rsqrt(jnp.mean(centered * centered, axis=1, keepdims=True) + epsilon)
    normed = centered * inv_std
    unit_float = unit_rows.astype(jnp.float32)
    layer_out = (normed * norm_gain * unit_float).astype(jnp.bfloat16)
    grad_float = grad_output.astype(jnp.float32)
    unit_grads = (grad_float * norm_gain * normed).astype(jnp.bfloat16)
    grad_normed = grad_float * norm_gain * unit_float
    mean_grad = jnp.mean(grad_normed, axis=1, keepdims=True)
    mean_cross = jnp.mean(grad_normed * normed, axis=1, keepdims=True)
    out_grads = (inv_std * (grad_normed - mean_grad - normed * mean_cross)).astype(jnp.bfloat16)

    def backward_step(carry_here, block_part, first_row):
        block_queries, block_grads, block_users = block_part
        block_size = block_queries.shape[0]
        remote_queries = block_queries.reshape(block_size, HEADS, HD)
        remote_grads = block_grads.reshape(block_size, HEADS, HD)
        scores = (
            jnp.einsum(
                "qhd,khd->hqk", remote_queries, key_heads, preferred_element_type=jnp.float32
            )
            * score_scale
        )
        visible = visible_pairs(
            block_users,
            first_row + jnp.arange(block_size, dtype=jnp.int32),
            arrived_users,
            own_places,
        )[None]
        weights = jnp.where(visible, jax.nn.silu(scores), 0.0).astype(jnp.bfloat16)
        weight_grads = jnp.einsum(
            "qhd,khd->hqk", remote_grads, value_heads, preferred_element_type=jnp.float32
        )
        score_grads = jnp.where(
            visible, weight_grads * silu_slope(scores) * score_scale, 0.0
        ).astype(jnp.bfloat16)
        value_sum = jnp.einsum(
            "hqk,qhd->khd", weights, remote_grads, preferred_element_type=jnp.float32
        ).reshape(slot_rows, feature_width)
        key_sum = jnp.einsum(
            "hqk,qhd->khd", score_grads, remote_queries, preferred_element_type=jnp.float32
        ).reshape(slot_rows, feature_width)
        new_keys = carry_here[0] + key_sum
        new_values = carry_here[1] + value_sum
        window_sum = (
            jnp.einsum("hqk,khd->qhd", score_grads, key_heads, preferred_element_type=jnp.float32)
            .reshape(block_size, feature_width)
            .astype(jnp.bfloat16)
        )
        return (
            new_keys,
            new_values,
            lax.dynamic_update_slice_in_dim(carry_here[2], window_sum, first_row, 0),
        )

    start_carry = (zero_rows, zero_rows, jnp.zeros((group_rows, feature_width), jnp.bfloat16))
    shard_piece = (
        lax.all_gather(queries, "ctx", axis=0, tiled=True),
        lax.all_gather(out_grads, "ctx", axis=0, tiled=True),
        lax.all_gather(arrived_users, "ctx", axis=0, tiled=True),
    )
    block_rows = block_length(shard_piece[0].shape[0], slot_rows)
    key_results = run_blocks(start_carry, shard_piece, block_rows, backward_step)
    key_grads = key_results[0]
    value_grads = key_results[1]
    query_grads = lax.psum_scatter(key_results[2], "ctx", scatter_dimension=0, tiled=True).astype(
        jnp.float32
    )
    grads_owned = jnp.concatenate(
        [
            unit_grads,
            query_grads.astype(jnp.bfloat16),
            key_grads.astype(jnp.bfloat16),
            value_grads.astype(jnp.bfloat16),
        ],
        axis=1,
    )
    returned = lax.all_to_all(grads_owned, "dp", split_axis=0, concat_axis=0, tiled=True)
    back_rows = jnp.take(returned, jnp.maximum(send_slot, 0), axis=0)
    grad_read = jnp.where(is_live[:, None], back_rows, jnp.zeros((), jnp.bfloat16))
    return (layer_out, grad_read)


STEP = 2
LIMIT = pltpu.CompilerParams(vmem_limit_bytes=16 * 2**20)


def device_of(owner, head):
    return (owner & ~1) | (head & 1), ((owner & 1) << 1) | (head >> 1)


def chunk_of(dp_index, ctx_index, readers):
    return ctx_index * readers + (dp_index & 1) * (readers // 2) + (dp_index >> 1)


def turned(index):
    return ((index & 1) << 1) | (index >> 1)


def vmem(count):
    return [pl.BlockSpec(memory_space=pltpu.VMEM)] * count


def hbm(count):
    return [pl.BlockSpec(memory_space=pltpu.HBM)] * count


def dot(left, right, left_dim, right_dim):
    return lax.dot_general(
        left, right, (((left_dim,), (right_dim,)), ((), ())), preferred_element_type=jnp.float32
    )


def owners_of(users, owner_ref):
    owners = jnp.zeros_like(users)
    for user in range(owner_ref.shape[0]):
        owners = jnp.where(users == user, owner_ref[user], owners)
    return owners


def lower_ones(size):
    earlier = lax.broadcasted_iota(jnp.int32, (size, size), 0)
    later = lax.broadcasted_iota(jnp.int32, (size, size), 1)
    return (earlier <= later).astype(jnp.bfloat16)


def my_place():
    my_dp, my_ctx = lax.axis_index("dp"), lax.axis_index("ctx")
    return ((my_ctx & 1) << 1) | (my_dp & 1), (my_dp & ~1) | (my_ctx >> 1), my_dp, my_ctx


def slot_kernel(
    owner_hbm,
    user_hbm,
    proj_hbm,
    send_hbm,
    slot_hbm,
    owner_ref,
    user_ref,
    slot_ref,
    proj_ref,
    send_ref,
    load_sems,
    store_sems,
    *,
    per_pair,
):
    slots = user_ref.shape[1]
    readers = slots // per_pair
    width = HEADS * HD
    loads = [
        pltpu.make_async_copy(source, target, load_sems.at[index])
        for index, (source, target) in enumerate(
            ((user_hbm, user_ref), (owner_hbm, owner_ref), (proj_hbm, proj_ref))
        )
    ]
    for copy in loads:
        copy.start()
    my_dp = lax.axis_index("dp")
    source = lax.broadcasted_iota(jnp.int32, (slots, slots), 0)
    target = lax.broadcasted_iota(jnp.int32, (slots, slots), 1)
    owner_range = lax.broadcasted_iota(jnp.int32, (readers, slots), 0)
    by_owner = lax.div(lax.broadcasted_iota(jnp.int32, (readers, slots), 1), per_pair)
    to_lane = (lax.div(target, per_pair) == my_dp) & (
        lax.rem(target, per_pair) == lax.rem(source, per_pair)
    )
    loads[0].wait()
    loads[1].wait()
    users = user_ref[...]
    owners = owners_of(users, owner_ref)
    is_live = users >= 0
    hits = ((owner_range == owners) & is_live).astype(jnp.float32)
    running = dot(hits.astype(jnp.bfloat16), lower_ones(slots), 1, 0)
    ranks = jnp.sum(hits * running, axis=0, keepdims=True).astype(jnp.int32) - 1
    slot = jnp.where(is_live, owners * per_pair + ranks, -1)
    slot_ref[...] = slot
    stores = [pltpu.make_async_copy(slot_ref, slot_hbm, store_sems.at[HEADS])]
    stores[0].start()
    placed = (source == slot).astype(jnp.bfloat16)
    tagged = jnp.broadcast_to((users + 1).astype(jnp.float32), (readers, slots))
    tagged = dot(tagged.astype(jnp.bfloat16), placed, 1, 1)
    tagged = jnp.where(by_owner == owner_range, tagged, 0.0).astype(jnp.bfloat16)
    tagged = dot(tagged, to_lane.astype(jnp.bfloat16), 1, 0).astype(jnp.bfloat16)
    extra = send_ref.shape[1] - 4 * per_pair
    for owner in range(readers):
        for head in range(HEADS):
            dp_index, ctx_index = device_of(owner, head)
            chunk = chunk_of(dp_index, ctx_index, readers)
            send_ref[chunk, 4 * per_pair :, :] = jnp.broadcast_to(
                tagged[owner : owner + 1], (extra, slots)
            )
    loads[2].wait()
    for half in range(2):
        for part in range(4):
            start = part * width + half * 2 * HD
            rows = dot(placed, proj_ref[:, start : start + 2 * HD], 1, 0).astype(jnp.bfloat16)
            for owner in range(readers):
                for side in range(2):
                    dp_index, ctx_index = device_of(owner, 2 * half + side)
                    chunk = chunk_of(dp_index, ctx_index, readers)
                    send_ref[chunk, part * per_pair : (part + 1) * per_pair, :] = rows[
                        owner * per_pair : (owner + 1) * per_pair, side * HD : (side + 1) * HD
                    ]
        for ctx_index in (half, 2 + half):
            span = pl.ds(ctx_index * readers, readers)
            stores.append(
                pltpu.make_async_copy(
                    send_ref.at[span], send_hbm.at[span], store_sems.at[ctx_index]
                )
            )
            stores[-1].start()
    for copy in stores:
        copy.wait()


def columns_kernel(slot_ref, grad_ref, *refs):
    piece_refs, back_ref = refs[:HEADS], refs[HEADS]
    slots = slot_ref.shape[1]
    slot = jnp.broadcast_to(slot_ref[...].astype(jnp.float32), (slots, slots)).T
    lane = lax.broadcasted_iota(jnp.int32, (slots, slots), 1).astype(jnp.float32)
    back_ref[...] = (slot == lane).astype(jnp.bfloat16)
    first = turned(lax.axis_index("ctx"))
    for step, piece_ref in enumerate(piece_refs):
        start = pl.multiple_of((first ^ step) * HD, HD)
        piece_ref[...] = grad_ref[:, pl.ds(start, HD)]


def group_kernel(*refs):
    piece_refs, grads_ref = refs[:HEADS], refs[HEADS]
    head = my_place()[0]
    for step, piece_ref in enumerate(piece_refs):
        slots = piece_ref.shape[0]
        start = pl.multiple_of(turned(head ^ step) * slots, slots)
        grads_ref[pl.ds(start, slots), :] = piece_ref[...]


def part_rows(rows_ref, part, first, last):
    readers = rows_ref.shape[0] // HEADS
    per_pair = HD // readers
    span = slice(part * per_pair, (part + 1) * per_pair)
    rows = [
        rows_ref[chunk_of(reader, window, readers), span, :]
        for window in range(first, last)
        for reader in range(readers)
    ]
    return jnp.concatenate(rows, axis=0)


def put_rows(out_ref, part, first, last, rows, readers):
    per_pair = HD // readers
    for window in range(first, last):
        for reader in range(readers):
            source = ((window - first) * readers + reader) * per_pair
            target = chunk_of(reader, window, readers) * per_pair
            out_ref[target : target + per_pair, part * HD : (part + 1) * HD] = rows[
                source : source + per_pair
            ].astype(jnp.bfloat16)


def window_users(rows_ref, window):
    readers = rows_ref.shape[0] // HEADS
    per_pair = HD // readers
    tags = rows_ref[window * readers : (window + 1) * readers, 4 * per_pair :, :]
    return jnp.sum(tags.astype(jnp.float32), axis=0)[:1]


def visible_block(users, first, last):
    size = HD
    query_users = [jnp.broadcast_to(users[window], (size, size)).T for window in range(first, last)]
    query_users = jnp.concatenate(query_users, axis=0)
    rows = lax.broadcasted_iota(jnp.int32, query_users.shape, 0)
    columns = lax.broadcasted_iota(jnp.int32, query_users.shape, 1)
    blocks = []
    for window in range(last):
        block = (query_users == users[window]) & (query_users > 0.0)
        if window >= first:
            block = block & (columns + (window - first) * size <= rows)
        blocks.append(block)
    return jnp.concatenate(blocks, axis=1)


def forward_kernel(rows_ref, grads_ref, gain_ref, attended_ref, stats_ref):
    size = HD
    scale = HD ** (-0.5)
    users = [window_users(rows_ref, window) for window in range(HEADS)]
    for first in range(0, HEADS, STEP):
        last = first + STEP
        queries = part_rows(rows_ref, 1, first, last)
        scores = dot(queries, part_rows(rows_ref, 2, 0, last), 1, 1) * scale
        visible = visible_block(users, first, last)
        weights = jnp.where(visible, scores * jax.nn.sigmoid(scores), 0.0).astype(jnp.bfloat16)
        block = dot(weights, part_rows(rows_ref, 3, 0, last), 1, 0)
        attended_ref[first * size : last * size] = block
        for window in range(first, last):
            here = slice(window * size, (window + 1) * size)
            attended = block[(window - first) * size : (window - first + 1) * size]
            grad_normed = (
                grads_ref[here].astype(jnp.float32)
                * gain_ref[...]
                * part_rows(rows_ref, 0, window, window + 1).astype(jnp.float32)
            )
            turned_att = attended.T
            turned_grad = grad_normed.T
            mean = jnp.mean(turned_att, axis=0, keepdims=True)
            centered = turned_att - mean
            spread = jnp.sum(centered * centered, axis=0, keepdims=True)
            grad_sum = jnp.sum(turned_grad, axis=0, keepdims=True)
            cross = jnp.sum(turned_grad * centered, axis=0, keepdims=True)
            stats_ref[0:1, here] = mean
            stats_ref[1:2, here] = spread
            stats_ref[2:3, here] = grad_sum
            stats_ref[3:4, here] = cross
            stats_ref[4:8, here] = jnp.zeros((4, size), jnp.float32)


def slope_kernel(rows_ref, slopes_ref, turned_slopes_ref, turned_weights_ref):
    size = HD
    scale = HD ** (-0.5)
    users = [window_users(rows_ref, window) for window in range(HEADS)]
    for first in range(0, HEADS, STEP):
        last = first + STEP
        queries = part_rows(rows_ref, 1, first, last)
        scores = dot(queries, part_rows(rows_ref, 2, 0, last), 1, 1) * scale
        sigmoid = jax.nn.sigmoid(scores)
        slopes = sigmoid * (1.0 + scores * (1.0 - sigmoid)) * scale
        visible = visible_block(users, first, last)
        slopes = jnp.where(visible, slopes, 0.0)
        weights = jnp.where(visible, scores * sigmoid, 0.0)
        slopes_ref[first * size : last * size, : last * size] = slopes
        turned_slopes_ref[: last * size, first * size : last * size] = slopes.T
        turned_weights_ref[: last * size, first * size : last * size] = weights.T.astype(
            jnp.bfloat16
        )


def backward_kernel(
    rows_ref,
    grads_ref,
    gain_ref,
    attended_ref,
    slopes_ref,
    turned_slopes_ref,
    turned_weights_ref,
    *refs,
):
    stats_refs = refs[:HEADS]
    out_hbm = refs[HEADS]
    layer_refs = refs[HEADS + 1 : 2 * HEADS + 1]
    layer_all, out_ref, out_grads, store_sems = refs[2 * HEADS + 1 :]
    head = my_place()[0]
    readers = rows_ref.shape[0] // HEADS
    size = HD
    width = float(HEADS * HD)
    stats = [stat_ref[...] for stat_ref in stats_refs]
    mean = sum(stat[0:1] for stat in stats) * (1.0 / HEADS)
    spread = sum(stat[1:2] + HD * (stat[0:1] - mean) * (stat[0:1] - mean) for stat in stats)
    inv_std = lax.rsqrt(spread / width + epsilon)
    mean_grad = sum(stat[2:3] for stat in stats) / width
    cross = sum(stat[3:4] + (stat[0:1] - mean) * stat[2:3] for stat in stats)
    mean_cross = cross * inv_std / width
    row = lax.broadcasted_iota(jnp.int32, (size, size), 0)
    for window in range(HEADS):
        here = slice(window * size, (window + 1) * size)
        packed = jnp.where(
            row == 0,
            mean[:, here],
            jnp.where(
                row == 1,
                inv_std[:, here],
                jnp.where(row == 2, mean_grad[:, here], mean_cross[:, here]),
            ),
        ).T
        unit = part_rows(rows_ref, 0, window, window + 1).astype(jnp.float32)
        grad_gain = grads_ref[here].astype(jnp.float32) * gain_ref[...]
        normed = (attended_ref[here] - packed[:, 0:1]) * packed[:, 1:2]
        layer_all[here] = (normed * gain_ref[...] * unit).astype(jnp.bfloat16)
        put_rows(out_ref, 0, window, window + 1, grad_gain * normed, readers)
        out_grads[here] = (
            packed[:, 1:2] * (grad_gain * unit - packed[:, 2:3] - normed * packed[:, 3:4])
        ).astype(jnp.bfloat16)
    stores = []
    for first in range(0, HEADS, STEP):
        last = first + STEP
        here = slice(first * size, last * size)
        upto = slice(0, last * size)
        after = slice(first * size, HEADS * size)
        score_grads = (
            dot(out_grads[here], part_rows(rows_ref, 3, 0, last), 1, 1) * slopes_ref[here, upto]
        ).astype(jnp.bfloat16)
        query_grads = dot(score_grads, part_rows(rows_ref, 2, 0, last), 1, 0)
        put_rows(out_ref, 1, first, last, query_grads, readers)
        turned_grads = (
            dot(part_rows(rows_ref, 3, first, last), out_grads[after], 1, 1)
            * turned_slopes_ref[here, after]
        ).astype(jnp.bfloat16)
        key_grads = dot(turned_grads, part_rows(rows_ref, 1, first, HEADS), 1, 0)
        put_rows(out_ref, 2, first, last, key_grads, readers)
        value_grads = dot(turned_weights_ref[here, after], out_grads[after], 1, 0)
        put_rows(out_ref, 3, first, last, value_grads, readers)
        span = pl.ds(first * size, STEP * size)
        stores.append(
            pltpu.make_async_copy(out_ref.at[span], out_hbm.at[span], store_sems.at[first])
        )
        stores[-1].start()
    for step, layer_ref in enumerate(layer_refs):
        start = pl.multiple_of(turned(head ^ step) * size, size)
        layer_ref[...] = layer_all[pl.ds(start, size), :]
    for copy in stores:
        copy.wait()


def unslot_kernel(back_ref, returned_ref, *refs, per_pair):
    piece_refs = refs[:HEADS]
    layer_hbm, grad_hbm, layer_ref, grad_ref, store_sems = refs[HEADS:]
    slots = back_ref.shape[0]
    readers = slots // per_pair
    width = HEADS * HD
    first = turned(lax.axis_index("ctx"))
    for step, piece_ref in enumerate(piece_refs):
        start = pl.multiple_of((first ^ step) * HD, HD)
        layer_ref[:, pl.ds(start, HD)] = piece_ref[...]
    stores = [pltpu.make_async_copy(layer_ref, layer_hbm, store_sems.at[2])]
    stores[0].start()
    heads = []
    for head in range(HEADS):
        chunks = []
        for owner in range(readers):
            dp_index, ctx_index = device_of(owner, head)
            start = chunk_of(dp_index, ctx_index, readers) * per_pair
            chunks.append(returned_ref[start : start + per_pair])
        heads.append(jnp.concatenate(chunks, axis=0))
    half = slots // 2
    for side in range(2):
        span = pl.ds(side * half, half)
        here = slice(side * half, (side + 1) * half)
        for head in range(HEADS):
            rows = dot(back_ref[here], heads[head], 1, 0).astype(jnp.bfloat16)
            for part in range(4):
                start = part * width + head * HD
                grad_ref[here, start : start + HD] = rows[:, part * HD : (part + 1) * HD]
        stores.append(
            pltpu.make_async_copy(grad_ref.at[span], grad_hbm.at[span], store_sems.at[side])
        )
        stores[-1].start()
    for copy in stores:
        copy.wait()


def send(value, target, back=False):
    width = lax.axis_size("ctx")
    pairs = []
    for dp_index in range(lax.axis_size("dp")):
        for ctx_index in range(width):
            to_dp, to_ctx = target(dp_index, ctx_index)
            pair = (dp_index * width + ctx_index, to_dp * width + to_ctx)
            pairs.append(pair[::-1] if back else pair)
    return lax.ppermute(value, ("dp", "ctx"), pairs)


def exchange(chunks):
    readers, width = lax.axis_size("dp"), lax.axis_size("ctx")
    order = [None] * (readers * width)
    for dp_index in range(readers):
        for ctx_index in range(width):
            order[chunk_of(dp_index, ctx_index, readers)] = dp_index * width + ctx_index
    return lax.all_to_all(
        chunks, ("dp", "ctx"), split_axis=0, concat_axis=0, tiled=True, axis_index_groups=[order]
    )


def swap(value, dp_bits, ctx_bits):
    return send(value, lambda dp_index, ctx_index: (dp_index ^ dp_bits, ctx_index ^ ctx_bits))


def regroup(pieces, back=False):
    moved = []
    for step, piece in enumerate(pieces):

        def target(dp_index, ctx_index, step=step):
            return device_of(dp_index, turned(ctx_index) ^ step)

        moved.append(send(piece, target, back))
    return moved


def by_heads(proj_read, norm_gain, owner_of, user_of, grad_output):
    slots = proj_read.shape[0]
    readers = lax.axis_size("dp")
    per_pair = slots // readers
    group_rows = slots * HEADS
    width = 4 * HD
    gain = lax.dynamic_slice_in_dim(norm_gain, my_place()[0] * HD, HD, 0).reshape(1, HD)
    piece_shape = jax.ShapeDtypeStruct((slots, HD), jnp.bfloat16)
    chunk_shape = (HEADS * readers, 4 * per_pair + 8, HD)
    outgoing, slot = pl.pallas_call(
        functools.partial(slot_kernel, per_pair=per_pair),
        out_shape=(
            jax.ShapeDtypeStruct(chunk_shape, jnp.bfloat16),
            jax.ShapeDtypeStruct((1, slots), jnp.int32),
        ),
        in_specs=hbm(3),
        out_specs=tuple(hbm(2)),
        scratch_shapes=[
            pltpu.SMEM(owner_of.shape, jnp.int32),
            pltpu.VMEM((1, slots), jnp.int32),
            pltpu.VMEM((1, slots), jnp.int32),
            pltpu.VMEM(proj_read.shape, jnp.bfloat16),
            pltpu.VMEM(chunk_shape, jnp.bfloat16),
            pltpu.SemaphoreType.DMA((3,)),
            pltpu.SemaphoreType.DMA((HEADS + 1,)),
        ],
        name="slot_rows",
    )(owner_of, user_of.reshape(1, slots), proj_read)
    rows = exchange(outgoing)
    *pieces, back = pl.pallas_call(
        columns_kernel,
        out_shape=(piece_shape,) * HEADS + (jax.ShapeDtypeStruct((slots, slots), jnp.bfloat16),),
        in_specs=vmem(2),
        out_specs=tuple(vmem(HEADS + 1)),
        compiler_params=LIMIT,
        name="cut_columns",
    )(slot, grad_output)
    grads = pl.pallas_call(
        group_kernel,
        out_shape=jax.ShapeDtypeStruct((group_rows, HD), jnp.bfloat16),
        in_specs=vmem(HEADS),
        out_specs=vmem(1)[0],
        compiler_params=LIMIT,
        name="lay_group",
    )(*regroup(pieces))
    attended, stats = pl.pallas_call(
        forward_kernel,
        out_shape=(
            jax.ShapeDtypeStruct((group_rows, HD), jnp.float32),
            jax.ShapeDtypeStruct((8, group_rows), jnp.float32),
        ),
        in_specs=vmem(3),
        out_specs=tuple(vmem(2)),
        compiler_params=LIMIT,
        name="forward",
    )(rows, grads, gain)
    late_rows, stats = lax.optimization_barrier((rows, stats))
    slopes = pl.pallas_call(
        slope_kernel,
        out_shape=(
            jax.ShapeDtypeStruct((group_rows, group_rows), jnp.float32),
            jax.ShapeDtypeStruct((group_rows, group_rows), jnp.float32),
            jax.ShapeDtypeStruct((group_rows, group_rows), jnp.bfloat16),
        ),
        in_specs=vmem(1),
        out_specs=tuple(vmem(3)),
        compiler_params=LIMIT,
        name="slopes",
    )(late_rows)
    all_stats = [stats, swap(stats, 1, 0), swap(stats, 0, 1), swap(stats, 1, 1)]
    results = pl.pallas_call(
        backward_kernel,
        out_shape=(jax.ShapeDtypeStruct((group_rows, width), jnp.bfloat16),)
        + (piece_shape,) * HEADS,
        in_specs=vmem(7 + HEADS),
        out_specs=tuple(hbm(1) + vmem(HEADS)),
        scratch_shapes=[
            pltpu.VMEM((group_rows, HD), jnp.bfloat16),
            pltpu.VMEM((group_rows, width), jnp.bfloat16),
            pltpu.VMEM((group_rows, HD), jnp.bfloat16),
            pltpu.SemaphoreType.DMA((HEADS,)),
        ],
        compiler_params=LIMIT,
        name="backward",
    )(rows, grads, gain, attended, *slopes, *all_stats)
    returned = exchange(results[0])
    layer_shape, grad_shape = (slots, HEADS * HD), (slots, 4 * HEADS * HD)
    return pl.pallas_call(
        functools.partial(unslot_kernel, per_pair=per_pair),
        out_shape=(
            jax.ShapeDtypeStruct(layer_shape, jnp.bfloat16),
            jax.ShapeDtypeStruct(grad_shape, jnp.bfloat16),
        ),
        in_specs=vmem(2 + HEADS),
        out_specs=tuple(hbm(2)),
        scratch_shapes=[
            pltpu.VMEM(layer_shape, jnp.bfloat16),
            pltpu.VMEM(grad_shape, jnp.bfloat16),
            pltpu.SemaphoreType.DMA((3,)),
        ],
        compiler_params=LIMIT,
        name="unslot_rows",
    )(back, returned, *regroup(results[1:], back=True))


def solution(mesh):
    in_specs = (P(("dp", "ctx"), None), P(), P(), P(("dp", "ctx")), P(("dp", "ctx"), None))
    out_specs = (P(("dp", "ctx"), None), P(("dp", "ctx"), None))
    local = by_heads if mesh.shape["ctx"] == HEADS else windowed
    return jax.shard_map(local, mesh=mesh, in_specs=in_specs, out_specs=out_specs, check_vma=False)
```

```python
import functools

import jax
import jax.numpy as jnp
from jax import lax
from jax.experimental import pallas as pl
from jax.experimental.pallas import tpu as pltpu
from jax.sharding import PartitionSpec as P

HEADS = 4
HD = 128


epsilon = 1e-05


def block_length(total_rows, shard_rows):
    shard_total = total_rows // shard_rows
    best_factor = 1
    for factor in range(1, shard_total + 1):
        if shard_total % factor == 0 and factor * shard_rows <= 1024:
            best_factor = factor
    return best_factor * shard_rows


def silu_slope(scores):
    sigmoid_part = jax.nn.sigmoid(scores)
    return sigmoid_part * (1.0 + scores * (1.0 - sigmoid_part))


def visible_pairs(query_users, query_places, key_users, key_places):
    same_user = (query_users[:, None] == key_users[None, :]) & (query_users[:, None] >= 0)
    return same_user & (key_places[None, :] <= query_places[:, None])


def run_blocks(carry_now, shard_piece, block_rows, step_fn):
    total_rows = shard_piece[0].shape[0]

    def one_block(block_index, carry_here):
        offset = block_index * block_rows
        block_part = tuple(
            (
                lax.dynamic_slice_in_dim(array_item, offset, block_rows, 0)
                for array_item in shard_piece
            )
        )
        return step_fn(carry_here, block_part, offset)

    return lax.fori_loop(0, total_rows // block_rows, one_block, carry_now)


def windowed(proj_read, norm_gain, owner_of, user_of, grad_output):
    slot_rows = proj_read.shape[0]
    reader_peers = lax.axis_size("dp")
    per_pair = slot_rows // reader_peers
    feature_width = HEADS * HD
    score_scale = HD ** (-0.5)
    group_rows = slot_rows * lax.axis_size("ctx")
    user_range = jnp.arange(owner_of.shape[0], dtype=jnp.int32)
    owners = jnp.sum(
        jnp.where(user_of[:, None] == user_range[None, :], owner_of[None, :], 0), axis=1
    )
    is_live = user_of >= 0
    owner_hits = (owners[:, None] == jnp.arange(reader_peers, dtype=jnp.int32)[None, :]) & is_live[
        :, None
    ]
    running = jnp.cumsum(owner_hits.astype(jnp.int32), axis=0) - 1
    ranks_mine = jnp.sum(jnp.where(owner_hits, running, 0), axis=1)
    send_slot = jnp.where(is_live, owners * per_pair + ranks_mine, -1)
    slot_range = jnp.arange(slot_rows, dtype=jnp.int32)
    slot_match = send_slot[None, :] == slot_range[:, None]
    filled = jnp.any(slot_match, axis=1)
    source_row = jnp.sum(jnp.where(slot_match, slot_range[None, :], 0), axis=1)
    outgoing = jnp.where(
        filled[:, None], jnp.take(proj_read, source_row, axis=0), jnp.zeros((), jnp.bfloat16)
    )
    outgoing_users = jnp.where(filled, jnp.take(user_of, source_row), -1)
    arrived, arrived_users = (
        lax.all_to_all(outgoing, "dp", split_axis=0, concat_axis=0, tiled=True),
        lax.all_to_all(outgoing_users, "dp", split_axis=0, concat_axis=0, tiled=True),
    )
    own_start = lax.axis_index("ctx") * slot_rows
    own_places = own_start + slot_range
    unit_rows = arrived[:, :feature_width]
    queries = arrived[:, feature_width : 2 * feature_width]
    key_values = arrived[:, 2 * feature_width :]
    query_heads = queries.reshape(slot_rows, HEADS, HD)
    key_heads = key_values[:, :feature_width].reshape(slot_rows, HEADS, HD)
    value_heads = key_values[:, feature_width:].reshape(slot_rows, HEADS, HD)

    def forward_step(total_out, block_part, first_row):
        block_kv, block_users = block_part
        block_size = block_kv.shape[0]
        remote_keys = block_kv[:, :feature_width].reshape(block_size, HEADS, HD)
        remote_values = block_kv[:, feature_width:].reshape(block_size, HEADS, HD)
        scores = (
            jnp.einsum("qhd,khd->hqk", query_heads, remote_keys, preferred_element_type=jnp.float32)
            * score_scale
        )
        visible = visible_pairs(
            arrived_users,
            own_places,
            block_users,
            first_row + jnp.arange(block_size, dtype=jnp.int32),
        )
        weights = jnp.where(visible[None], jax.nn.silu(scores), 0.0).astype(jnp.bfloat16)
        summed = jnp.einsum(
            "hqk,khd->qhd", weights, remote_values, preferred_element_type=jnp.float32
        )
        return total_out + summed.reshape(slot_rows, feature_width)

    zero_rows = jnp.zeros((slot_rows, feature_width), jnp.float32)
    shard_piece = (
        lax.all_gather(key_values, "ctx", axis=0, tiled=True),
        lax.all_gather(arrived_users, "ctx", axis=0, tiled=True),
    )
    block_rows = block_length(shard_piece[0].shape[0], slot_rows)
    forward_result = run_blocks(zero_rows, shard_piece, block_rows, forward_step)
    mean_out = jnp.mean(forward_result, axis=1, keepdims=True)
    centered = forward_result - mean_out
    inv_std = lax.rsqrt(jnp.mean(centered * centered, axis=1, keepdims=True) + epsilon)
    normed = centered * inv_std
    unit_float = unit_rows.astype(jnp.float32)
    layer_out = (normed * norm_gain * unit_float).astype(jnp.bfloat16)
    grad_float = grad_output.astype(jnp.float32)
    unit_grads = (grad_float * norm_gain * normed).astype(jnp.bfloat16)
    grad_normed = grad_float * norm_gain * unit_float
    mean_grad = jnp.mean(grad_normed, axis=1, keepdims=True)
    mean_cross = jnp.mean(grad_normed * normed, axis=1, keepdims=True)
    out_grads = (inv_std * (grad_normed - mean_grad - normed * mean_cross)).astype(jnp.bfloat16)

    def backward_step(carry_here, block_part, first_row):
        block_queries, block_grads, block_users = block_part
        block_size = block_queries.shape[0]
        remote_queries = block_queries.reshape(block_size, HEADS, HD)
        remote_grads = block_grads.reshape(block_size, HEADS, HD)
        scores = (
            jnp.einsum(
                "qhd,khd->hqk", remote_queries, key_heads, preferred_element_type=jnp.float32
            )
            * score_scale
        )
        visible = visible_pairs(
            block_users,
            first_row + jnp.arange(block_size, dtype=jnp.int32),
            arrived_users,
            own_places,
        )[None]
        weights = jnp.where(visible, jax.nn.silu(scores), 0.0).astype(jnp.bfloat16)
        weight_grads = jnp.einsum(
            "qhd,khd->hqk", remote_grads, value_heads, preferred_element_type=jnp.float32
        )
        score_grads = jnp.where(
            visible, weight_grads * silu_slope(scores) * score_scale, 0.0
        ).astype(jnp.bfloat16)
        value_sum = jnp.einsum(
            "hqk,qhd->khd", weights, remote_grads, preferred_element_type=jnp.float32
        ).reshape(slot_rows, feature_width)
        key_sum = jnp.einsum(
            "hqk,qhd->khd", score_grads, remote_queries, preferred_element_type=jnp.float32
        ).reshape(slot_rows, feature_width)
        new_keys = carry_here[0] + key_sum
        new_values = carry_here[1] + value_sum
        window_sum = (
            jnp.einsum("hqk,khd->qhd", score_grads, key_heads, preferred_element_type=jnp.float32)
            .reshape(block_size, feature_width)
            .astype(jnp.bfloat16)
        )
        return (
            new_keys,
            new_values,
            lax.dynamic_update_slice_in_dim(carry_here[2], window_sum, first_row, 0),
        )

    start_carry = (zero_rows, zero_rows, jnp.zeros((group_rows, feature_width), jnp.bfloat16))
    shard_piece = (
        lax.all_gather(queries, "ctx", axis=0, tiled=True),
        lax.all_gather(out_grads, "ctx", axis=0, tiled=True),
        lax.all_gather(arrived_users, "ctx", axis=0, tiled=True),
    )
    block_rows = block_length(shard_piece[0].shape[0], slot_rows)
    key_results = run_blocks(start_carry, shard_piece, block_rows, backward_step)
    key_grads = key_results[0]
    value_grads = key_results[1]
    query_grads = lax.psum_scatter(key_results[2], "ctx", scatter_dimension=0, tiled=True).astype(
        jnp.float32
    )
    grads_owned = jnp.concatenate(
        [
            unit_grads,
            query_grads.astype(jnp.bfloat16),
            key_grads.astype(jnp.bfloat16),
            value_grads.astype(jnp.bfloat16),
        ],
        axis=1,
    )
    returned = lax.all_to_all(grads_owned, "dp", split_axis=0, concat_axis=0, tiled=True)
    back_rows = jnp.take(returned, jnp.maximum(send_slot, 0), axis=0)
    grad_read = jnp.where(is_live[:, None], back_rows, jnp.zeros((), jnp.bfloat16))
    return (layer_out, grad_read)


STEP = 2
LIMIT = pltpu.CompilerParams(vmem_limit_bytes=16 * 2**20)


def device_of(owner, head):
    return (owner & ~1) | (head & 1), ((owner & 1) << 1) | (head >> 1)


SPANS = (3, 1, 2, 0)


def chunk_of(dp_index, ctx_index, readers):
    return turned(ctx_index) * readers + SPANS[dp_index >> 1] * 2 + (dp_index & 1)


def chunk_back(dp_index, ctx_index, readers):
    return ctx_index * readers + (dp_index & 1) * (readers // 2) + (dp_index >> 1)


def turned(index):
    return ((index & 1) << 1) | (index >> 1)


def vmem(count):
    return [pl.BlockSpec(memory_space=pltpu.VMEM)] * count


def hbm(count):
    return [pl.BlockSpec(memory_space=pltpu.HBM)] * count


def dot(left, right, left_dim, right_dim):
    return lax.dot_general(
        left, right, (((left_dim,), (right_dim,)), ((), ())), preferred_element_type=jnp.float32
    )


def owners_of(users, owner_ref):
    owners = jnp.zeros_like(users)
    for user in range(owner_ref.shape[0]):
        owners = jnp.where(users == user, owner_ref[user], owners)
    return owners


def lower_ones(size):
    earlier = lax.broadcasted_iota(jnp.int32, (size, size), 0)
    later = lax.broadcasted_iota(jnp.int32, (size, size), 1)
    return (earlier <= later).astype(jnp.bfloat16)


def my_place():
    my_dp, my_ctx = lax.axis_index("dp"), lax.axis_index("ctx")
    return ((my_ctx & 1) << 1) | (my_dp & 1), (my_dp & ~1) | (my_ctx >> 1), my_dp, my_ctx


def slot_kernel(
    owner_hbm,
    user_hbm,
    proj_hbm,
    send_hbm,
    slot_hbm,
    owner_ref,
    user_ref,
    slot_ref,
    proj_ref,
    send_ref,
    load_sems,
    store_sems,
    *,
    per_pair,
):
    slots = user_ref.shape[1]
    readers = slots // per_pair
    width = HEADS * HD
    loads = [
        pltpu.make_async_copy(source, target, load_sems.at[index])
        for index, (source, target) in enumerate(
            ((user_hbm, user_ref), (owner_hbm, owner_ref), (proj_hbm, proj_ref))
        )
    ]
    for copy in loads:
        copy.start()
    my_dp = lax.axis_index("dp")
    source = lax.broadcasted_iota(jnp.int32, (slots, slots), 0)
    target = lax.broadcasted_iota(jnp.int32, (slots, slots), 1)
    owner_range = lax.broadcasted_iota(jnp.int32, (readers, slots), 0)
    by_owner = lax.div(lax.broadcasted_iota(jnp.int32, (readers, slots), 1), per_pair)
    to_lane = (lax.div(target, per_pair) == my_dp) & (
        lax.rem(target, per_pair) == lax.rem(source, per_pair)
    )
    loads[0].wait()
    loads[1].wait()
    users = user_ref[...]
    owners = owners_of(users, owner_ref)
    is_live = users >= 0
    hits = ((owner_range == owners) & is_live).astype(jnp.float32)
    running = dot(hits.astype(jnp.bfloat16), lower_ones(slots), 1, 0)
    ranks = jnp.sum(hits * running, axis=0, keepdims=True).astype(jnp.int32) - 1
    slot = jnp.where(is_live, owners * per_pair + ranks, -1)
    slot_ref[...] = slot
    stores = [pltpu.make_async_copy(slot_ref, slot_hbm, store_sems.at[HEADS])]
    stores[0].start()
    placed = (source == slot).astype(jnp.bfloat16)
    tagged = jnp.broadcast_to((users + 1).astype(jnp.float32), (readers, slots))
    tagged = dot(tagged.astype(jnp.bfloat16), placed, 1, 1)
    tagged = jnp.where(by_owner == owner_range, tagged, 0.0).astype(jnp.bfloat16)
    tagged = dot(tagged, to_lane.astype(jnp.bfloat16), 1, 0).astype(jnp.bfloat16)
    extra = send_ref.shape[1] - 4 * per_pair
    for owner in range(readers):
        for head in range(HEADS):
            dp_index, ctx_index = device_of(owner, head)
            chunk = chunk_of(dp_index, ctx_index, readers)
            send_ref[chunk, 4 * per_pair :, :] = jnp.broadcast_to(
                tagged[owner : owner + 1], (extra, slots)
            )
    loads[2].wait()
    for half in range(2):
        for part in range(4):
            start = part * width + half * 2 * HD
            rows = dot(placed, proj_ref[:, start : start + 2 * HD], 1, 0).astype(jnp.bfloat16)
            for owner in range(readers):
                for side in range(2):
                    dp_index, ctx_index = device_of(owner, 2 * half + side)
                    chunk = chunk_of(dp_index, ctx_index, readers)
                    send_ref[chunk, part * per_pair : (part + 1) * per_pair, :] = rows[
                        owner * per_pair : (owner + 1) * per_pair, side * HD : (side + 1) * HD
                    ]
        for ctx_index in (half, 2 + half):
            span = pl.ds(turned(ctx_index) * readers, readers)
            stores.append(
                pltpu.make_async_copy(
                    send_ref.at[span], send_hbm.at[span], store_sems.at[ctx_index]
                )
            )
            stores[-1].start()
    for copy in stores:
        copy.wait()


def columns_kernel(slot_ref, grad_ref, *refs):
    piece_refs, back_ref = refs[:HEADS], refs[HEADS]
    slots = slot_ref.shape[1]
    slot = jnp.broadcast_to(slot_ref[...].astype(jnp.float32), (slots, slots)).T
    lane = lax.broadcasted_iota(jnp.int32, (slots, slots), 1).astype(jnp.float32)
    back_ref[...] = (slot == lane).astype(jnp.bfloat16)
    first = turned(lax.axis_index("ctx"))
    for step, piece_ref in enumerate(piece_refs):
        start = pl.multiple_of((first ^ step) * HD, HD)
        piece_ref[...] = grad_ref[:, pl.ds(start, HD)]


def group_kernel(*refs):
    piece_refs, grads_ref = refs[:HEADS], refs[HEADS]
    head = my_place()[0]
    for step, piece_ref in enumerate(piece_refs):
        slots = piece_ref.shape[0]
        start = pl.multiple_of(turned(head ^ step) * slots, slots)
        grads_ref[pl.ds(start, slots), :] = piece_ref[...]


def part_rows(rows_ref, part, first, last):
    readers = rows_ref.shape[0] // HEADS
    per_pair = HD // readers
    span = slice(part * per_pair, (part + 1) * per_pair)
    rows = [
        rows_ref[chunk_of(reader, window, readers), span, :]
        for window in range(first, last)
        for reader in range(readers)
    ]
    return jnp.concatenate(rows, axis=0)


def put_rows(out_ref, part, first, last, rows, readers):
    per_pair = HD // readers
    for window in range(first, last):
        for reader in range(readers):
            source = ((window - first) * readers + reader) * per_pair
            target = chunk_back(reader, window, readers) * per_pair
            out_ref[target : target + per_pair, part * HD : (part + 1) * HD] = rows[
                source : source + per_pair
            ].astype(jnp.bfloat16)


def window_users(rows_ref, window):
    readers = rows_ref.shape[0] // HEADS
    per_pair = HD // readers
    first = turned(window) * readers
    tags = rows_ref[first : first + readers, 4 * per_pair :, :]
    return jnp.sum(tags.astype(jnp.float32), axis=0)[:1]


def visible_block(users, first, last):
    size = HD
    query_users = [jnp.broadcast_to(users[window], (size, size)).T for window in range(first, last)]
    query_users = jnp.concatenate(query_users, axis=0)
    rows = lax.broadcasted_iota(jnp.int32, query_users.shape, 0)
    columns = lax.broadcasted_iota(jnp.int32, query_users.shape, 1)
    blocks = []
    for window in range(last):
        block = (query_users == users[window]) & (query_users > 0.0)
        if window >= first:
            block = block & (columns + (window - first) * size <= rows)
        blocks.append(block)
    return jnp.concatenate(blocks, axis=1)


def forward_kernel(rows_ref, grads_ref, gain_ref, attended_ref, stats_ref):
    size = HD
    scale = HD ** (-0.5)
    users = [window_users(rows_ref, window) for window in range(HEADS)]
    for first in range(0, HEADS, STEP):
        last = first + STEP
        queries = part_rows(rows_ref, 1, first, last)
        scores = dot(queries, part_rows(rows_ref, 2, 0, last), 1, 1) * scale
        visible = visible_block(users, first, last)
        weights = jnp.where(visible, scores * jax.nn.sigmoid(scores), 0.0).astype(jnp.bfloat16)
        block = dot(weights, part_rows(rows_ref, 3, 0, last), 1, 0)
        attended_ref[first * size : last * size] = block
        for window in range(first, last):
            here = slice(window * size, (window + 1) * size)
            attended = block[(window - first) * size : (window - first + 1) * size]
            grad_normed = (
                grads_ref[here].astype(jnp.float32)
                * gain_ref[...]
                * part_rows(rows_ref, 0, window, window + 1).astype(jnp.float32)
            )
            turned_att = attended.T
            turned_grad = grad_normed.T
            mean = jnp.mean(turned_att, axis=0, keepdims=True)
            centered = turned_att - mean
            spread = jnp.sum(centered * centered, axis=0, keepdims=True)
            grad_sum = jnp.sum(turned_grad, axis=0, keepdims=True)
            cross = jnp.sum(turned_grad * centered, axis=0, keepdims=True)
            stats_ref[0:1, here] = mean
            stats_ref[1:2, here] = spread
            stats_ref[2:3, here] = grad_sum
            stats_ref[3:4, here] = cross
            stats_ref[4:8, here] = jnp.zeros((4, size), jnp.float32)


def slope_kernel(rows_ref, slopes_ref, turned_slopes_ref, turned_weights_ref):
    size = HD
    scale = HD ** (-0.5)
    users = [window_users(rows_ref, window) for window in range(HEADS)]
    for first in range(0, HEADS, STEP):
        last = first + STEP
        queries = part_rows(rows_ref, 1, first, last)
        scores = dot(queries, part_rows(rows_ref, 2, 0, last), 1, 1) * scale
        sigmoid = jax.nn.sigmoid(scores)
        slopes = sigmoid * (1.0 + scores * (1.0 - sigmoid)) * scale
        visible = visible_block(users, first, last)
        slopes = jnp.where(visible, slopes, 0.0)
        weights = jnp.where(visible, scores * sigmoid, 0.0)
        slopes_ref[first * size : last * size, : last * size] = slopes
        turned_slopes_ref[: last * size, first * size : last * size] = slopes.T
        turned_weights_ref[: last * size, first * size : last * size] = weights.T.astype(
            jnp.bfloat16
        )


def backward_kernel(
    rows_ref,
    grads_ref,
    gain_ref,
    attended_ref,
    slopes_ref,
    turned_slopes_ref,
    turned_weights_ref,
    *refs,
):
    stats_refs = refs[:HEADS]
    out_hbm = refs[HEADS]
    layer_refs = refs[HEADS + 1 : 2 * HEADS + 1]
    layer_all, out_ref, store_sems = refs[2 * HEADS + 1 :]
    head = my_place()[0]
    readers = rows_ref.shape[0] // HEADS
    size = HD
    width = float(HEADS * HD)
    stats = [stat_ref[...] for stat_ref in stats_refs]
    mean = sum(stat[0:1] for stat in stats) * (1.0 / HEADS)
    spread = sum(stat[1:2] + HD * (stat[0:1] - mean) * (stat[0:1] - mean) for stat in stats)
    inv_std = lax.rsqrt(spread / width + epsilon)
    mean_grad = sum(stat[2:3] for stat in stats) / width
    cross = sum(stat[3:4] + (stat[0:1] - mean) * stat[2:3] for stat in stats)
    mean_cross = cross * inv_std / width
    row = lax.broadcasted_iota(jnp.int32, (size, size), 0)
    out_grads = []
    for window in range(HEADS):
        here = slice(window * size, (window + 1) * size)
        packed = jnp.where(
            row == 0,
            mean[:, here],
            jnp.where(
                row == 1,
                inv_std[:, here],
                jnp.where(row == 2, mean_grad[:, here], mean_cross[:, here]),
            ),
        ).T
        unit = part_rows(rows_ref, 0, window, window + 1).astype(jnp.float32)
        grad_gain = grads_ref[here].astype(jnp.float32) * gain_ref[...]
        normed = (attended_ref[here] - packed[:, 0:1]) * packed[:, 1:2]
        layer_all[here] = (normed * gain_ref[...] * unit).astype(jnp.bfloat16)
        put_rows(out_ref, 0, window, window + 1, grad_gain * normed, readers)
        out_grads.append(
            packed[:, 1:2] * (grad_gain * unit - packed[:, 2:3] - normed * packed[:, 3:4])
        )
    out_grads = jnp.concatenate(out_grads, axis=0).astype(jnp.bfloat16)
    stores = []
    for first in range(0, HEADS, STEP):
        last = first + STEP
        here = slice(first * size, last * size)
        upto = slice(0, last * size)
        after = slice(first * size, HEADS * size)
        score_grads = (
            dot(out_grads[here], part_rows(rows_ref, 3, 0, last), 1, 1) * slopes_ref[here, upto]
        ).astype(jnp.bfloat16)
        query_grads = dot(score_grads, part_rows(rows_ref, 2, 0, last), 1, 0)
        put_rows(out_ref, 1, first, last, query_grads, readers)
        turned_grads = (
            dot(part_rows(rows_ref, 3, first, last), out_grads[after], 1, 1)
            * turned_slopes_ref[here, after]
        ).astype(jnp.bfloat16)
        key_grads = dot(turned_grads, part_rows(rows_ref, 1, first, HEADS), 1, 0)
        put_rows(out_ref, 2, first, last, key_grads, readers)
        value_grads = dot(turned_weights_ref[here, after], out_grads[after], 1, 0)
        put_rows(out_ref, 3, first, last, value_grads, readers)
        for window in range(first, last):
            span = pl.ds(window * size, size)
            stores.append(
                pltpu.make_async_copy(out_ref.at[span], out_hbm.at[span], store_sems.at[window])
            )
            stores[-1].start()
    for step, layer_ref in enumerate(layer_refs):
        start = pl.multiple_of(turned(head ^ step) * size, size)
        layer_ref[...] = layer_all[pl.ds(start, size), :]
    for copy in stores:
        copy.wait()


def unslot_kernel(back_ref, returned_ref, *refs, per_pair):
    piece_refs = refs[:HEADS]
    layer_hbm, grad_hbm, layer_ref, grad_ref, store_sems = refs[HEADS:]
    slots = back_ref.shape[0]
    readers = slots // per_pair
    width = HEADS * HD
    first = turned(lax.axis_index("ctx"))
    for step, piece_ref in enumerate(piece_refs):
        start = pl.multiple_of((first ^ step) * HD, HD)
        layer_ref[:, pl.ds(start, HD)] = piece_ref[...]
    stores = [pltpu.make_async_copy(layer_ref, layer_hbm, store_sems.at[2])]
    stores[0].start()
    heads = []
    for head in range(HEADS):
        chunks = []
        for owner in range(readers):
            dp_index, ctx_index = device_of(owner, head)
            start = chunk_back(dp_index, ctx_index, readers) * per_pair
            chunks.append(returned_ref[start : start + per_pair])
        heads.append(jnp.concatenate(chunks, axis=0))
    half = slots // 2
    for side in range(2):
        span = pl.ds(side * half, half)
        here = slice(side * half, (side + 1) * half)
        for head in range(HEADS):
            rows = dot(back_ref[here], heads[head], 1, 0).astype(jnp.bfloat16)
            for part in range(4):
                start = part * width + head * HD
                grad_ref[here, start : start + HD] = rows[:, part * HD : (part + 1) * HD]
        stores.append(
            pltpu.make_async_copy(grad_ref.at[span], grad_hbm.at[span], store_sems.at[side])
        )
        stores[-1].start()
    for copy in stores:
        copy.wait()


def send(value, target, back=False):
    width = lax.axis_size("ctx")
    pairs = []
    for dp_index in range(lax.axis_size("dp")):
        for ctx_index in range(width):
            to_dp, to_ctx = target(dp_index, ctx_index)
            pair = (dp_index * width + ctx_index, to_dp * width + to_ctx)
            pairs.append(pair[::-1] if back else pair)
    return lax.ppermute(value, ("dp", "ctx"), pairs)


def exchange(chunks, place):
    readers, width = lax.axis_size("dp"), lax.axis_size("ctx")
    order = [None] * (readers * width)
    for dp_index in range(readers):
        for ctx_index in range(width):
            order[place(dp_index, ctx_index, readers)] = dp_index * width + ctx_index
    return lax.all_to_all(
        chunks, ("dp", "ctx"), split_axis=0, concat_axis=0, tiled=True, axis_index_groups=[order]
    )


def swap(value, dp_bits, ctx_bits):
    return send(value, lambda dp_index, ctx_index: (dp_index ^ dp_bits, ctx_index ^ ctx_bits))


def regroup(pieces, back=False):
    moved = []
    for step, piece in enumerate(pieces):

        def target(dp_index, ctx_index, step=step):
            return device_of(dp_index, turned(ctx_index) ^ step)

        moved.append(send(piece, target, back))
    return moved


def by_heads(proj_read, norm_gain, owner_of, user_of, grad_output):
    slots = proj_read.shape[0]
    readers = lax.axis_size("dp")
    per_pair = slots // readers
    group_rows = slots * HEADS
    width = 4 * HD
    gain = lax.dynamic_slice_in_dim(norm_gain, my_place()[0] * HD, HD, 0).reshape(1, HD)
    piece_shape = jax.ShapeDtypeStruct((slots, HD), jnp.bfloat16)
    chunk_shape = (HEADS * readers, 4 * per_pair + 8, HD)
    outgoing, slot = pl.pallas_call(
        functools.partial(slot_kernel, per_pair=per_pair),
        out_shape=(
            jax.ShapeDtypeStruct(chunk_shape, jnp.bfloat16),
            jax.ShapeDtypeStruct((1, slots), jnp.int32),
        ),
        in_specs=hbm(3),
        out_specs=tuple(hbm(2)),
        scratch_shapes=[
            pltpu.SMEM(owner_of.shape, jnp.int32),
            pltpu.VMEM((1, slots), jnp.int32),
            pltpu.VMEM((1, slots), jnp.int32),
            pltpu.VMEM(proj_read.shape, jnp.bfloat16),
            pltpu.VMEM(chunk_shape, jnp.bfloat16),
            pltpu.SemaphoreType.DMA((3,)),
            pltpu.SemaphoreType.DMA((HEADS + 1,)),
        ],
        name="slot_rows",
    )(owner_of, user_of.reshape(1, slots), proj_read)
    rows = exchange(outgoing, chunk_of)
    *pieces, back = pl.pallas_call(
        columns_kernel,
        out_shape=(piece_shape,) * HEADS + (jax.ShapeDtypeStruct((slots, slots), jnp.bfloat16),),
        in_specs=vmem(2),
        out_specs=tuple(vmem(HEADS + 1)),
        compiler_params=LIMIT,
        name="cut_columns",
    )(slot, grad_output)
    grads = pl.pallas_call(
        group_kernel,
        out_shape=jax.ShapeDtypeStruct((group_rows, HD), jnp.bfloat16),
        in_specs=vmem(HEADS),
        out_specs=vmem(1)[0],
        compiler_params=LIMIT,
        name="lay_group",
    )(*regroup(pieces))
    attended, stats = pl.pallas_call(
        forward_kernel,
        out_shape=(
            jax.ShapeDtypeStruct((group_rows, HD), jnp.float32),
            jax.ShapeDtypeStruct((8, group_rows), jnp.float32),
        ),
        in_specs=vmem(3),
        out_specs=tuple(vmem(2)),
        compiler_params=LIMIT,
        name="forward",
    )(rows, grads, gain)
    late_rows, stats = lax.optimization_barrier((rows, stats))
    slopes = pl.pallas_call(
        slope_kernel,
        out_shape=(
            jax.ShapeDtypeStruct((group_rows, group_rows), jnp.float32),
            jax.ShapeDtypeStruct((group_rows, group_rows), jnp.float32),
            jax.ShapeDtypeStruct((group_rows, group_rows), jnp.bfloat16),
        ),
        in_specs=vmem(1),
        out_specs=tuple(vmem(3)),
        compiler_params=LIMIT,
        name="slopes",
    )(late_rows)
    all_stats = [stats, swap(stats, 1, 0), swap(stats, 0, 1), swap(stats, 1, 1)]
    results = pl.pallas_call(
        backward_kernel,
        out_shape=(jax.ShapeDtypeStruct((group_rows, width), jnp.bfloat16),)
        + (piece_shape,) * HEADS,
        in_specs=vmem(7 + HEADS),
        out_specs=tuple(hbm(1) + vmem(HEADS)),
        scratch_shapes=[
            pltpu.VMEM((group_rows, HD), jnp.bfloat16),
            pltpu.VMEM((group_rows, width), jnp.bfloat16),
            pltpu.SemaphoreType.DMA((HEADS,)),
        ],
        compiler_params=LIMIT,
        name="backward",
    )(rows, grads, gain, attended, *slopes, *all_stats)
    returned = exchange(results[0], chunk_back)
    layer_shape, grad_shape = (slots, HEADS * HD), (slots, 4 * HEADS * HD)
    return pl.pallas_call(
        functools.partial(unslot_kernel, per_pair=per_pair),
        out_shape=(
            jax.ShapeDtypeStruct(layer_shape, jnp.bfloat16),
            jax.ShapeDtypeStruct(grad_shape, jnp.bfloat16),
        ),
        in_specs=vmem(2 + HEADS),
        out_specs=tuple(hbm(2)),
        scratch_shapes=[
            pltpu.VMEM(layer_shape, jnp.bfloat16),
            pltpu.VMEM(grad_shape, jnp.bfloat16),
            pltpu.SemaphoreType.DMA((3,)),
        ],
        compiler_params=LIMIT,
        name="unslot_rows",
    )(back, returned, *regroup(results[1:], back=True))


def solution(mesh):
    in_specs = (P(("dp", "ctx"), None), P(), P(), P(("dp", "ctx")), P(("dp", "ctx"), None))
    out_specs = (P(("dp", "ctx"), None), P(("dp", "ctx"), None))
    fits = mesh.shape["ctx"] == HEADS and mesh.shape["dp"] == 2 * len(SPANS)
    local = by_heads if fits else windowed
    return jax.shard_map(local, mesh=mesh, in_specs=in_specs, out_specs=out_specs, check_vma=False)
```

```python
import functools

import jax
import jax.numpy as jnp
from jax import lax
from jax.experimental import pallas as pl
from jax.experimental.pallas import tpu as pltpu
from jax.sharding import PartitionSpec as P

HEADS = 4
HD = 128


epsilon = 1e-05


def block_length(total_rows, shard_rows):
    shard_total = total_rows // shard_rows
    best_factor = 1
    for factor in range(1, shard_total + 1):
        if shard_total % factor == 0 and factor * shard_rows <= 1024:
            best_factor = factor
    return best_factor * shard_rows


def silu_slope(scores):
    sigmoid_part = jax.nn.sigmoid(scores)
    return sigmoid_part * (1.0 + scores * (1.0 - sigmoid_part))


def visible_pairs(query_users, query_places, key_users, key_places):
    same_user = (query_users[:, None] == key_users[None, :]) & (query_users[:, None] >= 0)
    return same_user & (key_places[None, :] <= query_places[:, None])


def run_blocks(carry_now, shard_piece, block_rows, step_fn):
    total_rows = shard_piece[0].shape[0]

    def one_block(block_index, carry_here):
        offset = block_index * block_rows
        block_part = tuple(
            (
                lax.dynamic_slice_in_dim(array_item, offset, block_rows, 0)
                for array_item in shard_piece
            )
        )
        return step_fn(carry_here, block_part, offset)

    return lax.fori_loop(0, total_rows // block_rows, one_block, carry_now)


def windowed(proj_read, norm_gain, owner_of, user_of, grad_output):
    slot_rows = proj_read.shape[0]
    reader_peers = lax.axis_size("dp")
    per_pair = slot_rows // reader_peers
    feature_width = HEADS * HD
    score_scale = HD ** (-0.5)
    group_rows = slot_rows * lax.axis_size("ctx")
    user_range = jnp.arange(owner_of.shape[0], dtype=jnp.int32)
    owners = jnp.sum(
        jnp.where(user_of[:, None] == user_range[None, :], owner_of[None, :], 0), axis=1
    )
    is_live = user_of >= 0
    owner_hits = (owners[:, None] == jnp.arange(reader_peers, dtype=jnp.int32)[None, :]) & is_live[
        :, None
    ]
    running = jnp.cumsum(owner_hits.astype(jnp.int32), axis=0) - 1
    ranks_mine = jnp.sum(jnp.where(owner_hits, running, 0), axis=1)
    send_slot = jnp.where(is_live, owners * per_pair + ranks_mine, -1)
    slot_range = jnp.arange(slot_rows, dtype=jnp.int32)
    slot_match = send_slot[None, :] == slot_range[:, None]
    filled = jnp.any(slot_match, axis=1)
    source_row = jnp.sum(jnp.where(slot_match, slot_range[None, :], 0), axis=1)
    outgoing = jnp.where(
        filled[:, None], jnp.take(proj_read, source_row, axis=0), jnp.zeros((), jnp.bfloat16)
    )
    outgoing_users = jnp.where(filled, jnp.take(user_of, source_row), -1)
    arrived, arrived_users = (
        lax.all_to_all(outgoing, "dp", split_axis=0, concat_axis=0, tiled=True),
        lax.all_to_all(outgoing_users, "dp", split_axis=0, concat_axis=0, tiled=True),
    )
    own_start = lax.axis_index("ctx") * slot_rows
    own_places = own_start + slot_range
    unit_rows = arrived[:, :feature_width]
    queries = arrived[:, feature_width : 2 * feature_width]
    key_values = arrived[:, 2 * feature_width :]
    query_heads = queries.reshape(slot_rows, HEADS, HD)
    key_heads = key_values[:, :feature_width].reshape(slot_rows, HEADS, HD)
    value_heads = key_values[:, feature_width:].reshape(slot_rows, HEADS, HD)

    def forward_step(total_out, block_part, first_row):
        block_kv, block_users = block_part
        block_size = block_kv.shape[0]
        remote_keys = block_kv[:, :feature_width].reshape(block_size, HEADS, HD)
        remote_values = block_kv[:, feature_width:].reshape(block_size, HEADS, HD)
        scores = (
            jnp.einsum("qhd,khd->hqk", query_heads, remote_keys, preferred_element_type=jnp.float32)
            * score_scale
        )
        visible = visible_pairs(
            arrived_users,
            own_places,
            block_users,
            first_row + jnp.arange(block_size, dtype=jnp.int32),
        )
        weights = jnp.where(visible[None], jax.nn.silu(scores), 0.0).astype(jnp.bfloat16)
        summed = jnp.einsum(
            "hqk,khd->qhd", weights, remote_values, preferred_element_type=jnp.float32
        )
        return total_out + summed.reshape(slot_rows, feature_width)

    zero_rows = jnp.zeros((slot_rows, feature_width), jnp.float32)
    shard_piece = (
        lax.all_gather(key_values, "ctx", axis=0, tiled=True),
        lax.all_gather(arrived_users, "ctx", axis=0, tiled=True),
    )
    block_rows = block_length(shard_piece[0].shape[0], slot_rows)
    forward_result = run_blocks(zero_rows, shard_piece, block_rows, forward_step)
    mean_out = jnp.mean(forward_result, axis=1, keepdims=True)
    centered = forward_result - mean_out
    inv_std = lax.rsqrt(jnp.mean(centered * centered, axis=1, keepdims=True) + epsilon)
    normed = centered * inv_std
    unit_float = unit_rows.astype(jnp.float32)
    layer_out = (normed * norm_gain * unit_float).astype(jnp.bfloat16)
    grad_float = grad_output.astype(jnp.float32)
    unit_grads = (grad_float * norm_gain * normed).astype(jnp.bfloat16)
    grad_normed = grad_float * norm_gain * unit_float
    mean_grad = jnp.mean(grad_normed, axis=1, keepdims=True)
    mean_cross = jnp.mean(grad_normed * normed, axis=1, keepdims=True)
    out_grads = (inv_std * (grad_normed - mean_grad - normed * mean_cross)).astype(jnp.bfloat16)

    def backward_step(carry_here, block_part, first_row):
        block_queries, block_grads, block_users = block_part
        block_size = block_queries.shape[0]
        remote_queries = block_queries.reshape(block_size, HEADS, HD)
        remote_grads = block_grads.reshape(block_size, HEADS, HD)
        scores = (
            jnp.einsum(
                "qhd,khd->hqk", remote_queries, key_heads, preferred_element_type=jnp.float32
            )
            * score_scale
        )
        visible = visible_pairs(
            block_users,
            first_row + jnp.arange(block_size, dtype=jnp.int32),
            arrived_users,
            own_places,
        )[None]
        weights = jnp.where(visible, jax.nn.silu(scores), 0.0).astype(jnp.bfloat16)
        weight_grads = jnp.einsum(
            "qhd,khd->hqk", remote_grads, value_heads, preferred_element_type=jnp.float32
        )
        score_grads = jnp.where(
            visible, weight_grads * silu_slope(scores) * score_scale, 0.0
        ).astype(jnp.bfloat16)
        value_sum = jnp.einsum(
            "hqk,qhd->khd", weights, remote_grads, preferred_element_type=jnp.float32
        ).reshape(slot_rows, feature_width)
        key_sum = jnp.einsum(
            "hqk,qhd->khd", score_grads, remote_queries, preferred_element_type=jnp.float32
        ).reshape(slot_rows, feature_width)
        new_keys = carry_here[0] + key_sum
        new_values = carry_here[1] + value_sum
        window_sum = (
            jnp.einsum("hqk,khd->qhd", score_grads, key_heads, preferred_element_type=jnp.float32)
            .reshape(block_size, feature_width)
            .astype(jnp.bfloat16)
        )
        return (
            new_keys,
            new_values,
            lax.dynamic_update_slice_in_dim(carry_here[2], window_sum, first_row, 0),
        )

    start_carry = (zero_rows, zero_rows, jnp.zeros((group_rows, feature_width), jnp.bfloat16))
    shard_piece = (
        lax.all_gather(queries, "ctx", axis=0, tiled=True),
        lax.all_gather(out_grads, "ctx", axis=0, tiled=True),
        lax.all_gather(arrived_users, "ctx", axis=0, tiled=True),
    )
    block_rows = block_length(shard_piece[0].shape[0], slot_rows)
    key_results = run_blocks(start_carry, shard_piece, block_rows, backward_step)
    key_grads = key_results[0]
    value_grads = key_results[1]
    query_grads = lax.psum_scatter(key_results[2], "ctx", scatter_dimension=0, tiled=True).astype(
        jnp.float32
    )
    grads_owned = jnp.concatenate(
        [
            unit_grads,
            query_grads.astype(jnp.bfloat16),
            key_grads.astype(jnp.bfloat16),
            value_grads.astype(jnp.bfloat16),
        ],
        axis=1,
    )
    returned = lax.all_to_all(grads_owned, "dp", split_axis=0, concat_axis=0, tiled=True)
    back_rows = jnp.take(returned, jnp.maximum(send_slot, 0), axis=0)
    grad_read = jnp.where(is_live[:, None], back_rows, jnp.zeros((), jnp.bfloat16))
    return (layer_out, grad_read)


STEP = 2
LIMIT = pltpu.CompilerParams(vmem_limit_bytes=16 * 2**20)


def device_of(owner, head):
    return (owner & ~1) | (head & 1), ((owner & 1) << 1) | (head >> 1)


SPANS = (3, 1, 2, 0)


def chunk_of(dp_index, ctx_index, readers):
    return turned(ctx_index) * readers + SPANS[dp_index >> 1] * 2 + (dp_index & 1)


def chunk_back(dp_index, ctx_index, readers):
    return ctx_index * readers + (dp_index & 1) * (readers // 2) + (dp_index >> 1)


def turned(index):
    return ((index & 1) << 1) | (index >> 1)


def vmem(count):
    return [pl.BlockSpec(memory_space=pltpu.VMEM)] * count


def hbm(count):
    return [pl.BlockSpec(memory_space=pltpu.HBM)] * count


def dot(left, right, left_dim, right_dim):
    return lax.dot_general(
        left, right, (((left_dim,), (right_dim,)), ((), ())), preferred_element_type=jnp.float32
    )


def owners_of(users, owner_ref):
    owners = jnp.zeros_like(users)
    for user in range(owner_ref.shape[0]):
        owners = jnp.where(users == user, owner_ref[user], owners)
    return owners


def lower_ones(size):
    earlier = lax.broadcasted_iota(jnp.int32, (size, size), 0)
    later = lax.broadcasted_iota(jnp.int32, (size, size), 1)
    return (earlier <= later).astype(jnp.bfloat16)


def my_place():
    my_dp, my_ctx = lax.axis_index("dp"), lax.axis_index("ctx")
    return ((my_ctx & 1) << 1) | (my_dp & 1), (my_dp & ~1) | (my_ctx >> 1), my_dp, my_ctx


def slot_kernel(
    owner_hbm,
    user_hbm,
    proj_hbm,
    send_hbm,
    slot_hbm,
    owner_ref,
    user_ref,
    slot_ref,
    proj_ref,
    send_ref,
    load_sems,
    store_sems,
    *,
    per_pair,
):
    slots = user_ref.shape[1]
    readers = slots // per_pair
    width = HEADS * HD
    loads = [
        pltpu.make_async_copy(source, target, load_sems.at[index])
        for index, (source, target) in enumerate(
            ((user_hbm, user_ref), (owner_hbm, owner_ref), (proj_hbm, proj_ref))
        )
    ]
    for copy in loads:
        copy.start()
    my_dp = lax.axis_index("dp")
    source = lax.broadcasted_iota(jnp.int32, (slots, slots), 0)
    owner_range = lax.broadcasted_iota(jnp.int32, (readers, slots), 0)
    loads[0].wait()
    loads[1].wait()
    users = user_ref[...]
    owners = owners_of(users, owner_ref)
    is_live = users >= 0
    hits = ((owner_range == owners) & is_live).astype(jnp.float32)
    running = dot(hits.astype(jnp.bfloat16), lower_ones(slots), 1, 0)
    ranks = jnp.sum(hits * running, axis=0, keepdims=True).astype(jnp.int32) - 1
    slot = jnp.where(is_live, owners * per_pair + ranks, -1)
    slot_ref[...] = slot
    stores = [pltpu.make_async_copy(slot_ref, slot_hbm, store_sems.at[HEADS])]
    stores[0].start()
    placed = (source == slot).astype(jnp.bfloat16)
    tagged = (hits * (users + 1).astype(jnp.float32)).astype(jnp.bfloat16)
    to_lane = (source == my_dp * per_pair + ranks).astype(jnp.bfloat16)
    tagged = dot(tagged, to_lane, 1, 1).astype(jnp.bfloat16)
    extra = send_ref.shape[1] - 4 * per_pair
    for owner in range(readers):
        for head in range(HEADS):
            dp_index, ctx_index = device_of(owner, head)
            chunk = chunk_of(dp_index, ctx_index, readers)
            send_ref[chunk, 4 * per_pair :, :] = jnp.broadcast_to(
                tagged[owner : owner + 1], (extra, slots)
            )
    loads[2].wait()
    for half in range(2):
        for part in range(4):
            start = part * width + half * 2 * HD
            rows = dot(placed, proj_ref[:, start : start + 2 * HD], 1, 0).astype(jnp.bfloat16)
            for owner in range(readers):
                for side in range(2):
                    dp_index, ctx_index = device_of(owner, 2 * half + side)
                    chunk = chunk_of(dp_index, ctx_index, readers)
                    send_ref[chunk, part * per_pair : (part + 1) * per_pair, :] = rows[
                        owner * per_pair : (owner + 1) * per_pair, side * HD : (side + 1) * HD
                    ]
        for ctx_index in (half, 2 + half):
            span = pl.ds(turned(ctx_index) * readers, readers)
            stores.append(
                pltpu.make_async_copy(
                    send_ref.at[span], send_hbm.at[span], store_sems.at[ctx_index]
                )
            )
            stores[-1].start()
    for copy in stores:
        copy.wait()


def columns_kernel(slot_ref, grad_ref, *refs):
    piece_refs, back_ref = refs[:HEADS], refs[HEADS]
    slots = slot_ref.shape[1]
    slot = jnp.broadcast_to(slot_ref[...].astype(jnp.float32), (slots, slots)).T
    lane = lax.broadcasted_iota(jnp.int32, (slots, slots), 1).astype(jnp.float32)
    back_ref[...] = (slot == lane).astype(jnp.bfloat16)
    first = turned(lax.axis_index("ctx"))
    for step, piece_ref in enumerate(piece_refs):
        start = pl.multiple_of((first ^ step) * HD, HD)
        piece_ref[...] = grad_ref[:, pl.ds(start, HD)]


def group_kernel(*refs):
    piece_refs, grads_ref = refs[:HEADS], refs[HEADS]
    head = my_place()[0]
    for step, piece_ref in enumerate(piece_refs):
        slots = piece_ref.shape[0]
        start = pl.multiple_of(turned(head ^ step) * slots, slots)
        grads_ref[pl.ds(start, slots), :] = piece_ref[...]


def part_rows(rows_ref, part, first, last):
    readers = rows_ref.shape[0] // HEADS
    per_pair = HD // readers
    span = slice(part * per_pair, (part + 1) * per_pair)
    rows = [
        rows_ref[chunk_of(reader, window, readers), span, :]
        for window in range(first, last)
        for reader in range(readers)
    ]
    return jnp.concatenate(rows, axis=0)


def put_rows(out_ref, part, first, last, rows, readers):
    per_pair = HD // readers
    for window in range(first, last):
        for reader in range(readers):
            source = ((window - first) * readers + reader) * per_pair
            target = chunk_back(reader, window, readers) * per_pair
            out_ref[target : target + per_pair, part * HD : (part + 1) * HD] = rows[
                source : source + per_pair
            ].astype(jnp.bfloat16)


def window_users(rows_ref, window):
    readers = rows_ref.shape[0] // HEADS
    per_pair = HD // readers
    first = turned(window) * readers
    tags = rows_ref[first : first + readers, 4 * per_pair :, :]
    return jnp.sum(tags.astype(jnp.float32), axis=0)[:1]


def visible_block(users, first, last):
    size = HD
    query_users = [jnp.broadcast_to(users[window], (size, size)).T for window in range(first, last)]
    query_users = jnp.concatenate(query_users, axis=0)
    rows = lax.broadcasted_iota(jnp.int32, query_users.shape, 0)
    columns = lax.broadcasted_iota(jnp.int32, query_users.shape, 1)
    blocks = []
    for window in range(last):
        block = (query_users == users[window]) & (query_users > 0.0)
        if window >= first:
            block = block & (columns + (window - first) * size <= rows)
        blocks.append(block)
    return jnp.concatenate(blocks, axis=1)


def forward_kernel(rows_ref, grads_ref, gain_ref, attended_ref, stats_ref):
    size = HD
    scale = HD ** (-0.5)
    users = [window_users(rows_ref, window) for window in range(HEADS)]
    for first in range(0, HEADS, STEP):
        last = first + STEP
        queries = part_rows(rows_ref, 1, first, last)
        scores = dot(queries, part_rows(rows_ref, 2, 0, last), 1, 1) * scale
        visible = visible_block(users, first, last)
        weights = jnp.where(visible, scores * jax.nn.sigmoid(scores), 0.0).astype(jnp.bfloat16)
        block = dot(weights, part_rows(rows_ref, 3, 0, last), 1, 0)
        attended_ref[first * size : last * size] = block
        for window in range(first, last):
            here = slice(window * size, (window + 1) * size)
            attended = block[(window - first) * size : (window - first + 1) * size]
            grad_normed = (
                grads_ref[here].astype(jnp.float32)
                * gain_ref[...]
                * part_rows(rows_ref, 0, window, window + 1).astype(jnp.float32)
            )
            turned_att = attended.T
            turned_grad = grad_normed.T
            mean = jnp.mean(turned_att, axis=0, keepdims=True)
            centered = turned_att - mean
            spread = jnp.sum(centered * centered, axis=0, keepdims=True)
            grad_sum = jnp.sum(turned_grad, axis=0, keepdims=True)
            cross = jnp.sum(turned_grad * centered, axis=0, keepdims=True)
            stats_ref[0:1, here] = mean
            stats_ref[1:2, here] = spread
            stats_ref[2:3, here] = grad_sum
            stats_ref[3:4, here] = cross
            stats_ref[4:8, here] = jnp.zeros((4, size), jnp.float32)


def slope_kernel(rows_ref, slopes_ref, turned_slopes_ref, turned_weights_ref):
    size = HD
    scale = HD ** (-0.5)
    users = [window_users(rows_ref, window) for window in range(HEADS)]
    for first in range(0, HEADS, STEP):
        last = first + STEP
        queries = part_rows(rows_ref, 1, first, last)
        scores = dot(queries, part_rows(rows_ref, 2, 0, last), 1, 1) * scale
        sigmoid = jax.nn.sigmoid(scores)
        slopes = sigmoid * (1.0 + scores * (1.0 - sigmoid)) * scale
        visible = visible_block(users, first, last)
        slopes = jnp.where(visible, slopes, 0.0)
        weights = jnp.where(visible, scores * sigmoid, 0.0)
        slopes_ref[first * size : last * size, : last * size] = slopes
        turned_slopes_ref[: last * size, first * size : last * size] = slopes.T
        turned_weights_ref[: last * size, first * size : last * size] = weights.T.astype(
            jnp.bfloat16
        )


def backward_kernel(
    rows_ref,
    grads_ref,
    gain_ref,
    attended_ref,
    slopes_ref,
    turned_slopes_ref,
    turned_weights_ref,
    *refs,
):
    stats_refs = refs[:HEADS]
    out_hbm = refs[HEADS]
    layer_refs = refs[HEADS + 1 : 2 * HEADS + 1]
    layer_all, out_ref, store_sems = refs[2 * HEADS + 1 :]
    head = my_place()[0]
    readers = rows_ref.shape[0] // HEADS
    size = HD
    width = float(HEADS * HD)
    stats = [stat_ref[...] for stat_ref in stats_refs]
    mean = sum(stat[0:1] for stat in stats) * (1.0 / HEADS)
    spread = sum(stat[1:2] + HD * (stat[0:1] - mean) * (stat[0:1] - mean) for stat in stats)
    inv_std = lax.rsqrt(spread / width + epsilon)
    mean_grad = sum(stat[2:3] for stat in stats) / width
    cross = sum(stat[3:4] + (stat[0:1] - mean) * stat[2:3] for stat in stats)
    mean_cross = cross * inv_std / width
    row = lax.broadcasted_iota(jnp.int32, (size, size), 0)
    out_grads = []
    for window in range(HEADS):
        here = slice(window * size, (window + 1) * size)
        packed = jnp.where(
            row == 0,
            mean[:, here],
            jnp.where(
                row == 1,
                inv_std[:, here],
                jnp.where(row == 2, mean_grad[:, here], mean_cross[:, here]),
            ),
        ).T
        unit = part_rows(rows_ref, 0, window, window + 1).astype(jnp.float32)
        grad_gain = grads_ref[here].astype(jnp.float32) * gain_ref[...]
        normed = (attended_ref[here] - packed[:, 0:1]) * packed[:, 1:2]
        layer_all[here] = (normed * gain_ref[...] * unit).astype(jnp.bfloat16)
        put_rows(out_ref, 0, window, window + 1, grad_gain * normed, readers)
        out_grads.append(
            packed[:, 1:2] * (grad_gain * unit - packed[:, 2:3] - normed * packed[:, 3:4])
        )
    out_grads = jnp.concatenate(out_grads, axis=0).astype(jnp.bfloat16)
    stores = []
    for first in range(0, HEADS, STEP):
        last = first + STEP
        here = slice(first * size, last * size)
        upto = slice(0, last * size)
        after = slice(first * size, HEADS * size)
        score_grads = (
            dot(out_grads[here], part_rows(rows_ref, 3, 0, last), 1, 1) * slopes_ref[here, upto]
        ).astype(jnp.bfloat16)
        query_grads = dot(score_grads, part_rows(rows_ref, 2, 0, last), 1, 0)
        put_rows(out_ref, 1, first, last, query_grads, readers)
        turned_grads = (
            dot(part_rows(rows_ref, 3, first, last), out_grads[after], 1, 1)
            * turned_slopes_ref[here, after]
        ).astype(jnp.bfloat16)
        key_grads = dot(turned_grads, part_rows(rows_ref, 1, first, HEADS), 1, 0)
        put_rows(out_ref, 2, first, last, key_grads, readers)
        value_grads = dot(turned_weights_ref[here, after], out_grads[after], 1, 0)
        put_rows(out_ref, 3, first, last, value_grads, readers)
        for window in range(first, last):
            span = pl.ds(window * size, size)
            stores.append(
                pltpu.make_async_copy(out_ref.at[span], out_hbm.at[span], store_sems.at[window])
            )
            stores[-1].start()
    for step, layer_ref in enumerate(layer_refs):
        start = pl.multiple_of(turned(head ^ step) * size, size)
        layer_ref[...] = layer_all[pl.ds(start, size), :]
    for copy in stores:
        copy.wait()


def unslot_kernel(back_ref, returned_ref, *refs, per_pair):
    piece_refs = refs[:HEADS]
    layer_hbm, grad_hbm, layer_ref, grad_ref, store_sems = refs[HEADS:]
    slots = back_ref.shape[0]
    readers = slots // per_pair
    width = HEADS * HD
    first = turned(lax.axis_index("ctx"))
    for step, piece_ref in enumerate(piece_refs):
        start = pl.multiple_of((first ^ step) * HD, HD)
        layer_ref[:, pl.ds(start, HD)] = piece_ref[...]
    stores = [pltpu.make_async_copy(layer_ref, layer_hbm, store_sems.at[2])]
    stores[0].start()
    heads = []
    for head in range(HEADS):
        chunks = []
        for owner in range(readers):
            dp_index, ctx_index = device_of(owner, head)
            start = chunk_back(dp_index, ctx_index, readers) * per_pair
            chunks.append(returned_ref[start : start + per_pair])
        heads.append(jnp.concatenate(chunks, axis=0))
    half = slots // 2
    for side in range(2):
        span = pl.ds(side * half, half)
        here = slice(side * half, (side + 1) * half)
        for head in range(HEADS):
            rows = dot(back_ref[here], heads[head], 1, 0).astype(jnp.bfloat16)
            for part in range(4):
                start = part * width + head * HD
                grad_ref[here, start : start + HD] = rows[:, part * HD : (part + 1) * HD]
        stores.append(
            pltpu.make_async_copy(grad_ref.at[span], grad_hbm.at[span], store_sems.at[side])
        )
        stores[-1].start()
    for copy in stores:
        copy.wait()


def send(value, target, back=False):
    width = lax.axis_size("ctx")
    pairs = []
    for dp_index in range(lax.axis_size("dp")):
        for ctx_index in range(width):
            to_dp, to_ctx = target(dp_index, ctx_index)
            pair = (dp_index * width + ctx_index, to_dp * width + to_ctx)
            pairs.append(pair[::-1] if back else pair)
    return lax.ppermute(value, ("dp", "ctx"), pairs)


def exchange(chunks, place):
    readers, width = lax.axis_size("dp"), lax.axis_size("ctx")
    order = [None] * (readers * width)
    for dp_index in range(readers):
        for ctx_index in range(width):
            order[place(dp_index, ctx_index, readers)] = dp_index * width + ctx_index
    return lax.all_to_all(
        chunks, ("dp", "ctx"), split_axis=0, concat_axis=0, tiled=True, axis_index_groups=[order]
    )


def swap(value, dp_bits, ctx_bits):
    return send(value, lambda dp_index, ctx_index: (dp_index ^ dp_bits, ctx_index ^ ctx_bits))


def regroup(pieces, back=False):
    moved = []
    for step, piece in enumerate(pieces):

        def target(dp_index, ctx_index, step=step):
            return device_of(dp_index, turned(ctx_index) ^ step)

        moved.append(send(piece, target, back))
    return moved


def by_heads(proj_read, norm_gain, owner_of, user_of, grad_output):
    slots = proj_read.shape[0]
    readers = lax.axis_size("dp")
    per_pair = slots // readers
    group_rows = slots * HEADS
    width = 4 * HD
    gain = lax.dynamic_slice_in_dim(norm_gain, my_place()[0] * HD, HD, 0).reshape(1, HD)
    piece_shape = jax.ShapeDtypeStruct((slots, HD), jnp.bfloat16)
    chunk_shape = (HEADS * readers, 4 * per_pair + 8, HD)
    outgoing, slot = pl.pallas_call(
        functools.partial(slot_kernel, per_pair=per_pair),
        out_shape=(
            jax.ShapeDtypeStruct(chunk_shape, jnp.bfloat16),
            jax.ShapeDtypeStruct((1, slots), jnp.int32),
        ),
        in_specs=hbm(3),
        out_specs=tuple(hbm(2)),
        scratch_shapes=[
            pltpu.SMEM(owner_of.shape, jnp.int32),
            pltpu.VMEM((1, slots), jnp.int32),
            pltpu.VMEM((1, slots), jnp.int32),
            pltpu.VMEM(proj_read.shape, jnp.bfloat16),
            pltpu.VMEM(chunk_shape, jnp.bfloat16),
            pltpu.SemaphoreType.DMA((3,)),
            pltpu.SemaphoreType.DMA((HEADS + 1,)),
        ],
        name="slot_rows",
    )(owner_of, user_of.reshape(1, slots), proj_read)
    rows = exchange(outgoing, chunk_of)
    *pieces, back = pl.pallas_call(
        columns_kernel,
        out_shape=(piece_shape,) * HEADS + (jax.ShapeDtypeStruct((slots, slots), jnp.bfloat16),),
        in_specs=vmem(2),
        out_specs=tuple(vmem(HEADS + 1)),
        compiler_params=LIMIT,
        name="cut_columns",
    )(slot, grad_output)
    grads = pl.pallas_call(
        group_kernel,
        out_shape=jax.ShapeDtypeStruct((group_rows, HD), jnp.bfloat16),
        in_specs=vmem(HEADS),
        out_specs=vmem(1)[0],
        compiler_params=LIMIT,
        name="lay_group",
    )(*regroup(pieces))
    attended, stats = pl.pallas_call(
        forward_kernel,
        out_shape=(
            jax.ShapeDtypeStruct((group_rows, HD), jnp.float32),
            jax.ShapeDtypeStruct((8, group_rows), jnp.float32),
        ),
        in_specs=vmem(3),
        out_specs=tuple(vmem(2)),
        compiler_params=LIMIT,
        name="forward",
    )(rows, grads, gain)
    late_rows, stats = lax.optimization_barrier((rows, stats))
    slopes = pl.pallas_call(
        slope_kernel,
        out_shape=(
            jax.ShapeDtypeStruct((group_rows, group_rows), jnp.float32),
            jax.ShapeDtypeStruct((group_rows, group_rows), jnp.float32),
            jax.ShapeDtypeStruct((group_rows, group_rows), jnp.bfloat16),
        ),
        in_specs=vmem(1),
        out_specs=tuple(vmem(3)),
        compiler_params=LIMIT,
        name="slopes",
    )(late_rows)
    all_stats = [stats, swap(stats, 1, 0), swap(stats, 0, 1), swap(stats, 1, 1)]
    results = pl.pallas_call(
        backward_kernel,
        out_shape=(jax.ShapeDtypeStruct((group_rows, width), jnp.bfloat16),)
        + (piece_shape,) * HEADS,
        in_specs=vmem(7 + HEADS),
        out_specs=tuple(hbm(1) + vmem(HEADS)),
        scratch_shapes=[
            pltpu.VMEM((group_rows, HD), jnp.bfloat16),
            pltpu.VMEM((group_rows, width), jnp.bfloat16),
            pltpu.SemaphoreType.DMA((HEADS,)),
        ],
        compiler_params=LIMIT,
        name="backward",
    )(rows, grads, gain, attended, *slopes, *all_stats)
    returned = exchange(results[0], chunk_back)
    layer_shape, grad_shape = (slots, HEADS * HD), (slots, 4 * HEADS * HD)
    return pl.pallas_call(
        functools.partial(unslot_kernel, per_pair=per_pair),
        out_shape=(
            jax.ShapeDtypeStruct(layer_shape, jnp.bfloat16),
            jax.ShapeDtypeStruct(grad_shape, jnp.bfloat16),
        ),
        in_specs=vmem(2 + HEADS),
        out_specs=tuple(hbm(2)),
        scratch_shapes=[
            pltpu.VMEM(layer_shape, jnp.bfloat16),
            pltpu.VMEM(grad_shape, jnp.bfloat16),
            pltpu.SemaphoreType.DMA((3,)),
        ],
        compiler_params=LIMIT,
        name="unslot_rows",
    )(back, returned, *regroup(results[1:], back=True))


def solution(mesh):
    in_specs = (P(("dp", "ctx"), None), P(), P(), P(("dp", "ctx")), P(("dp", "ctx"), None))
    out_specs = (P(("dp", "ctx"), None), P(("dp", "ctx"), None))
    fits = mesh.shape["ctx"] == HEADS and mesh.shape["dp"] == 2 * len(SPANS)
    local = by_heads if fits else windowed
    return jax.shard_map(local, mesh=mesh, in_specs=in_specs, out_specs=out_specs, check_vma=False)
```

```python
import functools

import jax
import jax.numpy as jnp
from jax import lax
from jax.experimental import pallas as pl
from jax.experimental.pallas import tpu as pltpu
from jax.sharding import PartitionSpec as P

HEADS = 4
HD = 128


epsilon = 1e-05


def block_length(total_rows, shard_rows):
    shard_total = total_rows // shard_rows
    best_factor = 1
    for factor in range(1, shard_total + 1):
        if shard_total % factor == 0 and factor * shard_rows <= 1024:
            best_factor = factor
    return best_factor * shard_rows


def silu_slope(scores):
    sigmoid_part = jax.nn.sigmoid(scores)
    return sigmoid_part * (1.0 + scores * (1.0 - sigmoid_part))


def visible_pairs(query_users, query_places, key_users, key_places):
    same_user = (query_users[:, None] == key_users[None, :]) & (query_users[:, None] >= 0)
    return same_user & (key_places[None, :] <= query_places[:, None])


def run_blocks(carry_now, shard_piece, block_rows, step_fn):
    total_rows = shard_piece[0].shape[0]

    def one_block(block_index, carry_here):
        offset = block_index * block_rows
        block_part = tuple(
            (
                lax.dynamic_slice_in_dim(array_item, offset, block_rows, 0)
                for array_item in shard_piece
            )
        )
        return step_fn(carry_here, block_part, offset)

    return lax.fori_loop(0, total_rows // block_rows, one_block, carry_now)


def windowed(proj_read, norm_gain, owner_of, user_of, grad_output):
    slot_rows = proj_read.shape[0]
    reader_peers = lax.axis_size("dp")
    per_pair = slot_rows // reader_peers
    feature_width = HEADS * HD
    score_scale = HD ** (-0.5)
    group_rows = slot_rows * lax.axis_size("ctx")
    user_range = jnp.arange(owner_of.shape[0], dtype=jnp.int32)
    owners = jnp.sum(
        jnp.where(user_of[:, None] == user_range[None, :], owner_of[None, :], 0), axis=1
    )
    is_live = user_of >= 0
    owner_hits = (owners[:, None] == jnp.arange(reader_peers, dtype=jnp.int32)[None, :]) & is_live[
        :, None
    ]
    running = jnp.cumsum(owner_hits.astype(jnp.int32), axis=0) - 1
    ranks_mine = jnp.sum(jnp.where(owner_hits, running, 0), axis=1)
    send_slot = jnp.where(is_live, owners * per_pair + ranks_mine, -1)
    slot_range = jnp.arange(slot_rows, dtype=jnp.int32)
    slot_match = send_slot[None, :] == slot_range[:, None]
    filled = jnp.any(slot_match, axis=1)
    source_row = jnp.sum(jnp.where(slot_match, slot_range[None, :], 0), axis=1)
    outgoing = jnp.where(
        filled[:, None], jnp.take(proj_read, source_row, axis=0), jnp.zeros((), jnp.bfloat16)
    )
    outgoing_users = jnp.where(filled, jnp.take(user_of, source_row), -1)
    arrived, arrived_users = (
        lax.all_to_all(outgoing, "dp", split_axis=0, concat_axis=0, tiled=True),
        lax.all_to_all(outgoing_users, "dp", split_axis=0, concat_axis=0, tiled=True),
    )
    own_start = lax.axis_index("ctx") * slot_rows
    own_places = own_start + slot_range
    unit_rows = arrived[:, :feature_width]
    queries = arrived[:, feature_width : 2 * feature_width]
    key_values = arrived[:, 2 * feature_width :]
    query_heads = queries.reshape(slot_rows, HEADS, HD)
    key_heads = key_values[:, :feature_width].reshape(slot_rows, HEADS, HD)
    value_heads = key_values[:, feature_width:].reshape(slot_rows, HEADS, HD)

    def forward_step(total_out, block_part, first_row):
        block_kv, block_users = block_part
        block_size = block_kv.shape[0]
        remote_keys = block_kv[:, :feature_width].reshape(block_size, HEADS, HD)
        remote_values = block_kv[:, feature_width:].reshape(block_size, HEADS, HD)
        scores = (
            jnp.einsum("qhd,khd->hqk", query_heads, remote_keys, preferred_element_type=jnp.float32)
            * score_scale
        )
        visible = visible_pairs(
            arrived_users,
            own_places,
            block_users,
            first_row + jnp.arange(block_size, dtype=jnp.int32),
        )
        weights = jnp.where(visible[None], jax.nn.silu(scores), 0.0).astype(jnp.bfloat16)
        summed = jnp.einsum(
            "hqk,khd->qhd", weights, remote_values, preferred_element_type=jnp.float32
        )
        return total_out + summed.reshape(slot_rows, feature_width)

    zero_rows = jnp.zeros((slot_rows, feature_width), jnp.float32)
    shard_piece = (
        lax.all_gather(key_values, "ctx", axis=0, tiled=True),
        lax.all_gather(arrived_users, "ctx", axis=0, tiled=True),
    )
    block_rows = block_length(shard_piece[0].shape[0], slot_rows)
    forward_result = run_blocks(zero_rows, shard_piece, block_rows, forward_step)
    mean_out = jnp.mean(forward_result, axis=1, keepdims=True)
    centered = forward_result - mean_out
    inv_std = lax.rsqrt(jnp.mean(centered * centered, axis=1, keepdims=True) + epsilon)
    normed = centered * inv_std
    unit_float = unit_rows.astype(jnp.float32)
    layer_out = (normed * norm_gain * unit_float).astype(jnp.bfloat16)
    grad_float = grad_output.astype(jnp.float32)
    unit_grads = (grad_float * norm_gain * normed).astype(jnp.bfloat16)
    grad_normed = grad_float * norm_gain * unit_float
    mean_grad = jnp.mean(grad_normed, axis=1, keepdims=True)
    mean_cross = jnp.mean(grad_normed * normed, axis=1, keepdims=True)
    out_grads = (inv_std * (grad_normed - mean_grad - normed * mean_cross)).astype(jnp.bfloat16)

    def backward_step(carry_here, block_part, first_row):
        block_queries, block_grads, block_users = block_part
        block_size = block_queries.shape[0]
        remote_queries = block_queries.reshape(block_size, HEADS, HD)
        remote_grads = block_grads.reshape(block_size, HEADS, HD)
        scores = (
            jnp.einsum(
                "qhd,khd->hqk", remote_queries, key_heads, preferred_element_type=jnp.float32
            )
            * score_scale
        )
        visible = visible_pairs(
            block_users,
            first_row + jnp.arange(block_size, dtype=jnp.int32),
            arrived_users,
            own_places,
        )[None]
        weights = jnp.where(visible, jax.nn.silu(scores), 0.0).astype(jnp.bfloat16)
        weight_grads = jnp.einsum(
            "qhd,khd->hqk", remote_grads, value_heads, preferred_element_type=jnp.float32
        )
        score_grads = jnp.where(
            visible, weight_grads * silu_slope(scores) * score_scale, 0.0
        ).astype(jnp.bfloat16)
        value_sum = jnp.einsum(
            "hqk,qhd->khd", weights, remote_grads, preferred_element_type=jnp.float32
        ).reshape(slot_rows, feature_width)
        key_sum = jnp.einsum(
            "hqk,qhd->khd", score_grads, remote_queries, preferred_element_type=jnp.float32
        ).reshape(slot_rows, feature_width)
        new_keys = carry_here[0] + key_sum
        new_values = carry_here[1] + value_sum
        window_sum = (
            jnp.einsum("hqk,khd->qhd", score_grads, key_heads, preferred_element_type=jnp.float32)
            .reshape(block_size, feature_width)
            .astype(jnp.bfloat16)
        )
        return (
            new_keys,
            new_values,
            lax.dynamic_update_slice_in_dim(carry_here[2], window_sum, first_row, 0),
        )

    start_carry = (zero_rows, zero_rows, jnp.zeros((group_rows, feature_width), jnp.bfloat16))
    shard_piece = (
        lax.all_gather(queries, "ctx", axis=0, tiled=True),
        lax.all_gather(out_grads, "ctx", axis=0, tiled=True),
        lax.all_gather(arrived_users, "ctx", axis=0, tiled=True),
    )
    block_rows = block_length(shard_piece[0].shape[0], slot_rows)
    key_results = run_blocks(start_carry, shard_piece, block_rows, backward_step)
    key_grads = key_results[0]
    value_grads = key_results[1]
    query_grads = lax.psum_scatter(key_results[2], "ctx", scatter_dimension=0, tiled=True).astype(
        jnp.float32
    )
    grads_owned = jnp.concatenate(
        [
            unit_grads,
            query_grads.astype(jnp.bfloat16),
            key_grads.astype(jnp.bfloat16),
            value_grads.astype(jnp.bfloat16),
        ],
        axis=1,
    )
    returned = lax.all_to_all(grads_owned, "dp", split_axis=0, concat_axis=0, tiled=True)
    back_rows = jnp.take(returned, jnp.maximum(send_slot, 0), axis=0)
    grad_read = jnp.where(is_live[:, None], back_rows, jnp.zeros((), jnp.bfloat16))
    return (layer_out, grad_read)


STEP = 2
LIMIT = pltpu.CompilerParams(vmem_limit_bytes=16 * 2**20)


def device_of(owner, head):
    return (owner & ~1) | (head & 1), ((owner & 1) << 1) | (head >> 1)


SPANS = (3, 1, 2, 0)


def chunk_of(dp_index, ctx_index, readers):
    return turned(ctx_index) * readers + SPANS[dp_index >> 1] * 2 + (dp_index & 1)


def chunk_back(dp_index, ctx_index, readers):
    return ctx_index * readers + (dp_index & 1) * (readers // 2) + (dp_index >> 1)


def turned(index):
    return ((index & 1) << 1) | (index >> 1)


def vmem(count):
    return [pl.BlockSpec(memory_space=pltpu.VMEM)] * count


def hbm(count):
    return [pl.BlockSpec(memory_space=pltpu.HBM)] * count


def dot(left, right, left_dim, right_dim):
    return lax.dot_general(
        left, right, (((left_dim,), (right_dim,)), ((), ())), preferred_element_type=jnp.float32
    )


def owners_of(users, owner_ref):
    owners = jnp.zeros_like(users)
    for user in range(owner_ref.shape[0]):
        owners = jnp.where(users == user, owner_ref[user], owners)
    return owners


def lower_ones(size):
    earlier = lax.broadcasted_iota(jnp.int32, (size, size), 0)
    later = lax.broadcasted_iota(jnp.int32, (size, size), 1)
    return (earlier <= later).astype(jnp.bfloat16)


def my_place():
    my_dp, my_ctx = lax.axis_index("dp"), lax.axis_index("ctx")
    return ((my_ctx & 1) << 1) | (my_dp & 1), (my_dp & ~1) | (my_ctx >> 1), my_dp, my_ctx


def slot_kernel(
    owner_hbm,
    user_hbm,
    proj_hbm,
    send_hbm,
    slot_hbm,
    owner_ref,
    user_ref,
    slot_ref,
    proj_ref,
    send_ref,
    load_sems,
    store_sems,
    *,
    per_pair,
):
    slots = user_ref.shape[1]
    readers = slots // per_pair
    width = HEADS * HD
    loads = [
        pltpu.make_async_copy(source, target, load_sems.at[index])
        for index, (source, target) in enumerate(
            ((user_hbm, user_ref), (owner_hbm, owner_ref), (proj_hbm, proj_ref))
        )
    ]
    for copy in loads:
        copy.start()
    my_dp = lax.axis_index("dp")
    source = lax.broadcasted_iota(jnp.int32, (slots, slots), 0)
    owner_range = lax.broadcasted_iota(jnp.int32, (readers, slots), 0)
    loads[0].wait()
    loads[1].wait()
    users = user_ref[...]
    owners = owners_of(users, owner_ref)
    is_live = users >= 0
    hits = ((owner_range == owners) & is_live).astype(jnp.float32)
    running = dot(hits.astype(jnp.bfloat16), lower_ones(slots), 1, 0)
    ranks = jnp.sum(hits * running, axis=0, keepdims=True).astype(jnp.int32) - 1
    slot = jnp.where(is_live, owners * per_pair + ranks, -1)
    slot_ref[...] = slot
    stores = [pltpu.make_async_copy(slot_ref, slot_hbm, store_sems.at[HEADS])]
    stores[0].start()
    placed = (source == slot).astype(jnp.bfloat16)
    tagged = (hits * (users + 1).astype(jnp.float32)).astype(jnp.bfloat16)
    to_lane = (source == my_dp * per_pair + ranks).astype(jnp.bfloat16)
    tagged = dot(tagged, to_lane, 1, 1).astype(jnp.bfloat16)
    extra = send_ref.shape[1] - 4 * per_pair
    for owner in range(readers):
        for head in range(HEADS):
            dp_index, ctx_index = device_of(owner, head)
            chunk = chunk_of(dp_index, ctx_index, readers)
            send_ref[chunk, 4 * per_pair :, :] = jnp.broadcast_to(
                tagged[owner : owner + 1], (extra, slots)
            )
    loads[2].wait()
    for half in range(2):
        for part in range(4):
            start = part * width + half * 2 * HD
            rows = dot(placed, proj_ref[:, start : start + 2 * HD], 1, 0).astype(jnp.bfloat16)
            for owner in range(readers):
                for side in range(2):
                    dp_index, ctx_index = device_of(owner, 2 * half + side)
                    chunk = chunk_of(dp_index, ctx_index, readers)
                    send_ref[chunk, part * per_pair : (part + 1) * per_pair, :] = rows[
                        owner * per_pair : (owner + 1) * per_pair, side * HD : (side + 1) * HD
                    ]
        for ctx_index in (half, 2 + half):
            span = pl.ds(turned(ctx_index) * readers, readers)
            stores.append(
                pltpu.make_async_copy(
                    send_ref.at[span], send_hbm.at[span], store_sems.at[ctx_index]
                )
            )
            stores[-1].start()
    for copy in stores:
        copy.wait()


def columns_kernel(slot_ref, grad_ref, *refs):
    piece_refs, back_ref = refs[:HEADS], refs[HEADS]
    slots = slot_ref.shape[1]
    slot = jnp.broadcast_to(slot_ref[...].astype(jnp.float32), (slots, slots)).T
    lane = lax.broadcasted_iota(jnp.int32, (slots, slots), 1).astype(jnp.float32)
    back_ref[...] = (slot == lane).astype(jnp.bfloat16)
    first = turned(lax.axis_index("ctx"))
    for step, piece_ref in enumerate(piece_refs):
        start = pl.multiple_of((first ^ step) * HD, HD)
        piece_ref[...] = grad_ref[:, pl.ds(start, HD)]


def group_kernel(*refs):
    piece_refs, grads_ref = refs[:HEADS], refs[HEADS]
    head = my_place()[0]
    for step, piece_ref in enumerate(piece_refs):
        slots = piece_ref.shape[0]
        start = pl.multiple_of(turned(head ^ step) * slots, slots)
        grads_ref[pl.ds(start, slots), :] = piece_ref[...]


def part_rows(rows_ref, part, first, last):
    readers = rows_ref.shape[0] // HEADS
    per_pair = HD // readers
    span = slice(part * per_pair, (part + 1) * per_pair)
    rows = [
        rows_ref[chunk_of(reader, window, readers), span, :]
        for window in range(first, last)
        for reader in range(readers)
    ]
    return jnp.concatenate(rows, axis=0)


def put_rows(out_ref, part, first, last, rows, readers):
    per_pair = HD // readers
    for window in range(first, last):
        for reader in range(readers):
            source = ((window - first) * readers + reader) * per_pair
            target = chunk_back(reader, window, readers) * per_pair
            out_ref[target : target + per_pair, part * HD : (part + 1) * HD] = rows[
                source : source + per_pair
            ].astype(jnp.bfloat16)


def window_users(rows_ref, window):
    readers = rows_ref.shape[0] // HEADS
    per_pair = HD // readers
    first = turned(window) * readers
    tags = rows_ref[first : first + readers, 4 * per_pair :, :]
    return jnp.sum(tags.astype(jnp.float32), axis=0)[:1]


def visible_block(users, first, last):
    size = HD
    query_users = [jnp.broadcast_to(users[window], (size, size)).T for window in range(first, last)]
    query_users = jnp.concatenate(query_users, axis=0)
    rows = lax.broadcasted_iota(jnp.int32, query_users.shape, 0)
    columns = lax.broadcasted_iota(jnp.int32, query_users.shape, 1)
    blocks = []
    for window in range(last):
        block = (query_users == users[window]) & (query_users > 0.0)
        if window >= first:
            block = block & (columns + (window - first) * size <= rows)
        blocks.append(block)
    return jnp.concatenate(blocks, axis=1)


def forward_kernel(rows_ref, grads_ref, gain_ref, attended_ref, stats_ref):
    size = HD
    scale = HD ** (-0.5)
    users = [window_users(rows_ref, window) for window in range(HEADS)]
    for first in range(0, HEADS, STEP):
        last = first + STEP
        queries = part_rows(rows_ref, 1, first, last)
        scores = dot(queries, part_rows(rows_ref, 2, 0, last), 1, 1) * scale
        visible = visible_block(users, first, last)
        weights = jnp.where(visible, scores * jax.nn.sigmoid(scores), 0.0).astype(jnp.bfloat16)
        block = dot(weights, part_rows(rows_ref, 3, 0, last), 1, 0)
        attended_ref[first * size : last * size] = block
        for window in range(first, last):
            here = slice(window * size, (window + 1) * size)
            attended = block[(window - first) * size : (window - first + 1) * size]
            grad_normed = (
                grads_ref[here].astype(jnp.float32)
                * gain_ref[...]
                * part_rows(rows_ref, 0, window, window + 1).astype(jnp.float32)
            )
            turned_att = attended.T
            turned_grad = grad_normed.T
            mean = jnp.mean(turned_att, axis=0, keepdims=True)
            centered = turned_att - mean
            spread = jnp.sum(centered * centered, axis=0, keepdims=True)
            grad_sum = jnp.sum(turned_grad, axis=0, keepdims=True)
            cross = jnp.sum(turned_grad * centered, axis=0, keepdims=True)
            stats_ref[0:1, here] = mean
            stats_ref[1:2, here] = spread
            stats_ref[2:3, here] = grad_sum
            stats_ref[3:4, here] = cross


def slope_kernel(rows_ref, slopes_ref, turned_slopes_ref, turned_weights_ref):
    size = HD
    scale = HD ** (-0.5)
    users = [window_users(rows_ref, window) for window in range(HEADS)]
    for first in range(0, HEADS, STEP):
        last = first + STEP
        queries = part_rows(rows_ref, 1, first, last)
        scores = dot(queries, part_rows(rows_ref, 2, 0, last), 1, 1) * scale
        sigmoid = jax.nn.sigmoid(scores)
        slopes = sigmoid * (1.0 + scores * (1.0 - sigmoid)) * scale
        visible = visible_block(users, first, last)
        slopes = jnp.where(visible, slopes, 0.0)
        weights = jnp.where(visible, scores * sigmoid, 0.0)
        slopes_ref[first * size : last * size, : last * size] = slopes
        turned_slopes_ref[: last * size, first * size : last * size] = slopes.T
        turned_weights_ref[: last * size, first * size : last * size] = weights.T.astype(
            jnp.bfloat16
        )


def backward_kernel(
    rows_ref,
    grads_ref,
    gain_ref,
    attended_ref,
    slopes_ref,
    turned_slopes_ref,
    turned_weights_ref,
    *refs,
):
    stats_refs = refs[:HEADS]
    out_hbm = refs[HEADS]
    layer_refs = refs[HEADS + 1 : 2 * HEADS + 1]
    layer_all, out_ref, store_sems = refs[2 * HEADS + 1 :]
    head = my_place()[0]
    readers = rows_ref.shape[0] // HEADS
    size = HD
    width = float(HEADS * HD)
    stats = [stat_ref[...] for stat_ref in stats_refs]
    mean = sum(stat[0:1] for stat in stats) * (1.0 / HEADS)
    spread = sum(stat[1:2] + HD * (stat[0:1] - mean) * (stat[0:1] - mean) for stat in stats)
    inv_std = lax.rsqrt(spread / width + epsilon)
    mean_grad = sum(stat[2:3] for stat in stats) / width
    cross = sum(stat[3:4] + (stat[0:1] - mean) * stat[2:3] for stat in stats)
    mean_cross = cross * inv_std / width
    packed = [
        stat[:, window * size : (window + 1) * size]
        for window in range(HEADS)
        for stat in (mean, inv_std, mean_grad, mean_cross)
    ]
    packed.append(jnp.zeros((size - len(packed), size), jnp.float32))
    packed = jnp.concatenate(packed, axis=0).T
    out_grads = []
    for window in range(HEADS):
        here = slice(window * size, (window + 1) * size)
        row_mean, row_inv, row_grad, row_cross = [
            packed[:, 4 * window + index : 4 * window + index + 1] for index in range(4)
        ]
        unit = part_rows(rows_ref, 0, window, window + 1).astype(jnp.float32)
        grad_gain = grads_ref[here].astype(jnp.float32) * gain_ref[...]
        normed = (attended_ref[here] - row_mean) * row_inv
        layer_all[here] = (normed * gain_ref[...] * unit).astype(jnp.bfloat16)
        put_rows(out_ref, 0, window, window + 1, grad_gain * normed, readers)
        out_grads.append(row_inv * (grad_gain * unit - row_grad - normed * row_cross))
    out_grads = jnp.concatenate(out_grads, axis=0).astype(jnp.bfloat16)
    stores = []
    for first in range(0, HEADS, STEP):
        last = first + STEP
        here = slice(first * size, last * size)
        upto = slice(0, last * size)
        after = slice(first * size, HEADS * size)
        score_grads = (
            dot(out_grads[here], part_rows(rows_ref, 3, 0, last), 1, 1) * slopes_ref[here, upto]
        ).astype(jnp.bfloat16)
        query_grads = dot(score_grads, part_rows(rows_ref, 2, 0, last), 1, 0)
        put_rows(out_ref, 1, first, last, query_grads, readers)
        turned_grads = (
            dot(part_rows(rows_ref, 3, first, last), out_grads[after], 1, 1)
            * turned_slopes_ref[here, after]
        ).astype(jnp.bfloat16)
        key_grads = dot(turned_grads, part_rows(rows_ref, 1, first, HEADS), 1, 0)
        put_rows(out_ref, 2, first, last, key_grads, readers)
        value_grads = dot(turned_weights_ref[here, after], out_grads[after], 1, 0)
        put_rows(out_ref, 3, first, last, value_grads, readers)
        for window in range(first, last):
            span = pl.ds(window * size, size)
            stores.append(
                pltpu.make_async_copy(out_ref.at[span], out_hbm.at[span], store_sems.at[window])
            )
            stores[-1].start()
    for step, layer_ref in enumerate(layer_refs):
        start = pl.multiple_of(turned(head ^ step) * size, size)
        layer_ref[...] = layer_all[pl.ds(start, size), :]
    for copy in stores:
        copy.wait()


def unslot_kernel(back_ref, returned_ref, *refs, per_pair):
    piece_refs = refs[:HEADS]
    layer_hbm, grad_hbm, layer_ref, grad_ref, store_sems = refs[HEADS:]
    slots = back_ref.shape[0]
    readers = slots // per_pair
    width = HEADS * HD
    first = turned(lax.axis_index("ctx"))
    for step, piece_ref in enumerate(piece_refs):
        start = pl.multiple_of((first ^ step) * HD, HD)
        layer_ref[:, pl.ds(start, HD)] = piece_ref[...]
    stores = [pltpu.make_async_copy(layer_ref, layer_hbm, store_sems.at[2])]
    stores[0].start()
    heads = []
    for head in range(HEADS):
        chunks = []
        for owner in range(readers):
            dp_index, ctx_index = device_of(owner, head)
            start = chunk_back(dp_index, ctx_index, readers) * per_pair
            chunks.append(returned_ref[start : start + per_pair])
        heads.append(jnp.concatenate(chunks, axis=0))
    half = slots // 2
    for side in range(2):
        span = pl.ds(side * half, half)
        here = slice(side * half, (side + 1) * half)
        for head in range(HEADS):
            rows = dot(back_ref[here], heads[head], 1, 0).astype(jnp.bfloat16)
            for part in range(4):
                start = part * width + head * HD
                grad_ref[here, start : start + HD] = rows[:, part * HD : (part + 1) * HD]
        stores.append(
            pltpu.make_async_copy(grad_ref.at[span], grad_hbm.at[span], store_sems.at[side])
        )
        stores[-1].start()
    for copy in stores:
        copy.wait()


def send(value, target, back=False):
    width = lax.axis_size("ctx")
    pairs = []
    for dp_index in range(lax.axis_size("dp")):
        for ctx_index in range(width):
            to_dp, to_ctx = target(dp_index, ctx_index)
            pair = (dp_index * width + ctx_index, to_dp * width + to_ctx)
            pairs.append(pair[::-1] if back else pair)
    return lax.ppermute(value, ("dp", "ctx"), pairs)


def exchange(chunks, place):
    readers, width = lax.axis_size("dp"), lax.axis_size("ctx")
    order = [None] * (readers * width)
    for dp_index in range(readers):
        for ctx_index in range(width):
            order[place(dp_index, ctx_index, readers)] = dp_index * width + ctx_index
    return lax.all_to_all(
        chunks, ("dp", "ctx"), split_axis=0, concat_axis=0, tiled=True, axis_index_groups=[order]
    )


def swap(value, dp_bits, ctx_bits):
    return send(value, lambda dp_index, ctx_index: (dp_index ^ dp_bits, ctx_index ^ ctx_bits))


def regroup(pieces, back=False):
    moved = []
    for step, piece in enumerate(pieces):

        def target(dp_index, ctx_index, step=step):
            return device_of(dp_index, turned(ctx_index) ^ step)

        moved.append(send(piece, target, back))
    return moved


def by_heads(proj_read, norm_gain, owner_of, user_of, grad_output):
    slots = proj_read.shape[0]
    readers = lax.axis_size("dp")
    per_pair = slots // readers
    group_rows = slots * HEADS
    width = 4 * HD
    gain = lax.dynamic_slice_in_dim(norm_gain, my_place()[0] * HD, HD, 0).reshape(1, HD)
    piece_shape = jax.ShapeDtypeStruct((slots, HD), jnp.bfloat16)
    chunk_shape = (HEADS * readers, 4 * per_pair + 8, HD)
    outgoing, slot = pl.pallas_call(
        functools.partial(slot_kernel, per_pair=per_pair),
        out_shape=(
            jax.ShapeDtypeStruct(chunk_shape, jnp.bfloat16),
            jax.ShapeDtypeStruct((1, slots), jnp.int32),
        ),
        in_specs=hbm(3),
        out_specs=tuple(hbm(2)),
        scratch_shapes=[
            pltpu.SMEM(owner_of.shape, jnp.int32),
            pltpu.VMEM((1, slots), jnp.int32),
            pltpu.VMEM((1, slots), jnp.int32),
            pltpu.VMEM(proj_read.shape, jnp.bfloat16),
            pltpu.VMEM(chunk_shape, jnp.bfloat16),
            pltpu.SemaphoreType.DMA((3,)),
            pltpu.SemaphoreType.DMA((HEADS + 1,)),
        ],
        name="slot_rows",
    )(owner_of, user_of.reshape(1, slots), proj_read)
    rows = exchange(outgoing, chunk_of)
    *pieces, back = pl.pallas_call(
        columns_kernel,
        out_shape=(piece_shape,) * HEADS + (jax.ShapeDtypeStruct((slots, slots), jnp.bfloat16),),
        in_specs=vmem(2),
        out_specs=tuple(vmem(HEADS + 1)),
        compiler_params=LIMIT,
        name="cut_columns",
    )(slot, grad_output)
    grads = pl.pallas_call(
        group_kernel,
        out_shape=jax.ShapeDtypeStruct((group_rows, HD), jnp.bfloat16),
        in_specs=vmem(HEADS),
        out_specs=vmem(1)[0],
        compiler_params=LIMIT,
        name="lay_group",
    )(*regroup(pieces))
    attended, stats = pl.pallas_call(
        forward_kernel,
        out_shape=(
            jax.ShapeDtypeStruct((group_rows, HD), jnp.float32),
            jax.ShapeDtypeStruct((4, group_rows), jnp.float32),
        ),
        in_specs=vmem(3),
        out_specs=tuple(vmem(2)),
        compiler_params=LIMIT,
        name="forward",
    )(rows, grads, gain)
    late_rows, stats = lax.optimization_barrier((rows, stats))
    slopes = pl.pallas_call(
        slope_kernel,
        out_shape=(
            jax.ShapeDtypeStruct((group_rows, group_rows), jnp.float32),
            jax.ShapeDtypeStruct((group_rows, group_rows), jnp.float32),
            jax.ShapeDtypeStruct((group_rows, group_rows), jnp.bfloat16),
        ),
        in_specs=vmem(1),
        out_specs=tuple(vmem(3)),
        compiler_params=LIMIT,
        name="slopes",
    )(late_rows)
    all_stats = [stats, swap(stats, 1, 0), swap(stats, 0, 1), swap(stats, 1, 1)]
    results = pl.pallas_call(
        backward_kernel,
        out_shape=(jax.ShapeDtypeStruct((group_rows, width), jnp.bfloat16),)
        + (piece_shape,) * HEADS,
        in_specs=vmem(7 + HEADS),
        out_specs=tuple(hbm(1) + vmem(HEADS)),
        scratch_shapes=[
            pltpu.VMEM((group_rows, HD), jnp.bfloat16),
            pltpu.VMEM((group_rows, width), jnp.bfloat16),
            pltpu.SemaphoreType.DMA((HEADS,)),
        ],
        compiler_params=LIMIT,
        name="backward",
    )(rows, grads, gain, attended, *slopes, *all_stats)
    returned = exchange(results[0], chunk_back)
    layer_shape, grad_shape = (slots, HEADS * HD), (slots, 4 * HEADS * HD)
    return pl.pallas_call(
        functools.partial(unslot_kernel, per_pair=per_pair),
        out_shape=(
            jax.ShapeDtypeStruct(layer_shape, jnp.bfloat16),
            jax.ShapeDtypeStruct(grad_shape, jnp.bfloat16),
        ),
        in_specs=vmem(2 + HEADS),
        out_specs=tuple(hbm(2)),
        scratch_shapes=[
            pltpu.VMEM(layer_shape, jnp.bfloat16),
            pltpu.VMEM(grad_shape, jnp.bfloat16),
            pltpu.SemaphoreType.DMA((3,)),
        ],
        compiler_params=LIMIT,
        name="unslot_rows",
    )(back, returned, *regroup(results[1:], back=True))


def solution(mesh):
    in_specs = (P(("dp", "ctx"), None), P(), P(), P(("dp", "ctx")), P(("dp", "ctx"), None))
    out_specs = (P(("dp", "ctx"), None), P(("dp", "ctx"), None))
    fits = mesh.shape["ctx"] == HEADS and mesh.shape["dp"] == 2 * len(SPANS)
    local = by_heads if fits else windowed
    return jax.shard_map(local, mesh=mesh, in_specs=in_specs, out_specs=out_specs, check_vma=False)
```

```python
import functools

import jax
import jax.numpy as jnp
from jax import lax
from jax.experimental import pallas as pl
from jax.experimental.pallas import tpu as pltpu
from jax.sharding import PartitionSpec as P

HEADS = 4
HD = 128


epsilon = 1e-05


def block_length(total_rows, shard_rows):
    shard_total = total_rows // shard_rows
    best_factor = 1
    for factor in range(1, shard_total + 1):
        if shard_total % factor == 0 and factor * shard_rows <= 1024:
            best_factor = factor
    return best_factor * shard_rows


def silu_slope(scores):
    sigmoid_part = jax.nn.sigmoid(scores)
    return sigmoid_part * (1.0 + scores * (1.0 - sigmoid_part))


def visible_pairs(query_users, query_places, key_users, key_places):
    same_user = (query_users[:, None] == key_users[None, :]) & (query_users[:, None] >= 0)
    return same_user & (key_places[None, :] <= query_places[:, None])


def run_blocks(carry_now, shard_piece, block_rows, step_fn):
    total_rows = shard_piece[0].shape[0]

    def one_block(block_index, carry_here):
        offset = block_index * block_rows
        block_part = tuple(
            (
                lax.dynamic_slice_in_dim(array_item, offset, block_rows, 0)
                for array_item in shard_piece
            )
        )
        return step_fn(carry_here, block_part, offset)

    return lax.fori_loop(0, total_rows // block_rows, one_block, carry_now)


def windowed(proj_read, norm_gain, owner_of, user_of, grad_output):
    slot_rows = proj_read.shape[0]
    reader_peers = lax.axis_size("dp")
    per_pair = slot_rows // reader_peers
    feature_width = HEADS * HD
    score_scale = HD ** (-0.5)
    group_rows = slot_rows * lax.axis_size("ctx")
    user_range = jnp.arange(owner_of.shape[0], dtype=jnp.int32)
    owners = jnp.sum(
        jnp.where(user_of[:, None] == user_range[None, :], owner_of[None, :], 0), axis=1
    )
    is_live = user_of >= 0
    owner_hits = (owners[:, None] == jnp.arange(reader_peers, dtype=jnp.int32)[None, :]) & is_live[
        :, None
    ]
    running = jnp.cumsum(owner_hits.astype(jnp.int32), axis=0) - 1
    ranks_mine = jnp.sum(jnp.where(owner_hits, running, 0), axis=1)
    send_slot = jnp.where(is_live, owners * per_pair + ranks_mine, -1)
    slot_range = jnp.arange(slot_rows, dtype=jnp.int32)
    slot_match = send_slot[None, :] == slot_range[:, None]
    filled = jnp.any(slot_match, axis=1)
    source_row = jnp.sum(jnp.where(slot_match, slot_range[None, :], 0), axis=1)
    outgoing = jnp.where(
        filled[:, None], jnp.take(proj_read, source_row, axis=0), jnp.zeros((), jnp.bfloat16)
    )
    outgoing_users = jnp.where(filled, jnp.take(user_of, source_row), -1)
    arrived, arrived_users = (
        lax.all_to_all(outgoing, "dp", split_axis=0, concat_axis=0, tiled=True),
        lax.all_to_all(outgoing_users, "dp", split_axis=0, concat_axis=0, tiled=True),
    )
    own_start = lax.axis_index("ctx") * slot_rows
    own_places = own_start + slot_range
    unit_rows = arrived[:, :feature_width]
    queries = arrived[:, feature_width : 2 * feature_width]
    key_values = arrived[:, 2 * feature_width :]
    query_heads = queries.reshape(slot_rows, HEADS, HD)
    key_heads = key_values[:, :feature_width].reshape(slot_rows, HEADS, HD)
    value_heads = key_values[:, feature_width:].reshape(slot_rows, HEADS, HD)

    def forward_step(total_out, block_part, first_row):
        block_kv, block_users = block_part
        block_size = block_kv.shape[0]
        remote_keys = block_kv[:, :feature_width].reshape(block_size, HEADS, HD)
        remote_values = block_kv[:, feature_width:].reshape(block_size, HEADS, HD)
        scores = (
            jnp.einsum("qhd,khd->hqk", query_heads, remote_keys, preferred_element_type=jnp.float32)
            * score_scale
        )
        visible = visible_pairs(
            arrived_users,
            own_places,
            block_users,
            first_row + jnp.arange(block_size, dtype=jnp.int32),
        )
        weights = jnp.where(visible[None], jax.nn.silu(scores), 0.0).astype(jnp.bfloat16)
        summed = jnp.einsum(
            "hqk,khd->qhd", weights, remote_values, preferred_element_type=jnp.float32
        )
        return total_out + summed.reshape(slot_rows, feature_width)

    zero_rows = jnp.zeros((slot_rows, feature_width), jnp.float32)
    shard_piece = (
        lax.all_gather(key_values, "ctx", axis=0, tiled=True),
        lax.all_gather(arrived_users, "ctx", axis=0, tiled=True),
    )
    block_rows = block_length(shard_piece[0].shape[0], slot_rows)
    forward_result = run_blocks(zero_rows, shard_piece, block_rows, forward_step)
    mean_out = jnp.mean(forward_result, axis=1, keepdims=True)
    centered = forward_result - mean_out
    inv_std = lax.rsqrt(jnp.mean(centered * centered, axis=1, keepdims=True) + epsilon)
    normed = centered * inv_std
    unit_float = unit_rows.astype(jnp.float32)
    layer_out = (normed * norm_gain * unit_float).astype(jnp.bfloat16)
    grad_float = grad_output.astype(jnp.float32)
    unit_grads = (grad_float * norm_gain * normed).astype(jnp.bfloat16)
    grad_normed = grad_float * norm_gain * unit_float
    mean_grad = jnp.mean(grad_normed, axis=1, keepdims=True)
    mean_cross = jnp.mean(grad_normed * normed, axis=1, keepdims=True)
    out_grads = (inv_std * (grad_normed - mean_grad - normed * mean_cross)).astype(jnp.bfloat16)

    def backward_step(carry_here, block_part, first_row):
        block_queries, block_grads, block_users = block_part
        block_size = block_queries.shape[0]
        remote_queries = block_queries.reshape(block_size, HEADS, HD)
        remote_grads = block_grads.reshape(block_size, HEADS, HD)
        scores = (
            jnp.einsum(
                "qhd,khd->hqk", remote_queries, key_heads, preferred_element_type=jnp.float32
            )
            * score_scale
        )
        visible = visible_pairs(
            block_users,
            first_row + jnp.arange(block_size, dtype=jnp.int32),
            arrived_users,
            own_places,
        )[None]
        weights = jnp.where(visible, jax.nn.silu(scores), 0.0).astype(jnp.bfloat16)
        weight_grads = jnp.einsum(
            "qhd,khd->hqk", remote_grads, value_heads, preferred_element_type=jnp.float32
        )
        score_grads = jnp.where(
            visible, weight_grads * silu_slope(scores) * score_scale, 0.0
        ).astype(jnp.bfloat16)
        value_sum = jnp.einsum(
            "hqk,qhd->khd", weights, remote_grads, preferred_element_type=jnp.float32
        ).reshape(slot_rows, feature_width)
        key_sum = jnp.einsum(
            "hqk,qhd->khd", score_grads, remote_queries, preferred_element_type=jnp.float32
        ).reshape(slot_rows, feature_width)
        new_keys = carry_here[0] + key_sum
        new_values = carry_here[1] + value_sum
        window_sum = (
            jnp.einsum("hqk,khd->qhd", score_grads, key_heads, preferred_element_type=jnp.float32)
            .reshape(block_size, feature_width)
            .astype(jnp.bfloat16)
        )
        return (
            new_keys,
            new_values,
            lax.dynamic_update_slice_in_dim(carry_here[2], window_sum, first_row, 0),
        )

    start_carry = (zero_rows, zero_rows, jnp.zeros((group_rows, feature_width), jnp.bfloat16))
    shard_piece = (
        lax.all_gather(queries, "ctx", axis=0, tiled=True),
        lax.all_gather(out_grads, "ctx", axis=0, tiled=True),
        lax.all_gather(arrived_users, "ctx", axis=0, tiled=True),
    )
    block_rows = block_length(shard_piece[0].shape[0], slot_rows)
    key_results = run_blocks(start_carry, shard_piece, block_rows, backward_step)
    key_grads = key_results[0]
    value_grads = key_results[1]
    query_grads = lax.psum_scatter(key_results[2], "ctx", scatter_dimension=0, tiled=True).astype(
        jnp.float32
    )
    grads_owned = jnp.concatenate(
        [
            unit_grads,
            query_grads.astype(jnp.bfloat16),
            key_grads.astype(jnp.bfloat16),
            value_grads.astype(jnp.bfloat16),
        ],
        axis=1,
    )
    returned = lax.all_to_all(grads_owned, "dp", split_axis=0, concat_axis=0, tiled=True)
    back_rows = jnp.take(returned, jnp.maximum(send_slot, 0), axis=0)
    grad_read = jnp.where(is_live[:, None], back_rows, jnp.zeros((), jnp.bfloat16))
    return (layer_out, grad_read)


STEP = 2
LIMIT = pltpu.CompilerParams(vmem_limit_bytes=16 * 2**20)


def device_of(owner, head):
    return (owner & ~1) | (head & 1), ((owner & 1) << 1) | (head >> 1)


SPANS = (3, 1, 2, 0)


def chunk_of(dp_index, ctx_index, readers):
    return turned(ctx_index) * readers + SPANS[dp_index >> 1] * 2 + (dp_index & 1)


def chunk_back(dp_index, ctx_index, readers):
    return ctx_index * readers + (dp_index & 1) * (readers // 2) + (dp_index >> 1)


def turned(index):
    return ((index & 1) << 1) | (index >> 1)


def vmem(count):
    return [pl.BlockSpec(memory_space=pltpu.VMEM)] * count


def hbm(count):
    return [pl.BlockSpec(memory_space=pltpu.HBM)] * count


def dot(left, right, left_dim, right_dim):
    return lax.dot_general(
        left, right, (((left_dim,), (right_dim,)), ((), ())), preferred_element_type=jnp.float32
    )


def owners_of(users, owner_ref):
    owners = jnp.zeros_like(users)
    for user in range(owner_ref.shape[0]):
        owners = jnp.where(users == user, owner_ref[user], owners)
    return owners


def lower_ones(size):
    earlier = lax.broadcasted_iota(jnp.int32, (size, size), 0)
    later = lax.broadcasted_iota(jnp.int32, (size, size), 1)
    return (earlier <= later).astype(jnp.bfloat16)


def my_place():
    my_dp, my_ctx = lax.axis_index("dp"), lax.axis_index("ctx")
    return ((my_ctx & 1) << 1) | (my_dp & 1), (my_dp & ~1) | (my_ctx >> 1), my_dp, my_ctx


def slot_kernel(
    owner_hbm,
    user_hbm,
    proj_hbm,
    send_hbm,
    slot_hbm,
    owner_ref,
    user_ref,
    slot_ref,
    proj_ref,
    send_ref,
    load_sems,
    store_sems,
    *,
    per_pair,
):
    slots = user_ref.shape[1]
    readers = slots // per_pair
    width = HEADS * HD
    loads = [
        pltpu.make_async_copy(source, target, load_sems.at[index])
        for index, (source, target) in enumerate(
            ((user_hbm, user_ref), (owner_hbm, owner_ref), (proj_hbm, proj_ref))
        )
    ]
    for copy in loads:
        copy.start()
    my_dp = lax.axis_index("dp")
    source = lax.broadcasted_iota(jnp.int32, (slots, slots), 0)
    owner_range = lax.broadcasted_iota(jnp.int32, (readers, slots), 0)
    loads[0].wait()
    loads[1].wait()
    users = user_ref[...]
    owners = owners_of(users, owner_ref)
    is_live = users >= 0
    hits = ((owner_range == owners) & is_live).astype(jnp.float32)
    running = dot(hits.astype(jnp.bfloat16), lower_ones(slots), 1, 0)
    ranks = jnp.sum(hits * running, axis=0, keepdims=True).astype(jnp.int32) - 1
    slot = jnp.where(is_live, owners * per_pair + ranks, -1)
    slot_ref[...] = slot
    stores = [pltpu.make_async_copy(slot_ref, slot_hbm, store_sems.at[HEADS])]
    stores[0].start()
    placed = (source == slot).astype(jnp.bfloat16)
    tagged = (hits * (users + 1).astype(jnp.float32)).astype(jnp.bfloat16)
    to_lane = (source == my_dp * per_pair + ranks).astype(jnp.bfloat16)
    tagged = dot(tagged, to_lane, 1, 1).astype(jnp.bfloat16)
    extra = send_ref.shape[1] - 4 * per_pair
    for owner in range(readers):
        for head in range(HEADS):
            dp_index, ctx_index = device_of(owner, head)
            chunk = chunk_of(dp_index, ctx_index, readers)
            send_ref[chunk, 4 * per_pair :, :] = jnp.broadcast_to(
                tagged[owner : owner + 1], (extra, slots)
            )
    loads[2].wait()
    for half in range(2):
        for part in range(4):
            start = part * width + half * 2 * HD
            rows = dot(placed, proj_ref[:, start : start + 2 * HD], 1, 0).astype(jnp.bfloat16)
            for owner in range(readers):
                for side in range(2):
                    dp_index, ctx_index = device_of(owner, 2 * half + side)
                    chunk = chunk_of(dp_index, ctx_index, readers)
                    send_ref[chunk, part * per_pair : (part + 1) * per_pair, :] = rows[
                        owner * per_pair : (owner + 1) * per_pair, side * HD : (side + 1) * HD
                    ]
        for ctx_index in (half, 2 + half):
            span = pl.ds(turned(ctx_index) * readers, readers)
            stores.append(
                pltpu.make_async_copy(
                    send_ref.at[span], send_hbm.at[span], store_sems.at[ctx_index]
                )
            )
            stores[-1].start()
    for copy in stores:
        copy.wait()


def columns_kernel(slot_ref, grad_ref, *refs):
    piece_refs, back_ref = refs[:HEADS], refs[HEADS]
    slots = slot_ref.shape[1]
    slot = jnp.broadcast_to(slot_ref[...].astype(jnp.float32), (slots, slots)).T
    lane = lax.broadcasted_iota(jnp.int32, (slots, slots), 1).astype(jnp.float32)
    back_ref[...] = (slot == lane).astype(jnp.bfloat16)
    first = turned(lax.axis_index("ctx"))
    for step, piece_ref in enumerate(piece_refs):
        start = pl.multiple_of((first ^ step) * HD, HD)
        piece_ref[...] = grad_ref[:, pl.ds(start, HD)]


def group_kernel(*refs):
    piece_refs, grads_ref = refs[:HEADS], refs[HEADS]
    head = my_place()[0]
    for step, piece_ref in enumerate(piece_refs):
        slots = piece_ref.shape[0]
        start = pl.multiple_of(turned(head ^ step) * slots, slots)
        grads_ref[pl.ds(start, slots), :] = piece_ref[...]


def part_rows(rows_ref, part, first, last):
    readers = rows_ref.shape[0] // HEADS
    per_pair = HD // readers
    span = slice(part * per_pair, (part + 1) * per_pair)
    rows = [
        rows_ref[chunk_of(reader, window, readers), span, :]
        for window in range(first, last)
        for reader in range(readers)
    ]
    return jnp.concatenate(rows, axis=0)


def put_rows(out_ref, part, first, last, rows, readers):
    per_pair = HD // readers
    for window in range(first, last):
        for reader in range(readers):
            source = ((window - first) * readers + reader) * per_pair
            target = chunk_back(reader, window, readers) * per_pair
            out_ref[target : target + per_pair, part * HD : (part + 1) * HD] = rows[
                source : source + per_pair
            ].astype(jnp.bfloat16)


def window_users(rows_ref, window):
    readers = rows_ref.shape[0] // HEADS
    per_pair = HD // readers
    first = turned(window) * readers
    tags = rows_ref[first : first + readers, 4 * per_pair :, :]
    return jnp.sum(tags.astype(jnp.float32), axis=0)[:1]


def visible_block(users, first, last):
    size = HD
    query_users = [jnp.broadcast_to(users[window], (size, size)).T for window in range(first, last)]
    query_users = jnp.concatenate(query_users, axis=0)
    rows = lax.broadcasted_iota(jnp.int32, query_users.shape, 0)
    columns = lax.broadcasted_iota(jnp.int32, query_users.shape, 1)
    blocks = []
    for window in range(last):
        block = (query_users == users[window]) & (query_users > 0.0)
        if window >= first:
            block = block & (columns + (window - first) * size <= rows)
        blocks.append(block)
    return jnp.concatenate(blocks, axis=1)


def forward_kernel(rows_ref, grads_ref, gain_ref, attended_ref, stats_ref):
    size = HD
    scale = HD ** (-0.5)
    users = [window_users(rows_ref, window) for window in range(HEADS)]
    for first in range(0, HEADS, STEP):
        last = first + STEP
        queries = part_rows(rows_ref, 1, first, last)
        scores = dot(queries, part_rows(rows_ref, 2, 0, last), 1, 1) * scale
        visible = visible_block(users, first, last)
        weights = jnp.where(visible, scores * jax.nn.sigmoid(scores), 0.0).astype(jnp.bfloat16)
        block = dot(weights, part_rows(rows_ref, 3, 0, last), 1, 0)
        attended_ref[first * size : last * size] = block
        for window in range(first, last):
            here = slice(window * size, (window + 1) * size)
            attended = block[(window - first) * size : (window - first + 1) * size]
            grad_normed = (
                grads_ref[here].astype(jnp.float32)
                * gain_ref[...]
                * part_rows(rows_ref, 0, window, window + 1).astype(jnp.float32)
            )
            turned_att = attended.T
            turned_grad = grad_normed.T
            mean = jnp.mean(turned_att, axis=0, keepdims=True)
            centered = turned_att - mean
            spread = jnp.sum(centered * centered, axis=0, keepdims=True)
            grad_sum = jnp.sum(turned_grad, axis=0, keepdims=True)
            cross = jnp.sum(turned_grad * centered, axis=0, keepdims=True)
            stats_ref[0:1, here] = mean
            stats_ref[1:2, here] = spread
            stats_ref[2:3, here] = grad_sum
            stats_ref[3:4, here] = cross


def slope_kernel(
    rows_ref,
    grads_ref,
    gain_ref,
    slopes_ref,
    turned_slopes_ref,
    turned_weights_ref,
    gate_ref,
    grad_gain_ref,
    grad_normed_ref,
):
    size = HD
    scale = HD ** (-0.5)
    users = [window_users(rows_ref, window) for window in range(HEADS)]
    gate = part_rows(rows_ref, 0, 0, HEADS).astype(jnp.float32) * gain_ref[...]
    grads = grads_ref[...].astype(jnp.float32)
    gate_ref[...] = gate
    grad_gain_ref[...] = grads * gain_ref[...]
    grad_normed_ref[...] = grads * gate
    for first in range(0, HEADS, STEP):
        last = first + STEP
        queries = part_rows(rows_ref, 1, first, last)
        scores = dot(queries, part_rows(rows_ref, 2, 0, last), 1, 1) * scale
        sigmoid = jax.nn.sigmoid(scores)
        slopes = sigmoid * (1.0 + scores * (1.0 - sigmoid)) * scale
        visible = visible_block(users, first, last)
        slopes = jnp.where(visible, slopes, 0.0)
        weights = jnp.where(visible, scores * sigmoid, 0.0)
        slopes_ref[first * size : last * size, : last * size] = slopes
        turned_slopes_ref[: last * size, first * size : last * size] = slopes.T
        turned_weights_ref[: last * size, first * size : last * size] = weights.T.astype(
            jnp.bfloat16
        )


def backward_kernel(
    rows_ref,
    attended_ref,
    slopes_ref,
    turned_slopes_ref,
    turned_weights_ref,
    gate_ref,
    grad_gain_ref,
    grad_normed_ref,
    *refs,
):
    stats_refs = refs[:HEADS]
    out_hbm = refs[HEADS]
    layer_refs = refs[HEADS + 1 : 2 * HEADS + 1]
    layer_all, out_ref, store_sems = refs[2 * HEADS + 1 :]
    head = my_place()[0]
    readers = rows_ref.shape[0] // HEADS
    size = HD
    width = float(HEADS * HD)
    stats = [stat_ref[...] for stat_ref in stats_refs]
    mean = sum(stat[0:1] for stat in stats) * (1.0 / HEADS)
    spread = sum(stat[1:2] + HD * (stat[0:1] - mean) * (stat[0:1] - mean) for stat in stats)
    inv_std = lax.rsqrt(spread / width + epsilon)
    mean_grad = sum(stat[2:3] for stat in stats) / width
    cross = sum(stat[3:4] + (stat[0:1] - mean) * stat[2:3] for stat in stats)
    mean_cross = cross * inv_std / width
    packed = [
        stat[:, window * size : (window + 1) * size]
        for window in range(HEADS)
        for stat in (mean, inv_std, mean_grad, mean_cross)
    ]
    packed.append(jnp.zeros((size - len(packed), size), jnp.float32))
    packed = jnp.concatenate(packed, axis=0).T
    out_grads = []
    for window in range(HEADS):
        here = slice(window * size, (window + 1) * size)
        row_mean, row_inv, row_grad, row_cross = [
            packed[:, 4 * window + index : 4 * window + index + 1] for index in range(4)
        ]
        normed = (attended_ref[here] - row_mean) * row_inv
        layer_all[here] = (normed * gate_ref[here]).astype(jnp.bfloat16)
        put_rows(out_ref, 0, window, window + 1, grad_gain_ref[here] * normed, readers)
        out_grads.append(row_inv * (grad_normed_ref[here] - row_grad - normed * row_cross))
    out_grads = jnp.concatenate(out_grads, axis=0).astype(jnp.bfloat16)
    stores = []
    for first in range(0, HEADS, STEP):
        last = first + STEP
        here = slice(first * size, last * size)
        upto = slice(0, last * size)
        after = slice(first * size, HEADS * size)
        score_grads = (
            dot(out_grads[here], part_rows(rows_ref, 3, 0, last), 1, 1) * slopes_ref[here, upto]
        ).astype(jnp.bfloat16)
        query_grads = dot(score_grads, part_rows(rows_ref, 2, 0, last), 1, 0)
        put_rows(out_ref, 1, first, last, query_grads, readers)
        turned_grads = (
            dot(part_rows(rows_ref, 3, first, last), out_grads[after], 1, 1)
            * turned_slopes_ref[here, after]
        ).astype(jnp.bfloat16)
        key_grads = dot(turned_grads, part_rows(rows_ref, 1, first, HEADS), 1, 0)
        put_rows(out_ref, 2, first, last, key_grads, readers)
        value_grads = dot(turned_weights_ref[here, after], out_grads[after], 1, 0)
        put_rows(out_ref, 3, first, last, value_grads, readers)
        for window in range(first, last):
            span = pl.ds(window * size, size)
            stores.append(
                pltpu.make_async_copy(out_ref.at[span], out_hbm.at[span], store_sems.at[window])
            )
            stores[-1].start()
    for step, layer_ref in enumerate(layer_refs):
        start = pl.multiple_of(turned(head ^ step) * size, size)
        layer_ref[...] = layer_all[pl.ds(start, size), :]
    for copy in stores:
        copy.wait()


def unslot_kernel(back_ref, returned_ref, *refs, per_pair):
    piece_refs = refs[:HEADS]
    layer_hbm, grad_hbm, layer_ref, grad_ref, store_sems = refs[HEADS:]
    slots = back_ref.shape[0]
    readers = slots // per_pair
    width = HEADS * HD
    first = turned(lax.axis_index("ctx"))
    for step, piece_ref in enumerate(piece_refs):
        start = pl.multiple_of((first ^ step) * HD, HD)
        layer_ref[:, pl.ds(start, HD)] = piece_ref[...]
    stores = [pltpu.make_async_copy(layer_ref, layer_hbm, store_sems.at[2])]
    stores[0].start()
    heads = []
    for head in range(HEADS):
        chunks = []
        for owner in range(readers):
            dp_index, ctx_index = device_of(owner, head)
            start = chunk_back(dp_index, ctx_index, readers) * per_pair
            chunks.append(returned_ref[start : start + per_pair])
        heads.append(jnp.concatenate(chunks, axis=0))
    half = slots // 2
    for side in range(2):
        span = pl.ds(side * half, half)
        here = slice(side * half, (side + 1) * half)
        for head in range(HEADS):
            rows = dot(back_ref[here], heads[head], 1, 0).astype(jnp.bfloat16)
            for part in range(4):
                start = part * width + head * HD
                grad_ref[here, start : start + HD] = rows[:, part * HD : (part + 1) * HD]
        stores.append(
            pltpu.make_async_copy(grad_ref.at[span], grad_hbm.at[span], store_sems.at[side])
        )
        stores[-1].start()
    for copy in stores:
        copy.wait()


def send(value, target, back=False):
    width = lax.axis_size("ctx")
    pairs = []
    for dp_index in range(lax.axis_size("dp")):
        for ctx_index in range(width):
            to_dp, to_ctx = target(dp_index, ctx_index)
            pair = (dp_index * width + ctx_index, to_dp * width + to_ctx)
            pairs.append(pair[::-1] if back else pair)
    return lax.ppermute(value, ("dp", "ctx"), pairs)


def exchange(chunks, place):
    readers, width = lax.axis_size("dp"), lax.axis_size("ctx")
    order = [None] * (readers * width)
    for dp_index in range(readers):
        for ctx_index in range(width):
            order[place(dp_index, ctx_index, readers)] = dp_index * width + ctx_index
    return lax.all_to_all(
        chunks, ("dp", "ctx"), split_axis=0, concat_axis=0, tiled=True, axis_index_groups=[order]
    )


def swap(value, dp_bits, ctx_bits):
    return send(value, lambda dp_index, ctx_index: (dp_index ^ dp_bits, ctx_index ^ ctx_bits))


def regroup(pieces, back=False):
    moved = []
    for step, piece in enumerate(pieces):

        def target(dp_index, ctx_index, step=step):
            return device_of(dp_index, turned(ctx_index) ^ step)

        moved.append(send(piece, target, back))
    return moved


def by_heads(proj_read, norm_gain, owner_of, user_of, grad_output):
    slots = proj_read.shape[0]
    readers = lax.axis_size("dp")
    per_pair = slots // readers
    group_rows = slots * HEADS
    width = 4 * HD
    gain = lax.dynamic_slice_in_dim(norm_gain, my_place()[0] * HD, HD, 0).reshape(1, HD)
    piece_shape = jax.ShapeDtypeStruct((slots, HD), jnp.bfloat16)
    chunk_shape = (HEADS * readers, 4 * per_pair + 8, HD)
    outgoing, slot = pl.pallas_call(
        functools.partial(slot_kernel, per_pair=per_pair),
        out_shape=(
            jax.ShapeDtypeStruct(chunk_shape, jnp.bfloat16),
            jax.ShapeDtypeStruct((1, slots), jnp.int32),
        ),
        in_specs=hbm(3),
        out_specs=tuple(hbm(2)),
        scratch_shapes=[
            pltpu.SMEM(owner_of.shape, jnp.int32),
            pltpu.VMEM((1, slots), jnp.int32),
            pltpu.VMEM((1, slots), jnp.int32),
            pltpu.VMEM(proj_read.shape, jnp.bfloat16),
            pltpu.VMEM(chunk_shape, jnp.bfloat16),
            pltpu.SemaphoreType.DMA((3,)),
            pltpu.SemaphoreType.DMA((HEADS + 1,)),
        ],
        name="slot_rows",
    )(owner_of, user_of.reshape(1, slots), proj_read)
    rows = exchange(outgoing, chunk_of)
    *pieces, back = pl.pallas_call(
        columns_kernel,
        out_shape=(piece_shape,) * HEADS + (jax.ShapeDtypeStruct((slots, slots), jnp.bfloat16),),
        in_specs=vmem(2),
        out_specs=tuple(vmem(HEADS + 1)),
        compiler_params=LIMIT,
        name="cut_columns",
    )(slot, grad_output)
    grads = pl.pallas_call(
        group_kernel,
        out_shape=jax.ShapeDtypeStruct((group_rows, HD), jnp.bfloat16),
        in_specs=vmem(HEADS),
        out_specs=vmem(1)[0],
        compiler_params=LIMIT,
        name="lay_group",
    )(*regroup(pieces))
    attended, stats = pl.pallas_call(
        forward_kernel,
        out_shape=(
            jax.ShapeDtypeStruct((group_rows, HD), jnp.float32),
            jax.ShapeDtypeStruct((4, group_rows), jnp.float32),
        ),
        in_specs=vmem(3),
        out_specs=tuple(vmem(2)),
        compiler_params=LIMIT,
        name="forward",
    )(rows, grads, gain)
    late_rows, stats = lax.optimization_barrier((rows, stats))
    slopes = pl.pallas_call(
        slope_kernel,
        out_shape=(
            jax.ShapeDtypeStruct((group_rows, group_rows), jnp.float32),
            jax.ShapeDtypeStruct((group_rows, group_rows), jnp.float32),
            jax.ShapeDtypeStruct((group_rows, group_rows), jnp.bfloat16),
        )
        + (jax.ShapeDtypeStruct((group_rows, HD), jnp.float32),) * 3,
        in_specs=vmem(3),
        out_specs=tuple(vmem(6)),
        compiler_params=LIMIT,
        name="slopes",
    )(late_rows, grads, gain)
    all_stats = [stats, swap(stats, 1, 0), swap(stats, 0, 1), swap(stats, 1, 1)]
    results = pl.pallas_call(
        backward_kernel,
        out_shape=(jax.ShapeDtypeStruct((group_rows, width), jnp.bfloat16),)
        + (piece_shape,) * HEADS,
        in_specs=vmem(8 + HEADS),
        out_specs=tuple(hbm(1) + vmem(HEADS)),
        scratch_shapes=[
            pltpu.VMEM((group_rows, HD), jnp.bfloat16),
            pltpu.VMEM((group_rows, width), jnp.bfloat16),
            pltpu.SemaphoreType.DMA((HEADS,)),
        ],
        compiler_params=LIMIT,
        name="backward",
    )(rows, attended, *slopes, *all_stats)
    returned = exchange(results[0], chunk_back)
    layer_shape, grad_shape = (slots, HEADS * HD), (slots, 4 * HEADS * HD)
    return pl.pallas_call(
        functools.partial(unslot_kernel, per_pair=per_pair),
        out_shape=(
            jax.ShapeDtypeStruct(layer_shape, jnp.bfloat16),
            jax.ShapeDtypeStruct(grad_shape, jnp.bfloat16),
        ),
        in_specs=vmem(2 + HEADS),
        out_specs=tuple(hbm(2)),
        scratch_shapes=[
            pltpu.VMEM(layer_shape, jnp.bfloat16),
            pltpu.VMEM(grad_shape, jnp.bfloat16),
            pltpu.SemaphoreType.DMA((3,)),
        ],
        compiler_params=LIMIT,
        name="unslot_rows",
    )(back, returned, *regroup(results[1:], back=True))


def solution(mesh):
    in_specs = (P(("dp", "ctx"), None), P(), P(), P(("dp", "ctx")), P(("dp", "ctx"), None))
    out_specs = (P(("dp", "ctx"), None), P(("dp", "ctx"), None))
    fits = mesh.shape["ctx"] == HEADS and mesh.shape["dp"] == 2 * len(SPANS)
    local = by_heads if fits else windowed
    return jax.shard_map(local, mesh=mesh, in_specs=in_specs, out_specs=out_specs, check_vma=False)
```

```python
import functools

import jax
import jax.numpy as jnp
from jax import lax
from jax.experimental import pallas as pl
from jax.experimental.pallas import tpu as pltpu
from jax.sharding import PartitionSpec as P

HEADS = 4
HD = 128


epsilon = 1e-05


def block_length(total_rows, shard_rows):
    shard_total = total_rows // shard_rows
    best_factor = 1
    for factor in range(1, shard_total + 1):
        if shard_total % factor == 0 and factor * shard_rows <= 1024:
            best_factor = factor
    return best_factor * shard_rows


def silu_slope(scores):
    sigmoid_part = jax.nn.sigmoid(scores)
    return sigmoid_part * (1.0 + scores * (1.0 - sigmoid_part))


def visible_pairs(query_users, query_places, key_users, key_places):
    same_user = (query_users[:, None] == key_users[None, :]) & (query_users[:, None] >= 0)
    return same_user & (key_places[None, :] <= query_places[:, None])


def run_blocks(carry_now, shard_piece, block_rows, step_fn):
    total_rows = shard_piece[0].shape[0]

    def one_block(block_index, carry_here):
        offset = block_index * block_rows
        block_part = tuple(
            (
                lax.dynamic_slice_in_dim(array_item, offset, block_rows, 0)
                for array_item in shard_piece
            )
        )
        return step_fn(carry_here, block_part, offset)

    return lax.fori_loop(0, total_rows // block_rows, one_block, carry_now)


def windowed(proj_read, norm_gain, owner_of, user_of, grad_output):
    slot_rows = proj_read.shape[0]
    reader_peers = lax.axis_size("dp")
    per_pair = slot_rows // reader_peers
    feature_width = HEADS * HD
    score_scale = HD ** (-0.5)
    group_rows = slot_rows * lax.axis_size("ctx")
    user_range = jnp.arange(owner_of.shape[0], dtype=jnp.int32)
    owners = jnp.sum(
        jnp.where(user_of[:, None] == user_range[None, :], owner_of[None, :], 0), axis=1
    )
    is_live = user_of >= 0
    owner_hits = (owners[:, None] == jnp.arange(reader_peers, dtype=jnp.int32)[None, :]) & is_live[
        :, None
    ]
    running = jnp.cumsum(owner_hits.astype(jnp.int32), axis=0) - 1
    ranks_mine = jnp.sum(jnp.where(owner_hits, running, 0), axis=1)
    send_slot = jnp.where(is_live, owners * per_pair + ranks_mine, -1)
    slot_range = jnp.arange(slot_rows, dtype=jnp.int32)
    slot_match = send_slot[None, :] == slot_range[:, None]
    filled = jnp.any(slot_match, axis=1)
    source_row = jnp.sum(jnp.where(slot_match, slot_range[None, :], 0), axis=1)
    outgoing = jnp.where(
        filled[:, None], jnp.take(proj_read, source_row, axis=0), jnp.zeros((), jnp.bfloat16)
    )
    outgoing_users = jnp.where(filled, jnp.take(user_of, source_row), -1)
    arrived, arrived_users = (
        lax.all_to_all(outgoing, "dp", split_axis=0, concat_axis=0, tiled=True),
        lax.all_to_all(outgoing_users, "dp", split_axis=0, concat_axis=0, tiled=True),
    )
    own_start = lax.axis_index("ctx") * slot_rows
    own_places = own_start + slot_range
    unit_rows = arrived[:, :feature_width]
    queries = arrived[:, feature_width : 2 * feature_width]
    key_values = arrived[:, 2 * feature_width :]
    query_heads = queries.reshape(slot_rows, HEADS, HD)
    key_heads = key_values[:, :feature_width].reshape(slot_rows, HEADS, HD)
    value_heads = key_values[:, feature_width:].reshape(slot_rows, HEADS, HD)

    def forward_step(total_out, block_part, first_row):
        block_kv, block_users = block_part
        block_size = block_kv.shape[0]
        remote_keys = block_kv[:, :feature_width].reshape(block_size, HEADS, HD)
        remote_values = block_kv[:, feature_width:].reshape(block_size, HEADS, HD)
        scores = (
            jnp.einsum("qhd,khd->hqk", query_heads, remote_keys, preferred_element_type=jnp.float32)
            * score_scale
        )
        visible = visible_pairs(
            arrived_users,
            own_places,
            block_users,
            first_row + jnp.arange(block_size, dtype=jnp.int32),
        )
        weights = jnp.where(visible[None], jax.nn.silu(scores), 0.0).astype(jnp.bfloat16)
        summed = jnp.einsum(
            "hqk,khd->qhd", weights, remote_values, preferred_element_type=jnp.float32
        )
        return total_out + summed.reshape(slot_rows, feature_width)

    zero_rows = jnp.zeros((slot_rows, feature_width), jnp.float32)
    shard_piece = (
        lax.all_gather(key_values, "ctx", axis=0, tiled=True),
        lax.all_gather(arrived_users, "ctx", axis=0, tiled=True),
    )
    block_rows = block_length(shard_piece[0].shape[0], slot_rows)
    forward_result = run_blocks(zero_rows, shard_piece, block_rows, forward_step)
    mean_out = jnp.mean(forward_result, axis=1, keepdims=True)
    centered = forward_result - mean_out
    inv_std = lax.rsqrt(jnp.mean(centered * centered, axis=1, keepdims=True) + epsilon)
    normed = centered * inv_std
    unit_float = unit_rows.astype(jnp.float32)
    layer_out = (normed * norm_gain * unit_float).astype(jnp.bfloat16)
    grad_float = grad_output.astype(jnp.float32)
    unit_grads = (grad_float * norm_gain * normed).astype(jnp.bfloat16)
    grad_normed = grad_float * norm_gain * unit_float
    mean_grad = jnp.mean(grad_normed, axis=1, keepdims=True)
    mean_cross = jnp.mean(grad_normed * normed, axis=1, keepdims=True)
    out_grads = (inv_std * (grad_normed - mean_grad - normed * mean_cross)).astype(jnp.bfloat16)

    def backward_step(carry_here, block_part, first_row):
        block_queries, block_grads, block_users = block_part
        block_size = block_queries.shape[0]
        remote_queries = block_queries.reshape(block_size, HEADS, HD)
        remote_grads = block_grads.reshape(block_size, HEADS, HD)
        scores = (
            jnp.einsum(
                "qhd,khd->hqk", remote_queries, key_heads, preferred_element_type=jnp.float32
            )
            * score_scale
        )
        visible = visible_pairs(
            block_users,
            first_row + jnp.arange(block_size, dtype=jnp.int32),
            arrived_users,
            own_places,
        )[None]
        weights = jnp.where(visible, jax.nn.silu(scores), 0.0).astype(jnp.bfloat16)
        weight_grads = jnp.einsum(
            "qhd,khd->hqk", remote_grads, value_heads, preferred_element_type=jnp.float32
        )
        score_grads = jnp.where(
            visible, weight_grads * silu_slope(scores) * score_scale, 0.0
        ).astype(jnp.bfloat16)
        value_sum = jnp.einsum(
            "hqk,qhd->khd", weights, remote_grads, preferred_element_type=jnp.float32
        ).reshape(slot_rows, feature_width)
        key_sum = jnp.einsum(
            "hqk,qhd->khd", score_grads, remote_queries, preferred_element_type=jnp.float32
        ).reshape(slot_rows, feature_width)
        new_keys = carry_here[0] + key_sum
        new_values = carry_here[1] + value_sum
        window_sum = (
            jnp.einsum("hqk,khd->qhd", score_grads, key_heads, preferred_element_type=jnp.float32)
            .reshape(block_size, feature_width)
            .astype(jnp.bfloat16)
        )
        return (
            new_keys,
            new_values,
            lax.dynamic_update_slice_in_dim(carry_here[2], window_sum, first_row, 0),
        )

    start_carry = (zero_rows, zero_rows, jnp.zeros((group_rows, feature_width), jnp.bfloat16))
    shard_piece = (
        lax.all_gather(queries, "ctx", axis=0, tiled=True),
        lax.all_gather(out_grads, "ctx", axis=0, tiled=True),
        lax.all_gather(arrived_users, "ctx", axis=0, tiled=True),
    )
    block_rows = block_length(shard_piece[0].shape[0], slot_rows)
    key_results = run_blocks(start_carry, shard_piece, block_rows, backward_step)
    key_grads = key_results[0]
    value_grads = key_results[1]
    query_grads = lax.psum_scatter(key_results[2], "ctx", scatter_dimension=0, tiled=True).astype(
        jnp.float32
    )
    grads_owned = jnp.concatenate(
        [
            unit_grads,
            query_grads.astype(jnp.bfloat16),
            key_grads.astype(jnp.bfloat16),
            value_grads.astype(jnp.bfloat16),
        ],
        axis=1,
    )
    returned = lax.all_to_all(grads_owned, "dp", split_axis=0, concat_axis=0, tiled=True)
    back_rows = jnp.take(returned, jnp.maximum(send_slot, 0), axis=0)
    grad_read = jnp.where(is_live[:, None], back_rows, jnp.zeros((), jnp.bfloat16))
    return (layer_out, grad_read)


STEP = 2
LIMIT = pltpu.CompilerParams(vmem_limit_bytes=16 * 2**20)


def device_of(owner, head):
    return (owner & ~1) | (head & 1), ((owner & 1) << 1) | (head >> 1)


SPANS = (3, 1, 2, 0)


def chunk_of(dp_index, ctx_index, readers):
    return turned(ctx_index) * readers + SPANS[dp_index >> 1] * 2 + (dp_index & 1)


def chunk_back(dp_index, ctx_index, readers):
    return ctx_index * readers + (dp_index & 1) * (readers // 2) + (dp_index >> 1)


def turned(index):
    return ((index & 1) << 1) | (index >> 1)


def vmem(count):
    return [pl.BlockSpec(memory_space=pltpu.VMEM)] * count


def hbm(count):
    return [pl.BlockSpec(memory_space=pltpu.HBM)] * count


def dot(left, right, left_dim, right_dim):
    return lax.dot_general(
        left, right, (((left_dim,), (right_dim,)), ((), ())), preferred_element_type=jnp.float32
    )


def owners_of(users, owner_ref):
    owners = jnp.zeros_like(users)
    for user in range(owner_ref.shape[0]):
        owners = jnp.where(users == user, owner_ref[user], owners)
    return owners


def lower_ones(size):
    earlier = lax.broadcasted_iota(jnp.int32, (size, size), 0)
    later = lax.broadcasted_iota(jnp.int32, (size, size), 1)
    return (earlier <= later).astype(jnp.bfloat16)


def my_place():
    my_dp, my_ctx = lax.axis_index("dp"), lax.axis_index("ctx")
    return ((my_ctx & 1) << 1) | (my_dp & 1), (my_dp & ~1) | (my_ctx >> 1), my_dp, my_ctx


def slot_kernel(
    owner_hbm,
    user_hbm,
    proj_hbm,
    send_hbm,
    slot_hbm,
    owner_ref,
    user_ref,
    slot_ref,
    proj_ref,
    send_ref,
    load_sems,
    store_sems,
    *,
    per_pair,
):
    slots = user_ref.shape[1]
    readers = slots // per_pair
    width = HEADS * HD
    loads = [
        pltpu.make_async_copy(source, target, load_sems.at[index])
        for index, (source, target) in enumerate(
            ((user_hbm, user_ref), (owner_hbm, owner_ref), (proj_hbm, proj_ref))
        )
    ]
    for copy in loads:
        copy.start()
    my_dp = lax.axis_index("dp")
    source = lax.broadcasted_iota(jnp.int32, (slots, slots), 0)
    owner_range = lax.broadcasted_iota(jnp.int32, (readers, slots), 0)
    loads[0].wait()
    loads[1].wait()
    users = user_ref[...]
    owners = owners_of(users, owner_ref)
    is_live = users >= 0
    hits = ((owner_range == owners) & is_live).astype(jnp.float32)
    running = dot(hits.astype(jnp.bfloat16), lower_ones(slots), 1, 0)
    ranks = jnp.sum(hits * running, axis=0, keepdims=True).astype(jnp.int32) - 1
    slot = jnp.where(is_live, owners * per_pair + ranks, -1)
    slot_ref[...] = slot
    stores = [pltpu.make_async_copy(slot_ref, slot_hbm, store_sems.at[HEADS])]
    stores[0].start()
    placed = (source == slot).astype(jnp.bfloat16)
    tagged = (hits * (users + 1).astype(jnp.float32)).astype(jnp.bfloat16)
    to_lane = (source == my_dp * per_pair + ranks).astype(jnp.bfloat16)
    tagged = dot(tagged, to_lane, 1, 1).astype(jnp.bfloat16)
    extra = send_ref.shape[1] - 4 * per_pair
    for owner in range(readers):
        for head in range(HEADS):
            dp_index, ctx_index = device_of(owner, head)
            chunk = chunk_of(dp_index, ctx_index, readers)
            send_ref[chunk, 4 * per_pair :, :] = jnp.broadcast_to(
                tagged[owner : owner + 1], (extra, slots)
            )
    loads[2].wait()
    for half in range(2):
        for part in range(4):
            start = part * width + half * 2 * HD
            rows = dot(placed, proj_ref[:, start : start + 2 * HD], 1, 0).astype(jnp.bfloat16)
            for owner in range(readers):
                for side in range(2):
                    dp_index, ctx_index = device_of(owner, 2 * half + side)
                    chunk = chunk_of(dp_index, ctx_index, readers)
                    send_ref[chunk, part * per_pair : (part + 1) * per_pair, :] = rows[
                        owner * per_pair : (owner + 1) * per_pair, side * HD : (side + 1) * HD
                    ]
        for ctx_index in (half, 2 + half):
            span = pl.ds(turned(ctx_index) * readers, readers)
            stores.append(
                pltpu.make_async_copy(
                    send_ref.at[span], send_hbm.at[span], store_sems.at[ctx_index]
                )
            )
            stores[-1].start()
    for copy in stores:
        copy.wait()


def columns_kernel(slot_ref, grad_ref, *refs):
    piece_refs, back_ref = refs[:HEADS], refs[HEADS]
    slots = slot_ref.shape[1]
    slot = jnp.broadcast_to(slot_ref[...].astype(jnp.float32), (slots, slots)).T
    lane = lax.broadcasted_iota(jnp.int32, (slots, slots), 1).astype(jnp.float32)
    back_ref[...] = (slot == lane).astype(jnp.bfloat16)
    first = turned(lax.axis_index("ctx"))
    for step, piece_ref in enumerate(piece_refs):
        start = pl.multiple_of((first ^ step) * HD, HD)
        piece_ref[...] = grad_ref[:, pl.ds(start, HD)]


def group_kernel(*refs):
    piece_refs, grads_ref = refs[:HEADS], refs[HEADS]
    head = my_place()[0]
    for step, piece_ref in enumerate(piece_refs):
        slots = piece_ref.shape[0]
        start = pl.multiple_of(turned(head ^ step) * slots, slots)
        grads_ref[pl.ds(start, slots), :] = piece_ref[...]


def part_rows(rows_ref, part, first, last):
    readers = rows_ref.shape[0] // HEADS
    per_pair = HD // readers
    span = slice(part * per_pair, (part + 1) * per_pair)
    rows = [
        rows_ref[chunk_of(reader, window, readers), span, :]
        for window in range(first, last)
        for reader in range(readers)
    ]
    return jnp.concatenate(rows, axis=0)


def put_rows(out_ref, part, first, last, rows, readers):
    per_pair = HD // readers
    for window in range(first, last):
        for reader in range(readers):
            source = ((window - first) * readers + reader) * per_pair
            target = chunk_back(reader, window, readers) * per_pair
            out_ref[target : target + per_pair, part * HD : (part + 1) * HD] = rows[
                source : source + per_pair
            ].astype(jnp.bfloat16)


def window_users(rows_ref, window):
    readers = rows_ref.shape[0] // HEADS
    per_pair = HD // readers
    first = turned(window) * readers
    tags = rows_ref[first : first + readers, 4 * per_pair :, :]
    return jnp.sum(tags.astype(jnp.float32), axis=0)[:1]


def visible_block(users, first, last):
    size = HD
    query_users = [jnp.broadcast_to(users[window], (size, size)).T for window in range(first, last)]
    query_users = jnp.concatenate(query_users, axis=0)
    rows = lax.broadcasted_iota(jnp.int32, query_users.shape, 0)
    columns = lax.broadcasted_iota(jnp.int32, query_users.shape, 1)
    blocks = []
    for window in range(last):
        block = (query_users == users[window]) & (query_users > 0.0)
        if window >= first:
            block = block & (columns + (window - first) * size <= rows)
        blocks.append(block)
    return jnp.concatenate(blocks, axis=1)


def forward_kernel(rows_ref, grads_ref, gain_ref, attended_ref, stats_ref):
    size = HD
    scale = HD ** (-0.5)
    users = [window_users(rows_ref, window) for window in range(HEADS)]
    for first in range(0, HEADS, HEADS):
        last = first + HEADS
        queries = part_rows(rows_ref, 1, first, last)
        scores = dot(queries, part_rows(rows_ref, 2, 0, last), 1, 1) * scale
        visible = visible_block(users, first, last)
        weights = jnp.where(visible, scores * jax.nn.sigmoid(scores), 0.0).astype(jnp.bfloat16)
        block = dot(weights, part_rows(rows_ref, 3, 0, last), 1, 0)
        attended_ref[first * size : last * size] = block
        for window in range(first, last):
            here = slice(window * size, (window + 1) * size)
            attended = block[(window - first) * size : (window - first + 1) * size]
            grad_normed = (
                grads_ref[here].astype(jnp.float32)
                * gain_ref[...]
                * part_rows(rows_ref, 0, window, window + 1).astype(jnp.float32)
            )
            turned_att = attended.T
            turned_grad = grad_normed.T
            mean = jnp.mean(turned_att, axis=0, keepdims=True)
            centered = turned_att - mean
            spread = jnp.sum(centered * centered, axis=0, keepdims=True)
            grad_sum = jnp.sum(turned_grad, axis=0, keepdims=True)
            cross = jnp.sum(turned_grad * centered, axis=0, keepdims=True)
            stats_ref[0:1, here] = mean
            stats_ref[1:2, here] = spread
            stats_ref[2:3, here] = grad_sum
            stats_ref[3:4, here] = cross


def slope_kernel(
    rows_ref,
    grads_ref,
    gain_ref,
    slopes_ref,
    turned_slopes_ref,
    turned_weights_ref,
    gate_ref,
    grad_gain_ref,
    grad_normed_ref,
):
    size = HD
    scale = HD ** (-0.5)
    users = [window_users(rows_ref, window) for window in range(HEADS)]
    gate = part_rows(rows_ref, 0, 0, HEADS).astype(jnp.float32) * gain_ref[...]
    grads = grads_ref[...].astype(jnp.float32)
    gate_ref[...] = gate
    grad_gain_ref[...] = grads * gain_ref[...]
    grad_normed_ref[...] = grads * gate
    for first in range(0, HEADS, STEP):
        last = first + STEP
        queries = part_rows(rows_ref, 1, first, last)
        scores = dot(queries, part_rows(rows_ref, 2, 0, last), 1, 1) * scale
        sigmoid = jax.nn.sigmoid(scores)
        slopes = sigmoid * (1.0 + scores * (1.0 - sigmoid)) * scale
        visible = visible_block(users, first, last)
        slopes = jnp.where(visible, slopes, 0.0)
        weights = jnp.where(visible, scores * sigmoid, 0.0)
        slopes_ref[first * size : last * size, : last * size] = slopes
        turned_slopes_ref[: last * size, first * size : last * size] = slopes.T
        turned_weights_ref[: last * size, first * size : last * size] = weights.T.astype(
            jnp.bfloat16
        )


def backward_kernel(
    rows_ref,
    attended_ref,
    slopes_ref,
    turned_slopes_ref,
    turned_weights_ref,
    gate_ref,
    grad_gain_ref,
    grad_normed_ref,
    *refs,
):
    stats_refs = refs[:HEADS]
    out_hbm = refs[HEADS]
    layer_refs = refs[HEADS + 1 : 2 * HEADS + 1]
    layer_all, out_ref, store_sems = refs[2 * HEADS + 1 :]
    head = my_place()[0]
    readers = rows_ref.shape[0] // HEADS
    size = HD
    width = float(HEADS * HD)
    stats = [stat_ref[...] for stat_ref in stats_refs]
    mean = sum(stat[0:1] for stat in stats) * (1.0 / HEADS)
    spread = sum(stat[1:2] + HD * (stat[0:1] - mean) * (stat[0:1] - mean) for stat in stats)
    inv_std = lax.rsqrt(spread / width + epsilon)
    mean_grad = sum(stat[2:3] for stat in stats) / width
    cross = sum(stat[3:4] + (stat[0:1] - mean) * stat[2:3] for stat in stats)
    mean_cross = cross * inv_std / width
    packed = [
        stat[:, window * size : (window + 1) * size]
        for window in range(HEADS)
        for stat in (mean, inv_std, mean_grad, mean_cross)
    ]
    packed.append(jnp.zeros((size - len(packed), size), jnp.float32))
    packed = jnp.concatenate(packed, axis=0).T
    out_grads = []
    for window in range(HEADS):
        here = slice(window * size, (window + 1) * size)
        row_mean, row_inv, row_grad, row_cross = [
            packed[:, 4 * window + index : 4 * window + index + 1] for index in range(4)
        ]
        normed = (attended_ref[here] - row_mean) * row_inv
        layer_all[here] = (normed * gate_ref[here]).astype(jnp.bfloat16)
        put_rows(out_ref, 0, window, window + 1, grad_gain_ref[here] * normed, readers)
        out_grads.append(row_inv * (grad_normed_ref[here] - row_grad - normed * row_cross))
    out_grads = jnp.concatenate(out_grads, axis=0).astype(jnp.bfloat16)
    stores = []
    for first in range(0, HEADS, STEP):
        last = first + STEP
        here = slice(first * size, last * size)
        upto = slice(0, last * size)
        after = slice(first * size, HEADS * size)
        score_grads = (
            dot(out_grads[here], part_rows(rows_ref, 3, 0, last), 1, 1) * slopes_ref[here, upto]
        ).astype(jnp.bfloat16)
        query_grads = dot(score_grads, part_rows(rows_ref, 2, 0, last), 1, 0)
        put_rows(out_ref, 1, first, last, query_grads, readers)
        turned_grads = (
            dot(part_rows(rows_ref, 3, first, last), out_grads[after], 1, 1)
            * turned_slopes_ref[here, after]
        ).astype(jnp.bfloat16)
        key_grads = dot(turned_grads, part_rows(rows_ref, 1, first, HEADS), 1, 0)
        put_rows(out_ref, 2, first, last, key_grads, readers)
        value_grads = dot(turned_weights_ref[here, after], out_grads[after], 1, 0)
        put_rows(out_ref, 3, first, last, value_grads, readers)
        for window in range(first, last):
            span = pl.ds(window * size, size)
            stores.append(
                pltpu.make_async_copy(out_ref.at[span], out_hbm.at[span], store_sems.at[window])
            )
            stores[-1].start()
    for step, layer_ref in enumerate(layer_refs):
        start = pl.multiple_of(turned(head ^ step) * size, size)
        layer_ref[...] = layer_all[pl.ds(start, size), :]
    for copy in stores:
        copy.wait()


def unslot_kernel(back_ref, returned_ref, *refs, per_pair):
    piece_refs = refs[:HEADS]
    layer_hbm, grad_hbm, layer_ref, grad_ref, store_sems = refs[HEADS:]
    slots = back_ref.shape[0]
    readers = slots // per_pair
    width = HEADS * HD
    first = turned(lax.axis_index("ctx"))
    for step, piece_ref in enumerate(piece_refs):
        start = pl.multiple_of((first ^ step) * HD, HD)
        layer_ref[:, pl.ds(start, HD)] = piece_ref[...]
    stores = [pltpu.make_async_copy(layer_ref, layer_hbm, store_sems.at[2])]
    stores[0].start()
    heads = []
    for head in range(HEADS):
        chunks = []
        for owner in range(readers):
            dp_index, ctx_index = device_of(owner, head)
            start = chunk_back(dp_index, ctx_index, readers) * per_pair
            chunks.append(returned_ref[start : start + per_pair])
        heads.append(jnp.concatenate(chunks, axis=0))
    half = slots // 2
    for side in range(2):
        span = pl.ds(side * half, half)
        here = slice(side * half, (side + 1) * half)
        for head in range(HEADS):
            rows = dot(back_ref[here], heads[head], 1, 0).astype(jnp.bfloat16)
            for part in range(4):
                start = part * width + head * HD
                grad_ref[here, start : start + HD] = rows[:, part * HD : (part + 1) * HD]
        stores.append(
            pltpu.make_async_copy(grad_ref.at[span], grad_hbm.at[span], store_sems.at[side])
        )
        stores[-1].start()
    for copy in stores:
        copy.wait()


def send(value, target, back=False):
    width = lax.axis_size("ctx")
    pairs = []
    for dp_index in range(lax.axis_size("dp")):
        for ctx_index in range(width):
            to_dp, to_ctx = target(dp_index, ctx_index)
            pair = (dp_index * width + ctx_index, to_dp * width + to_ctx)
            pairs.append(pair[::-1] if back else pair)
    return lax.ppermute(value, ("dp", "ctx"), pairs)


def exchange(chunks, place):
    readers, width = lax.axis_size("dp"), lax.axis_size("ctx")
    order = [None] * (readers * width)
    for dp_index in range(readers):
        for ctx_index in range(width):
            order[place(dp_index, ctx_index, readers)] = dp_index * width + ctx_index
    return lax.all_to_all(
        chunks, ("dp", "ctx"), split_axis=0, concat_axis=0, tiled=True, axis_index_groups=[order]
    )


def swap(value, dp_bits, ctx_bits):
    return send(value, lambda dp_index, ctx_index: (dp_index ^ dp_bits, ctx_index ^ ctx_bits))


def regroup(pieces, back=False):
    moved = []
    for step, piece in enumerate(pieces):

        def target(dp_index, ctx_index, step=step):
            return device_of(dp_index, turned(ctx_index) ^ step)

        moved.append(send(piece, target, back))
    return moved


def by_heads(proj_read, norm_gain, owner_of, user_of, grad_output):
    slots = proj_read.shape[0]
    readers = lax.axis_size("dp")
    per_pair = slots // readers
    group_rows = slots * HEADS
    width = 4 * HD
    gain = lax.dynamic_slice_in_dim(norm_gain, my_place()[0] * HD, HD, 0).reshape(1, HD)
    piece_shape = jax.ShapeDtypeStruct((slots, HD), jnp.bfloat16)
    chunk_shape = (HEADS * readers, 4 * per_pair + 8, HD)
    outgoing, slot = pl.pallas_call(
        functools.partial(slot_kernel, per_pair=per_pair),
        out_shape=(
            jax.ShapeDtypeStruct(chunk_shape, jnp.bfloat16),
            jax.ShapeDtypeStruct((1, slots), jnp.int32),
        ),
        in_specs=hbm(3),
        out_specs=tuple(hbm(2)),
        scratch_shapes=[
            pltpu.SMEM(owner_of.shape, jnp.int32),
            pltpu.VMEM((1, slots), jnp.int32),
            pltpu.VMEM((1, slots), jnp.int32),
            pltpu.VMEM(proj_read.shape, jnp.bfloat16),
            pltpu.VMEM(chunk_shape, jnp.bfloat16),
            pltpu.SemaphoreType.DMA((3,)),
            pltpu.SemaphoreType.DMA((HEADS + 1,)),
        ],
        name="slot_rows",
    )(owner_of, user_of.reshape(1, slots), proj_read)
    rows = exchange(outgoing, chunk_of)
    *pieces, back = pl.pallas_call(
        columns_kernel,
        out_shape=(piece_shape,) * HEADS + (jax.ShapeDtypeStruct((slots, slots), jnp.bfloat16),),
        in_specs=vmem(2),
        out_specs=tuple(vmem(HEADS + 1)),
        compiler_params=LIMIT,
        name="cut_columns",
    )(slot, grad_output)
    grads = pl.pallas_call(
        group_kernel,
        out_shape=jax.ShapeDtypeStruct((group_rows, HD), jnp.bfloat16),
        in_specs=vmem(HEADS),
        out_specs=vmem(1)[0],
        compiler_params=LIMIT,
        name="lay_group",
    )(*regroup(pieces))
    attended, stats = pl.pallas_call(
        forward_kernel,
        out_shape=(
            jax.ShapeDtypeStruct((group_rows, HD), jnp.float32),
            jax.ShapeDtypeStruct((4, group_rows), jnp.float32),
        ),
        in_specs=vmem(3),
        out_specs=tuple(vmem(2)),
        compiler_params=LIMIT,
        name="forward",
    )(rows, grads, gain)
    late_rows, stats = lax.optimization_barrier((rows, stats))
    slopes = pl.pallas_call(
        slope_kernel,
        out_shape=(
            jax.ShapeDtypeStruct((group_rows, group_rows), jnp.float32),
            jax.ShapeDtypeStruct((group_rows, group_rows), jnp.float32),
            jax.ShapeDtypeStruct((group_rows, group_rows), jnp.bfloat16),
        )
        + (jax.ShapeDtypeStruct((group_rows, HD), jnp.float32),) * 3,
        in_specs=vmem(3),
        out_specs=tuple(vmem(6)),
        compiler_params=LIMIT,
        name="slopes",
    )(late_rows, grads, gain)
    all_stats = [stats, swap(stats, 1, 0), swap(stats, 0, 1), swap(stats, 1, 1)]
    results = pl.pallas_call(
        backward_kernel,
        out_shape=(jax.ShapeDtypeStruct((group_rows, width), jnp.bfloat16),)
        + (piece_shape,) * HEADS,
        in_specs=vmem(8 + HEADS),
        out_specs=tuple(hbm(1) + vmem(HEADS)),
        scratch_shapes=[
            pltpu.VMEM((group_rows, HD), jnp.bfloat16),
            pltpu.VMEM((group_rows, width), jnp.bfloat16),
            pltpu.SemaphoreType.DMA((HEADS,)),
        ],
        compiler_params=LIMIT,
        name="backward",
    )(rows, attended, *slopes, *all_stats)
    returned = exchange(results[0], chunk_back)
    layer_shape, grad_shape = (slots, HEADS * HD), (slots, 4 * HEADS * HD)
    return pl.pallas_call(
        functools.partial(unslot_kernel, per_pair=per_pair),
        out_shape=(
            jax.ShapeDtypeStruct(layer_shape, jnp.bfloat16),
            jax.ShapeDtypeStruct(grad_shape, jnp.bfloat16),
        ),
        in_specs=vmem(2 + HEADS),
        out_specs=tuple(hbm(2)),
        scratch_shapes=[
            pltpu.VMEM(layer_shape, jnp.bfloat16),
            pltpu.VMEM(grad_shape, jnp.bfloat16),
            pltpu.SemaphoreType.DMA((3,)),
        ],
        compiler_params=LIMIT,
        name="unslot_rows",
    )(back, returned, *regroup(results[1:], back=True))


def solution(mesh):
    in_specs = (P(("dp", "ctx"), None), P(), P(), P(("dp", "ctx")), P(("dp", "ctx"), None))
    out_specs = (P(("dp", "ctx"), None), P(("dp", "ctx"), None))
    fits = mesh.shape["ctx"] == HEADS and mesh.shape["dp"] == 2 * len(SPANS)
    local = by_heads if fits else windowed
    return jax.shard_map(local, mesh=mesh, in_specs=in_specs, out_specs=out_specs, check_vma=False)
```
